32 devices in a mesh: dp: 2 (over x), seq: 16 (over z, y, core).
Axes of the slice: x: 2, y: 2, z: 4, core: 2. Of those that a mesh axis runs over, the one named last changes fastest.
Arguments:
- block_in: bfloat16 [12, 2048, 1024], P('dp', 'seq'), may hold values from -6 to 6
- doc_starts: int32 [12, 4], P('dp'), may hold values from 0 to 2047, as said below
- cotangent: bfloat16 [12, 2048, 1024], P('dp', 'seq'), may hold values from -6 to 6
- norm1_gain: float32 [1024], replicated, may hold values from 0.5 to 1.5
- w_query: bfloat16 [1024, 512], replicated
- w_key: bfloat16 [1024, 512], replicated
- w_value: bfloat16 [1024, 1024], replicated, may hold values from -0.1875 to 0.1875
- w_outgate: bfloat16 [1024, 1024], replicated, may hold values from -0.1875 to 0.1875
- w_rank_down: bfloat16 [1024, 16], replicated, may hold values from -0.1875 to 0.1875
- w_rank_up: bfloat16 [16, 512], replicated, may hold values from -1.5 to 1.5
- decay_bias: float32 [512], replicated, may hold values from -1 to 8
- group_gain: float32 [256], replicated, may hold values from 0.5 to 1.5
- w_output: bfloat16 [1024, 1024], replicated, may hold values from -0.375 to 0.375
- norm2_gain: float32 [1024], replicated, may hold values from 0.5 to 1.5
- w_ffgate: bfloat16 [1024, 2816], replicated, may hold values from -0.1875 to 0.1875
- w_ffup: bfloat16 [1024, 2816], replicated, may hold values from -0.1875 to 0.1875
- w_ffdown: bfloat16 [2816, 1024], replicated, may hold values from -0.15625 to 0.15625
Outputs:
- block_out: bfloat16 [12, 2048, 1024], P('dp', 'seq')
- grad_in: float32 [12, 2048, 1024], P('dp', 'seq')
- grad_norm1: float32 [1024], P(('dp', 'seq'))
- grad_query: float32 [1024, 512], P(('dp', 'seq'))
- grad_key: float32 [1024, 512], P(('dp', 'seq'))
- grad_value: float32 [1024, 1024], P(('dp', 'seq'))
- grad_outgate: float32 [1024, 1024], P(('dp', 'seq'))
- grad_rank_down: float32 [1024, 16], P(('dp', 'seq'))
- grad_rank_up: float32 [16, 512], P(None, ('dp', 'seq'))
- grad_bias: float32 [512], P(('dp', 'seq'))
- grad_group: float32 [256], P(('dp', 'seq'))
- grad_output: float32 [1024, 1024], P(('dp', 'seq'))
- grad_norm2: float32 [1024], P(('dp', 'seq'))
- grad_ffgate: float32 [1024, 2816], P(('dp', 'seq'))
- grad_ffup: float32 [1024, 2816], P(('dp', 'seq'))
- grad_ffdown: float32 [2816, 1024], P(('dp', 'seq'))
The draws below stay inside these ranges and needn't reach their ends.
Inputs may be any that keep to these rules, and one draw needn't show every extreme that they name: `doc_starts`: each row lists 4 positions where a document begins, in no order and possibly repeated; the first entry is 0. In every block of 6 rows (the rows of one index of dp) one row, drawn from the seed, lists only 0.
All inputs are finite; a program needn't handle non-finite values.
Results may differ from the reference program's by a relative error of at most 0.025.
Values sent between devices are 32-bit elements; how exact they have to be, the bound alone decides.
No kernel may reach another device: no remote copies, remote signals or barrier semaphores. Data moves between devices by JAX's collectives and lax.ppermute only.
A program may use at most 256 MiB of HBM per device.

```python
import jax
import jax.numpy as jnp
from jax import lax

D = 1024
HEADS = 4
DK = 512
DV = 1024
RANK = 16
FF = 2816
SPAN = 64
DOCS = 4
ROWS_DP = 6
ROW_LEN = 2048
ROWS = 12
HV = 256


def draw_doc_starts(key, part):
    key = jax.random.fold_in(key, 11)
    first_key, second_key = jax.random.split(key)
    starts = jax.random.randint(first_key, (ROWS, DOCS), 1, ROW_LEN)
    column = jnp.arange(DOCS)[None, :]
    starts = jnp.where(column == 0, 0, starts)
    chosen = jax.random.randint(second_key, (ROWS // ROWS_DP,), 0, ROWS_DP)
    row_index = jnp.arange(ROWS)
    single = row_index % ROWS_DP == chosen[row_index // ROWS_DP]
    starts = jnp.where(single[:, None], 0, starts)
    return starts.astype(jnp.int32)


def shared_base(key):
    return jax.random.normal(key, (D, DK), jnp.float32)


def draw_w_query(key, part):
    base = shared_base(key)
    limit = 6.0 * D ** (-0.5)
    return jnp.clip(base * D ** (-0.5), -limit, limit).astype(jnp.bfloat16)


def draw_w_key(key, part):
    base = shared_base(key)
    key = jax.random.fold_in(key, 29)
    noise = jax.random.normal(key, (D, DK), jnp.float32)
    limit = 6.0 * D ** (-0.5)
    return jnp.clip((0.7 * base + 0.7 * noise) * D ** (-0.5), -limit, limit).astype(jnp.bfloat16)


def shard_levels(key, shape, pieces, low, top_value):
    level, own = 1.0, jax.random.fold_in(key, 6)
    for axis_at, parts in pieces:
        heights = jnp.exp(jax.random.uniform(jax.random.fold_in(own, axis_at), (parts,), jnp.float32, low / len(pieces), top_value / len(pieces)))
        level = level * jnp.repeat(heights, shape[axis_at] // parts).reshape([-1 if axis == axis_at else 1 for axis in range(len(shape))])
    return level


def scatter_about(key, shape, width, most, cuts=(), held_as=jnp.bfloat16):
    values = jax.random.normal(key, shape, jnp.float32) * width
    if len(cuts) > 0:
        values = shard_levels(key, shape, cuts, -0.22, 0.18) * values
    return jnp.clip(values, min=-most, max=most).astype(held_as)


def setup_inputs(seed: int = 0) -> dict:
    arg_keys = jax.random.split(jax.random.key(seed), 18)
    return {
        "block_in": scatter_about(arg_keys[0], (ROWS, ROW_LEN, D), 1.0, 6.0, ((0, 2), (1, 16))),
        "doc_starts": draw_doc_starts(jax.random.fold_in(arg_keys[17], 71), 0),
        "cotangent": scatter_about(arg_keys[2], (ROWS, ROW_LEN, D), 1.0, 6.0, ((0, 2), (1, 16))),
        "norm1_gain": jnp.clip(1.0 + 0.1 * jax.random.normal(arg_keys[3], (D,), jnp.float32), 0.5, 1.5),
        "w_query": draw_w_query(jax.random.fold_in(arg_keys[17], 71), 0),
        "w_key": draw_w_key(jax.random.fold_in(arg_keys[17], 71), 0),
        "w_value": scatter_about(arg_keys[6], (D, DV), D ** -0.5, 0.1875),
        "w_outgate": scatter_about(arg_keys[7], (D, DV), D ** -0.5, 0.1875),
        "w_rank_down": scatter_about(arg_keys[8], (D, RANK), D ** -0.5, 0.1875),
        "w_rank_up": scatter_about(arg_keys[9], (RANK, DK), RANK ** -0.5, 1.5),
        "decay_bias": jnp.clip(jax.random.uniform(arg_keys[10], (DK,), jnp.float32, -1.0, 8.0), -1.0, 8.0),
        "group_gain": jnp.clip(1.0 + 0.1 * jax.random.normal(arg_keys[11], (HV,), jnp.float32), 0.5, 1.5),
        "w_output": scatter_about(arg_keys[12], (DV, D), (DV // 4) ** -0.5, 0.375),
        "norm2_gain": jnp.clip(1.0 + 0.1 * jax.random.normal(arg_keys[13], (D,), jnp.float32), 0.5, 1.5),
        "w_ffgate": scatter_about(arg_keys[14], (D, FF), D ** -0.5, 0.1875),
        "w_ffup": scatter_about(arg_keys[15], (D, FF), D ** -0.5, 0.1875),
        "w_ffdown": scatter_about(arg_keys[16], (FF, D), (FF // 2) ** -0.5, 0.15625),
    }


epsilon = 1e-06
highest = lax.Precision.HIGHEST

@jax.custom_vjp
def low(v):
    return lax.optimization_barrier(v.astype(jnp.bfloat16)).astype(jnp.float32)

@jax.custom_vjp
def low_back(v):
    return v

def low_keep(v):
    return (low(v), None)

def low_pass(kept, grad):
    return (grad,)

def back_keep(v):
    return (v, None)

def back_low(kept, grad):
    return (low(grad),)
low.defvjp(low_keep, low_pass)
low_back.defvjp(back_keep, back_low)

def span_step(state, block):
    queries, key_rows, value_rows, log_decay, resets = block
    length = resets.shape[0]
    cumulative = jnp.cumsum(log_decay, axis=0)
    doc_ids = jnp.cumsum(resets)
    alive = (doc_ids == 0).astype(jnp.float32)
    scaled_q = queries * jnp.exp(cumulative)
    scaled_k = key_rows * jnp.exp(-cumulative)
    scores = jnp.einsum('ihc,jhc->hij', scaled_q, scaled_k, precision=highest)
    position = jnp.arange(length)
    visible = (doc_ids[:, None] == doc_ids[None, :]) & (position[:, None] >= position[None, :])
    scores = jnp.where(visible[None], scores, 0.0)
    inner = jnp.einsum('hij,jhe->ihe', scores, value_rows, precision=highest)
    outer = jnp.einsum('ihc,hce->ihe', scaled_q * alive[:, None, None], state, precision=highest)
    head_scale = queries.shape[-1] ** (-0.5)
    last_sum = cumulative[-1]
    tail_mask = (doc_ids == doc_ids[-1]).astype(jnp.float32)
    weighted = key_rows * jnp.exp(last_sum[None] - cumulative) * tail_mask[:, None, None]
    renewed = state * (jnp.exp(last_sum) * alive[-1])[:, :, None]
    renewed = renewed + jnp.einsum('jhc,jhe->hce', weighted, value_rows, precision=highest)
    return (renewed, head_scale * (inner + outer))

def run_spans(queries, key_rows, value_rows, log_decay, resets, state):
    length = resets.shape[0]
    blocks = length // SPAN
    heads_k = (blocks, SPAN, queries.shape[1], queries.shape[2])
    heads_v = (blocks, SPAN, value_rows.shape[1], value_rows.shape[2])
    final_state, outputs = lax.scan(jax.checkpoint(span_step), state, (queries.reshape(heads_k), key_rows.reshape(heads_k), value_rows.reshape(heads_v), log_decay.reshape(heads_k), resets.reshape(blocks, SPAN)))
    return (outputs.reshape(length, value_rows.shape[1], value_rows.shape[2]), final_state)

def dense(left, right):
    return jnp.dot(left, right, precision=highest)

def row_forward(row_in, row_resets, params):
    norm1_gain, w_query, w_key, w_value, w_outgate, w_rank_down, w_rank_up, decay_bias, group_gain, w_output, norm2_gain, w_ffgate, w_ffup, w_ffdown = params
    length = row_in.shape[0]
    head_k = w_query.shape[1] // HEADS
    head_v = w_value.shape[1] // HEADS
    inv_one = lax.rsqrt(lax.optimization_barrier(jnp.mean(row_in * row_in, axis=-1, keepdims=True)) + epsilon)
    normed = low(row_in * inv_one * norm1_gain)
    queries = low(low_back(dense(normed, w_query)))
    key_rows = low(low_back(dense(normed, w_key)))
    value_rows = low(low_back(dense(normed, w_value)))
    out_gate = low_back(dense(normed, w_outgate))
    rank_act = low(low_back(dense(normed, w_rank_down)))
    gate_pre = low_back(dense(rank_act, w_rank_up) + decay_bias)
    log_decay = jax.nn.log_sigmoid(gate_pre) / 16.0
    start_state = jnp.zeros((HEADS, head_k, head_v), jnp.float32)
    mixed, final_state = run_spans(queries.reshape(length, HEADS, head_k), key_rows.reshape(length, HEADS, head_k), value_rows.reshape(length, HEADS, head_v), log_decay.reshape(length, HEADS, head_k), row_resets, start_state)
    inv_head = lax.rsqrt(lax.optimization_barrier(jnp.mean(mixed * mixed, axis=-1, keepdims=True)) + epsilon)
    heads_normed = (mixed * inv_head * group_gain).reshape(length, HEADS * head_v)
    gated = low(heads_normed * jax.nn.silu(out_gate))
    middle = row_in + low_back(dense(gated, w_output))
    inv_two = lax.rsqrt(lax.optimization_barrier(jnp.mean(middle * middle, axis=-1, keepdims=True)) + epsilon)
    normed2 = low(middle * inv_two * norm2_gain)
    ff_gate = low_back(dense(normed2, w_ffgate))
    ff_up = low_back(dense(normed2, w_ffup))
    hidden = low(jax.nn.silu(ff_gate) * ff_up)
    return middle + low_back(dense(hidden, w_ffdown))

def reference(block_in, doc_starts, cotangent, norm1_gain, w_query, w_key, w_value, w_outgate, w_rank_down, w_rank_up, decay_bias, group_gain, w_output, norm2_gain, w_ffgate, w_ffup, w_ffdown):
    positions = jnp.arange(ROW_LEN).astype(jnp.int32)
    resets = jnp.any(doc_starts[:, :, None] == positions[None, None, :], axis=1).astype(jnp.float32)
    weights = tuple((item.astype(jnp.float32) for item in (norm1_gain, w_query, w_key, w_value, w_outgate, w_rank_down, w_rank_up, decay_bias, group_gain, w_output, norm2_gain, w_ffgate, w_ffup, w_ffdown)))
    inputs = block_in.astype(jnp.float32)

    def forward(values_in, params):

        def one_row(paired):
            return row_forward(paired[0], paired[1], params)
        return lax.map(jax.checkpoint(one_row), (values_in, resets))
    result, pull_back = jax.vjp(forward, inputs, weights)
    grad_in, grads = pull_back(cotangent.astype(jnp.float32))
    return (result.astype(jnp.bfloat16), grad_in, grads[0], grads[1], grads[2], grads[3], grads[4], grads[5], grads[6], grads[7], grads[8], grads[9], grads[10], grads[11], grads[12], grads[13])
```

```python
import functools

import jax
import jax.numpy as jnp
from jax import lax
from jax.experimental import pallas as pl
from jax.experimental.pallas import tpu as pltpu
from jax.sharding import PartitionSpec as P

HEADS = 4
EPS = 1e-06
MIB = 1 << 20
BF = jnp.bfloat16
F32 = jnp.float32
HIGHEST = lax.Precision.HIGHEST


def nn(a, b, precision=None):
    return lax.dot_general(
        a, b, (((1,), (0,)), ((), ())), precision=precision, preferred_element_type=F32
    )


def nt(a, b):
    return lax.dot_general(a, b, (((1,), (1,)), ((), ())), preferred_element_type=F32)


def tn(a, b):
    return lax.dot_general(a, b, (((0,), (0,)), ((), ())), preferred_element_type=F32)


def shape(dims, dtype):
    return jax.ShapeDtypeStruct(dims, dtype)


def call(body, out_shape, grid, in_specs, out_specs, prefetch=0, scratch=(), flops=0, moved=0):
    return pl.pallas_call(
        body,
        out_shape=out_shape,
        grid_spec=pltpu.PrefetchScalarGridSpec(
            num_scalar_prefetch=prefetch,
            grid=grid,
            in_specs=in_specs,
            out_specs=out_specs,
            scratch_shapes=list(scratch),
        ),
        compiler_params=pltpu.CompilerParams(vmem_limit_bytes=56 * MIB),
        cost_estimate=pl.CostEstimate(flops=flops, bytes_accessed=moved, transcendentals=0),
    )


def block(dims, index):
    return pl.BlockSpec(dims, index)


def whole(dims):
    zero = (0,) * len(dims)
    return pl.BlockSpec(dims, lambda *_: zero)


def reset_masks(docs_ref, row, docs, length):
    at_i = lax.broadcasted_iota(jnp.int32, (length, length), 0)
    at_j = lax.broadcasted_iota(jnp.int32, (length, length), 1)
    token = lax.broadcasted_iota(jnp.int32, (length, 1), 0)
    visible = at_i >= at_j
    alive = token >= 0
    tail = token >= 0
    whole_alive = jnp.float32(1.0)
    for n in range(docs):
        start = docs_ref[row * docs + n]
        visible = visible & jnp.logical_not((at_j < start) & (start <= at_i))
        inside = (start >= 0) & (start < length)
        first = jnp.where(start >= 0, start, length)
        alive = alive & (token < first)
        last = jnp.where(start < length, start, -1)
        tail = tail & (token >= last)
        whole_alive = whole_alive * jnp.where(inside, 0.0, 1.0)
    return visible, alive.astype(F32), tail.astype(F32), whole_alive


def lower_ones(length, strict=False):
    at_i = lax.broadcasted_iota(jnp.int32, (length, length), 0)
    at_j = lax.broadcasted_iota(jnp.int32, (length, length), 1)
    return (at_i > at_j if strict else at_i >= at_j).astype(F32)


def project_body(
    rows, docs, length, hk, hv, parts,
    docs_ref, table_ref, x_ref, gain_ref, wq_ref, wk_ref, wv_ref, wog_ref, wrd_ref, wru_ref, bias_ref,
    normed_ref, q_ref, k_ref, v_ref, og_ref, ra_ref, gp_ref, cum_ref, keep_ref, send_ref, decay_ref,
    hold,
):
    x = x_ref[...].astype(F32)
    inv = lax.rsqrt(jnp.mean(x * x, axis=-1, keepdims=True) + EPS)
    normed = (x * inv * gain_ref[...]).astype(BF)
    normed_ref[...] = normed
    rank = nn(normed, wrd_ref[...]).astype(BF)
    ra_ref[...] = rank
    gate = nn(rank, wru_ref[...]) + bias_ref[...]
    gp_ref[...] = gate
    q_ref[...] = nn(normed, wq_ref[...]).astype(BF)
    key = nn(normed, wk_ref[...]).astype(BF)
    k_ref[...] = key
    value = nn(normed, wv_ref[...]).astype(BF)
    v_ref[...] = value
    og_ref[...] = nn(normed, wog_ref[...])
    log_decay = (jnp.minimum(gate, 0.0) - jnp.log1p(jnp.exp(-jnp.abs(gate)))) * (1.0 / 16.0)
    tri = lower_ones(length)
    size = hv // parts
    for r in range(rows):
        at = slice(r * length, (r + 1) * length)
        row = pl.program_id(0) * rows + r
        cum = nn(tri, log_decay[at], HIGHEST)
        cum_ref[at, :] = cum
        _, _, tail, whole_alive = reset_masks(docs_ref, row, docs, length)
        last = cum[length - 1 :, :]
        decay_ref[r] = jnp.exp(last) * whole_alive
        weighted = (key[at].astype(F32) * jnp.exp(last - cum) * tail).astype(BF)
        for h in range(HEADS):
            hold[...] = tn(value[at, h * hv : (h + 1) * hv], weighted[:, h * hk : (h + 1) * hk])
            for j in range(parts // 2):
                first = pl.multiple_of(table_ref[j] * size, size)
                keep_ref[j, r, h] = hold[pl.ds(first, size), :]
                second = pl.multiple_of(table_ref[parts // 2 + j] * size, size)
                send_ref[j, r, h] = hold[pl.ds(second, size), :]


def project_all(x, docs, table, gain, wq, wk, wv, wog, wrd, wru, bias, dims):
    row_count, length, width, kw, vw, ndocs, parts = dims
    tokens = row_count * length
    rows = 2 if row_count % 2 == 0 else 1
    tm = rows * length
    hk, hv = kw // HEADS, vw // HEADS
    rank = wrd.shape[1]
    size = hv // parts
    tile = lambda n: block((tm, n), lambda i, *_: (i, 0))
    half = (parts // 2, row_count, HEADS, size, hk)
    half_block = block((parts // 2, rows, HEADS, size, hk), lambda i, *_: (0, i, 0, 0, 0))
    body = functools.partial(project_body, rows, ndocs, length, hk, hv, parts)
    return call(
        body,
        (
            shape((tokens, width), BF),
            shape((tokens, kw), BF),
            shape((tokens, kw), BF),
            shape((tokens, vw), BF),
            shape((tokens, vw), F32),
            shape((tokens, rank), BF),
            shape((tokens, kw), F32),
            shape((tokens, kw), F32),
            shape(half, F32),
            shape(half, F32),
            shape((row_count, 1, kw), F32),
        ),
        (row_count // rows,),
        [
            tile(width), whole((1, width)), whole(wq.shape), whole(wk.shape), whole(wv.shape),
            whole(wog.shape), whole(wrd.shape), whole(wru.shape), whole((1, kw)),
        ],
        (
            tile(width), tile(kw), tile(kw), tile(vw), tile(vw), tile(rank), tile(kw), tile(kw),
            half_block, half_block, block((rows, 1, kw), lambda i, *_: (i, 0, 0)),
        ),
        prefetch=2,
        scratch=[pltpu.VMEM((hv, hk), F32)],
        flops=2 * tokens * width * (2 * kw + 2 * vw),
        moved=20 * MIB,
    )(docs, table, x, gain.reshape(1, -1), wq, wk, wv, wog, wrd, wru, bias.reshape(1, -1))


def span_factors(cum, length):
    middle = cum[length // 2 - 1 : length // 2, :]
    return jnp.exp(cum - middle), jnp.exp(middle - cum)


def inner_body(docs, length, hk, hv, docs_ref, q_ref, k_ref, v_ref, cum_ref, inner_ref):
    visible, _, _, _ = reset_masks(docs_ref, pl.program_id(0), docs, length)
    up, down = span_factors(cum_ref[...], length)
    q = (q_ref[...].astype(F32) * up).astype(BF)
    k = (k_ref[...].astype(F32) * down).astype(BF)
    for h in range(HEADS):
        kk = slice(h * hk, (h + 1) * hk)
        vv = slice(h * hv, (h + 1) * hv)
        scores = jnp.where(visible, nt(q[:, kk], k[:, kk]), 0.0).astype(BF)
        inner_ref[:, vv] = nn(scores, v_ref[:, vv])


def inner_all(q, k, v, cum, docs, dims):
    row_count, length, width, kw, vw, ndocs, parts = dims
    tokens = row_count * length
    tile = lambda n: block((length, n), lambda i, *_: (i, 0))
    return call(
        functools.partial(inner_body, ndocs, length, kw // HEADS, vw // HEADS),
        shape((tokens, vw), F32),
        (row_count,),
        [tile(kw), tile(kw), tile(vw), tile(kw)],
        tile(vw),
        prefetch=1,
        flops=2 * tokens * length * (kw + vw),
        moved=8 * MIB,
    )(docs, q, k, v, cum)


def gather_state(state_ref, table_ref, h, parts):
    return jnp.concatenate([state_ref[table_ref[parts + p], 0, h] for p in range(parts)], axis=0)


def mix_body(
    docs, length, hk, hv, parts,
    docs_ref, table_ref, q_ref, cum_ref, inner_ref, og_ref, state_ref, gain_ref,
    mixed_ref, gated_ref, kept_ref,
):
    _, alive, _, _ = reset_masks(docs_ref, pl.program_id(0), docs, length)
    reach = (q_ref[...].astype(F32) * jnp.exp(cum_ref[...]) * alive).astype(BF)
    scale = hk ** (-0.5)
    for h in range(HEADS):
        kk = slice(h * hk, (h + 1) * hk)
        vv = slice(h * hv, (h + 1) * hv)
        state = gather_state(state_ref, table_ref, h, parts).astype(BF)
        kept_ref[0, h] = state
        mixed = scale * (inner_ref[:, vv] + nt(reach[:, kk], state))
        mixed_ref[:, vv] = mixed
        inv = lax.rsqrt(jnp.mean(mixed * mixed, axis=-1, keepdims=True) + EPS)
        og = og_ref[:, vv]
        gated_ref[:, vv] = (mixed * inv * gain_ref[...] * og * jax.nn.sigmoid(og)).astype(BF)


def mix_all(q, cum, inner, og, state, gain, docs, table, dims):
    row_count, length, width, kw, vw, ndocs, parts = dims
    tokens = row_count * length
    hk, hv = kw // HEADS, vw // HEADS
    tile = lambda n: block((length, n), lambda i, *_: (i, 0))
    return call(
        functools.partial(mix_body, ndocs, length, hk, hv, parts),
        (
            shape((tokens, vw), F32),
            shape((tokens, vw), BF),
            shape((row_count, HEADS, hv, hk), BF),
        ),
        (row_count,),
        [
            tile(kw), tile(kw), tile(vw), tile(vw),
            block((parts, 1, HEADS, hv // parts, hk), lambda i, *_: (0, i, 0, 0, 0)),
            whole((1, hv)),
        ],
        (tile(vw), tile(vw), block((1, HEADS, hv, hk), lambda i, *_: (i, 0, 0, 0))),
        prefetch=2,
        flops=2 * tokens * hk * vw,
        moved=18 * MIB,
    )(docs, table, q, cum, inner, og, state, gain.reshape(1, -1))


def ff_body(
    steps,
    x_ref, cot_ref, gated_ref, wo_ref, gain_ref, wg_ref, wu_ref, wd_ref,
    hidden_ref, dg_ref, du_ref, normed2_ref, out_ref, dmid_ref, dout_ref, dgated_ref, gnorm_ref,
    middle, total, back,
):
    step = pl.program_id(0)

    @pl.when(step == 0)
    def _():
        mid = x_ref[...].astype(F32) + nn(gated_ref[...], wo_ref[...])
        middle[...] = mid
        inv = lax.rsqrt(jnp.mean(mid * mid, axis=-1, keepdims=True) + EPS)
        normed2_ref[...] = (mid * inv * gain_ref[...]).astype(BF)

    normed2 = normed2_ref[...]
    gate = nn(normed2, wg_ref[...])
    up = nn(normed2, wu_ref[...])
    d_hidden = nt(cot_ref[...], wd_ref[...])
    sig = jax.nn.sigmoid(gate)
    act = gate * sig
    hidden = (act * up).astype(BF)
    dg = (d_hidden * up * sig * (1.0 + gate * (1.0 - sig))).astype(BF)
    du = (d_hidden * act).astype(BF)
    hidden_ref[...] = hidden
    dg_ref[...] = dg
    du_ref[...] = du
    more = nn(hidden, wd_ref[...])
    more_back = nt(dg, wg_ref[...]) + nt(du, wu_ref[...])

    @pl.when(step == 0)
    def _():
        total[...] = more
        back[...] = more_back

    @pl.when(step > 0)
    def _():
        total[...] += more
        back[...] += more_back

    @pl.when(step == steps - 1)
    def _():
        mid = middle[...]
        out_ref[...] = (mid + total[...]).astype(BF)
        inv = lax.rsqrt(jnp.mean(mid * mid, axis=-1, keepdims=True) + EPS)
        d_normed2 = back[...]
        gnorm_ref[...] = jnp.sum(d_normed2 * mid * inv, axis=0, keepdims=True)
        scaled = d_normed2 * gain_ref[...]
        d_middle = (
            cot_ref[...].astype(F32)
            + inv * scaled
            - mid * (inv * inv * inv) * jnp.mean(scaled * mid, axis=-1, keepdims=True)
        )
        dmid_ref[...] = d_middle
        d_out = d_middle.astype(BF)
        dout_ref[...] = d_out
        dgated_ref[...] = nt(d_out, wo_ref[...])


def ff_all(x, cot, gated, wo, gain, wg, wu, wd):
    tokens, width = x.shape
    vw = gated.shape[1]
    ff = wg.shape[1]
    tile = 256
    steps = ff // tile
    col = lambda n: block((n, tile), lambda i: (0, i))
    once = lambda dims: pl.BlockSpec(dims, lambda i: (0, 0), pipeline_mode=pl.Buffered(1))
    return call(
        functools.partial(ff_body, steps),
        (
            shape((tokens, ff), BF), shape((tokens, ff), BF), shape((tokens, ff), BF),
            shape((tokens, width), BF), shape((tokens, width), BF), shape((tokens, width), F32),
            shape((tokens, width), BF), shape((tokens, vw), F32), shape((1, width), F32),
        ),
        (steps,),
        [
            once((tokens, width)), once((tokens, width)), once((tokens, vw)), once(wo.shape),
            once((1, width)), col(width), col(width), block((tile, width), lambda i: (i, 0)),
        ],
        (
            col(tokens), col(tokens), col(tokens),
            whole((tokens, width)), whole((tokens, width)), whole((tokens, width)),
            whole((tokens, width)), whole((tokens, vw)), whole((1, width)),
        ),
        scratch=[pltpu.VMEM((tokens, width), F32)] * 3,
        flops=12 * tokens * width * ff,
        moved=45 * MIB,
    )(x, cot, gated, wo, gain.reshape(1, -1), wg, wu, wd)


def head_back_body(
    docs, length, hk, hv, parts,
    docs_ref, table_ref, dgated_ref, og_ref, mixed_ref, q_ref, cum_ref, gain_ref,
    dmix_ref, dog_ref, keep_ref, send_ref, ggroup_ref,
    hold,
):
    row = pl.program_id(0)
    _, alive, _, _ = reset_masks(docs_ref, row, docs, length)
    reach = (q_ref[...].astype(F32) * jnp.exp(cum_ref[...]) * alive).astype(BF)
    scale = hk ** (-0.5)
    size = hv // parts
    ggroup = jnp.zeros((1, hv), F32)
    for h in range(HEADS):
        kk = slice(h * hk, (h + 1) * hk)
        vv = slice(h * hv, (h + 1) * hv)
        mixed = mixed_ref[:, vv]
        inv = lax.rsqrt(jnp.mean(mixed * mixed, axis=-1, keepdims=True) + EPS)
        og = og_ref[:, vv]
        sig = jax.nn.sigmoid(og)
        dgated = dgated_ref[:, vv]
        unit = mixed * inv
        dog_ref[:, vv] = (
            dgated * unit * gain_ref[...] * sig * (1.0 + og * (1.0 - sig))
        ).astype(BF)
        d_heads = dgated * og * sig
        ggroup = ggroup + jnp.sum(d_heads * unit, axis=0, keepdims=True)
        scaled = d_heads * gain_ref[...]
        d_mixed = inv * scaled - mixed * (inv * inv * inv) * jnp.mean(
            scaled * mixed, axis=-1, keepdims=True
        )
        d_mixed = (scale * d_mixed).astype(BF)
        dmix_ref[:, vv] = d_mixed
        hold[...] = tn(d_mixed, reach[:, kk])
        for j in range(parts // 2):
            first = pl.multiple_of(table_ref[j] * size, size)
            keep_ref[j, 0, h] = hold[pl.ds(first, size), :]
            second = pl.multiple_of(table_ref[parts // 2 + j] * size, size)
            send_ref[j, 0, h] = hold[pl.ds(second, size), :]

    @pl.when(row == 0)
    def _():
        ggroup_ref[...] = ggroup

    @pl.when(row > 0)
    def _():
        ggroup_ref[...] += ggroup


def head_back_all(dgated, og, mixed, q, cum, gain, docs, table, dims):
    row_count, length, width, kw, vw, ndocs, parts = dims
    tokens = row_count * length
    hk, hv = kw // HEADS, vw // HEADS
    size = hv // parts
    tile = lambda n: block((length, n), lambda i, *_: (i, 0))
    half = (parts // 2, row_count, HEADS, size, hk)
    half_block = block((parts // 2, 1, HEADS, size, hk), lambda i, *_: (0, i, 0, 0, 0))
    return call(
        functools.partial(head_back_body, ndocs, length, hk, hv, parts),
        (
            shape((tokens, vw), BF), shape((tokens, vw), BF),
            shape(half, F32), shape(half, F32), shape((1, hv), F32),
        ),
        (row_count,),
        [tile(vw), tile(vw), tile(vw), tile(kw), tile(kw), whole((1, hv))],
        (tile(vw), tile(vw), half_block, half_block, whole((1, hv))),
        prefetch=2,
        scratch=[pltpu.VMEM((hv, hk), F32)],
        flops=2 * tokens * hk * vw,
        moved=20 * MIB,
    )(docs, table, dgated, og, mixed, q, cum, gain.reshape(1, -1))


def mix_back_body(
    docs, length, hk, hv, parts,
    docs_ref, table_ref, q_ref, k_ref, v_ref, cum_ref, gp_ref, ra_ref, dmix_ref, state_ref, grad_ref,
    wru_ref,
    dqkv_ref, drank_ref, grup_ref, gbias_ref,
):
    row = pl.program_id(0)
    kw = HEADS * hk
    visible, alive, tail, whole_alive = reset_masks(docs_ref, row, docs, length)
    cum = cum_ref[...]
    last = cum[length - 1 :, :]
    up, down = span_factors(cum, length)
    from_start = jnp.exp(cum) * alive
    to_end = jnp.exp(last - cum) * tail
    total = jnp.exp(last) * whole_alive
    q = q_ref[...].astype(F32)
    k = k_ref[...].astype(F32)
    q_span = (q * up).astype(BF)
    k_span = (k * down).astype(BF)
    reach = (q * from_start).astype(BF)
    weighted = (k * to_end).astype(BF)
    later, earlier, crossing = [], [], []
    for h in range(HEADS):
        kk = slice(h * hk, (h + 1) * hk)
        vv = slice(h * hv, (h + 1) * hv)
        qs, ks = q_span[:, kk], k_span[:, kk]
        d_mix = dmix_ref[:, vv]
        value = v_ref[:, vv]
        state = state_ref[0, h]
        grad32 = gather_state(grad_ref, table_ref, h, parts)
        grad = grad32.astype(BF)
        scores = jnp.where(visible, nt(qs, ks), 0.0).astype(BF)
        d_scores = jnp.where(visible, nt(d_mix, value), 0.0).astype(BF)
        dq_in = nn(d_scores, ks)
        dk_in = tn(d_scores, qs)
        dq_out = nn(d_mix, state)
        dk_out = nn(value, grad)
        dqkv_ref[:, kk] = (dq_in * up[:, kk] + dq_out * from_start[:, kk]).astype(BF)
        dqkv_ref[:, kw + h * hk : kw + (h + 1) * hk] = (
            dk_in * down[:, kk] + dk_out * to_end[:, kk]
        ).astype(BF)
        dqkv_ref[:, 2 * kw + h * hv : 2 * kw + (h + 1) * hv] = (
            tn(scores, d_mix) + nt(weighted[:, kk], grad)
        ).astype(BF)
        later.append(
            qs.astype(F32) * dq_in - ks.astype(F32) * dk_in + reach[:, kk].astype(F32) * dq_out
        )
        earlier.append(weighted[:, kk].astype(F32) * dk_out)
        crossing.append(jnp.sum(state.astype(F32) * grad32, axis=0, keepdims=True))
    later = jnp.concatenate(later, axis=1)
    earlier = jnp.concatenate(earlier, axis=1)
    crossing = jnp.concatenate(crossing, axis=1)
    at_i = lax.broadcasted_iota(jnp.int32, (length, length), 0)
    at_j = lax.broadcasted_iota(jnp.int32, (length, length), 1)
    after = (at_i <= at_j).astype(F32)
    before = (at_i > at_j).astype(F32)
    d_decay = nn(after, later, HIGHEST) + nn(before, earlier, HIGHEST) + total * crossing
    d_gate = (d_decay * jax.nn.sigmoid(-gp_ref[...]) * (1.0 / 16.0)).astype(BF)
    drank_ref[...] = nt(d_gate, wru_ref[...]).astype(BF)
    grup = tn(ra_ref[...], d_gate)
    gbias = jnp.sum(d_gate.astype(F32), axis=0, keepdims=True)

    @pl.when(row == 0)
    def _():
        grup_ref[...] = grup
        gbias_ref[...] = gbias

    @pl.when(row > 0)
    def _():
        grup_ref[...] += grup
        gbias_ref[...] += gbias


def mix_back_all(q, k, v, cum, gp, ra, dmix, state, grad, wru, docs, table, dims):
    row_count, length, width, kw, vw, ndocs, parts = dims
    tokens = row_count * length
    hk, hv = kw // HEADS, vw // HEADS
    rank = wru.shape[0]
    tile = lambda n: block((length, n), lambda i, *_: (i, 0))
    return call(
        functools.partial(mix_back_body, ndocs, length, hk, hv, parts),
        (
            shape((tokens, 2 * kw + vw), BF), shape((tokens, rank), BF),
            shape((rank, kw), F32), shape((1, kw), F32),
        ),
        (row_count,),
        [
            tile(kw), tile(kw), tile(vw), tile(kw), tile(kw), tile(rank), tile(vw),
            block((1, HEADS, hv, hk), lambda i, *_: (i, 0, 0, 0)),
            block((parts, 1, HEADS, hv // parts, hk), lambda i, *_: (0, i, 0, 0, 0)),
            whole((rank, kw)),
        ],
        (tile(2 * kw + vw), tile(rank), whole((rank, kw)), whole((1, kw))),
        prefetch=2,
        flops=16 * tokens * length * vw,
        moved=16 * MIB,
    )(docs, table, q, k, v, cum, gp, ra, dmix, state, grad, wru)


def input_back_body(
    kw, vw,
    x_ref, dmid_ref, dqkv_ref, dog_ref, drank_ref, gain_ref, wq_ref, wk_ref, wv_ref, wog_ref, wrd_ref,
    gin_ref, gnorm_ref,
):
    step = pl.program_id(0)
    d_normed = (
        nt(dqkv_ref[:, :kw], wq_ref[...])
        + nt(dqkv_ref[:, kw : 2 * kw], wk_ref[...])
        + nt(dqkv_ref[:, 2 * kw :], wv_ref[...])
        + nt(dog_ref[...], wog_ref[...])
        + nt(drank_ref[...], wrd_ref[...])
    )
    x = x_ref[...].astype(F32)
    inv = lax.rsqrt(jnp.mean(x * x, axis=-1, keepdims=True) + EPS)
    gnorm = jnp.sum(d_normed * x * inv, axis=0, keepdims=True)
    scaled = d_normed * gain_ref[...]
    gin_ref[...] = (
        dmid_ref[...]
        + inv * scaled
        - x * (inv * inv * inv) * jnp.mean(scaled * x, axis=-1, keepdims=True)
    )

    @pl.when(step == 0)
    def _():
        gnorm_ref[...] = gnorm

    @pl.when(step > 0)
    def _():
        gnorm_ref[...] += gnorm


def input_back_all(x, dmid, dqkv, dog, drank, gain, wq, wk, wv, wog, wrd):
    tokens, width = x.shape
    kw, vw = wq.shape[1], wv.shape[1]
    tm = 256 if tokens % 256 == 0 else 128
    tile = lambda n: block((tm, n), lambda i: (i, 0))
    return call(
        functools.partial(input_back_body, kw, vw),
        (shape((tokens, width), F32), shape((1, width), F32)),
        (tokens // tm,),
        [
            tile(width), tile(width), tile(2 * kw + vw), tile(vw), tile(drank.shape[1]),
            whole((1, width)), whole(wq.shape), whole(wk.shape), whole(wv.shape), whole(wog.shape),
            whole(wrd.shape),
        ],
        (tile(width), whole((1, width))),
        flops=2 * tokens * width * (2 * kw + 2 * vw),
        moved=20 * MIB,
    )(x, dmid, dqkv, dog, drank, gain.reshape(1, -1), wq, wk, wv, wog, wrd)


def weight_body(count, pieces, per, *refs):
    table_ref, left_ref = refs[:2]
    rights = refs[2 : 2 + count]
    outs = refs[2 + count : 2 + 3 * count]
    turned, hold = refs[2 + 3 * count :]

    @pl.when(pl.program_id(0) == 0)
    def _():
        turned[...] = left_ref[...].T

    for n in range(count):
        hold[...] = nn(turned[...], rights[n][...])
        keep_ref, send_ref = outs[2 * n], outs[2 * n + 1]
        for j in range(pieces // 2):
            first = pl.multiple_of(table_ref[j] * per, per)
            keep_ref[j] = hold[pl.ds(first, per), :]
            second = pl.multiple_of(table_ref[pieces // 2 + j] * per, per)
            send_ref[j] = hold[pl.ds(second, per), :]


def weight_grads(left, rights, table, tile=256):
    tokens, rows = left.shape
    pieces = table.shape[0]
    per = rows // pieces
    cols = rights[0].shape[1]
    if per % 8:
        out = []
        for right in rights:
            parts = tn(left, right).reshape(pieces, per, cols)[table]
            out.append((parts[: pieces // 2], parts[pieces // 2 :]))
        return out
    count = len(rights)
    half = shape((pieces // 2, per, cols), F32)
    half_block = block((pieces // 2, per, tile), lambda i, *_: (0, 0, i))
    flat = call(
        functools.partial(weight_body, count, pieces, per),
        (half,) * (2 * count),
        (cols // tile,),
        [whole((tokens, rows))] + [block((tokens, tile), lambda i, *_: (0, i))] * count,
        (half_block,) * (2 * count),
        prefetch=1,
        scratch=[pltpu.VMEM((rows, tokens), BF), pltpu.VMEM((rows, tile), F32)],
        flops=2 * tokens * rows * cols * count,
        moved=4 * rows * cols * count,
    )(table, left, *rights)
    return [(flat[2 * n], flat[2 * n + 1]) for n in range(count)]


def bits_of(n):
    return n.bit_length() - 1


class Links:
    def __init__(self):
        self.n_dp, self.n_seq = lax.axis_size("dp"), lax.axis_size("seq")
        self.seq_bits, self.dp_bits = bits_of(self.n_seq), bits_of(self.n_dp)
        self.at_seq = lax.axis_index("seq")
        self.me = lax.axis_index("dp") * self.n_seq + self.at_seq

    def swap(self, value, bit):
        name, n, flip = "seq", self.n_seq, 1 << bit
        if bit >= self.seq_bits:
            name, n, flip = "dp", self.n_dp, 1 << (bit - self.seq_bits)
        return lax.ppermute(value, name, [(i, i ^ flip) for i in range(n)])

    def table(self, order):
        n = 1 << len(order)
        places = [
            sum(((at >> (len(order) - 1 - k)) & 1) << bit for k, bit in enumerate(order))
            for at in range(n)
        ]
        here = self.me if n == self.n_dp * self.n_seq else self.at_seq
        return jnp.array(places, jnp.int32) ^ here

    def order(self, *seq_bits, across):
        dp = tuple(range(self.seq_bits, self.seq_bits + self.dp_bits))
        rest = [bit for bit in range(self.seq_bits) if bit not in seq_bits]
        order = list(seq_bits) + rest
        return tuple(order[:across]) + dp + tuple(order[across:])

    def reduce(self, pair, order):
        keep, send = pair
        for k, bit in enumerate(order):
            got = self.swap(send, bit)
            if k == len(order) - 1:
                return keep + got
            half = keep.shape[0] // 2
            send = keep[half:] + got[half:]
            keep = keep[:half] + got[:half]


def scan_states(links, keep, send, decays, backwards):
    bits = links.seq_bits
    levels = []
    decay = None if backwards else decays
    kept = [] if not backwards else decays
    for bit in range(bits - 1):
        got = links.swap(send, bit)
        if backwards:
            mine_d, got_d = kept[bit]
        else:
            mine_d, got_d = decay, links.swap(decay, bit)
            kept.append((mine_d, got_d))
            decay = mine_d * got_d
        odd = (links.at_seq >> bit) & 1
        second = (odd == 0) if backwards else (odd == 1)
        levels.append((second, keep, got, mine_d, got_d))
        total = jnp.where(second, mine_d * got + keep, got_d * keep + got)
        half = total.shape[0] // 2
        if bit < bits - 2:
            keep, send = total[:half], total[half:]
        else:
            keep = total
    flip = 1 << (bits - 1)
    pairs = [(i, i ^ flip) for i in range(links.n_seq) if ((i >> (bits - 1)) & 1) == int(backwards)]
    state = lax.ppermute(keep, "seq", pairs)
    for bit in reversed(range(bits - 1)):
        second, keep, got, mine_d, got_d = levels[bit]
        theirs = jnp.where(second, state, mine_d * state + keep)
        mine = jnp.where(second, got_d * state + got, state)
        state = jnp.concatenate([mine, links.swap(theirs, bit)], axis=0)
    return state, kept


def local(
    block_in, doc_starts, cotangent, norm1_gain, w_query, w_key, w_value, w_outgate, w_rank_down,
    w_rank_up, decay_bias, group_gain, w_output, norm2_gain, w_ffgate, w_ffup, w_ffdown,
):
    row_count, length, width = block_in.shape
    tokens = row_count * length
    kw, vw = w_query.shape[1], w_value.shape[1]
    links = Links()
    parts = links.n_seq
    everyone = links.n_dp * links.n_seq
    dims = (row_count, length, width, kw, vw, doc_starts.shape[1], parts)
    x = block_in.reshape(tokens, width)
    cot = cotangent.reshape(tokens, width)
    docs = (doc_starts - links.at_seq * length).reshape(-1)

    levels = tuple(range(links.seq_bits - 1))
    step = 1 << len(levels)
    source = links.table(tuple(levels))
    size = parts // step
    low = links.at_seq & (step - 1)
    reverse = jnp.array(
        [sum(((p >> b) & 1) << (len(levels) - 1 - b) for b in levels) for p in range(step)], jnp.int32
    )
    source = reverse ^ low
    place = reverse[jnp.arange(step) ^ low]
    spread = jnp.arange(size)
    to_piece = (source[:, None] * size + spread).reshape(-1)
    to_place = (place[:, None] * size + spread).reshape(-1)
    state_table = jnp.concatenate([to_piece, to_place]).astype(jnp.int32)

    normed, q, k, v, og, ra, gp, cum, keep, send, decay = project_all(
        x, docs, state_table, norm1_gain, w_query, w_key, w_value, w_outgate, w_rank_down, w_rank_up,
        decay_bias, dims,
    )
    decay = decay.reshape(1, row_count, HEADS, 1, kw // HEADS)
    state_in, decays = scan_states(links, keep, send, decay, False)
    inner = inner_all(q, k, v, cum, docs, dims)
    mixed, gated, state_kept = mix_all(q, cum, inner, og, state_in, group_gain, docs, state_table, dims)

    hidden, dg, du, normed2, block_out, d_middle, d_out, d_gated, gnorm2 = ff_all(
        x, cot, gated, w_output, norm2_gain, w_ffgate, w_ffup, w_ffdown
    )
    d_mix, d_og, keep, send, ggroup = head_back_all(
        d_gated, og, mixed, q, cum, group_gain, docs, state_table, dims
    )
    state_grad, _ = scan_states(links, keep, send, decays, True)

    order_a = links.order(0, across=1)
    order_b = links.order(0, 1, across=2)
    table_a, table_b = links.table(order_a), links.table(order_b)
    (gate_pair,) = weight_grads(normed2, [dg], table_a)
    (up_pair,) = weight_grads(normed2, [du], table_b)
    (down_pair,) = weight_grads(hidden, [cot], table_a)
    (output_pair,) = weight_grads(gated, [d_out], table_b)
    (og_pair,) = weight_grads(normed, [d_og], table_b)
    g_ffgate = links.reduce(gate_pair, order_a)
    g_ffup = links.reduce(up_pair, order_b)
    g_ffdown = links.reduce(down_pair, order_a)
    g_output = links.reduce(output_pair, order_b)
    g_outgate = links.reduce(og_pair, order_b)

    d_qkv, d_rank, grup, gbias = mix_back_all(
        q, k, v, cum, gp, ra, d_mix, state_kept, state_grad, w_rank_up, docs, state_table, dims
    )
    (qkv_pair,) = weight_grads(normed, [d_qkv], table_a)
    g_qkv = links.reduce(qkv_pair, order_a)
    grad_in, gnorm1 = input_back_all(
        x, d_middle, d_qkv, d_og, d_rank, norm1_gain, w_query, w_key, w_value, w_outgate, w_rank_down
    )
    g_rank_down = tn(normed, d_rank)

    rank = w_rank_up.shape[0]
    by_device = lambda value: value.reshape(everyone, -1)
    small = [
        by_device(g_rank_down),
        grup.reshape(rank, everyone, kw // everyone).transpose(1, 0, 2).reshape(everyone, -1),
        by_device(gnorm1), by_device(gnorm2), by_device(gbias), by_device(ggroup),
    ]
    widths = [part.shape[1] for part in small]
    packed = jnp.concatenate(small, axis=1)
    packed = jnp.pad(packed, ((0, 0), (0, -packed.shape[1] % 128)))[table_a]
    packed = packed.reshape(everyone, 1, -1)
    packed = links.reduce((packed[: everyone // 2], packed[everyone // 2 :]), order_a).reshape(-1)
    out_small, at = [], 0
    for n in widths:
        out_small.append(packed[at : at + n])
        at += n
    s_down, s_up, s_norm1, s_norm2, s_bias, s_group = out_small
    g_qkv = g_qkv[0]
    return (
        block_out.reshape(row_count, length, width),
        grad_in.reshape(row_count, length, width),
        s_norm1,
        g_qkv[:, :kw],
        g_qkv[:, kw : 2 * kw],
        g_qkv[:, 2 * kw :],
        g_outgate[0],
        s_down.reshape(-1, rank),
        s_up.reshape(rank, -1),
        s_bias,
        s_group,
        g_output[0],
        s_norm2,
        g_ffgate[0],
        g_ffup[0],
        g_ffdown[0],
    )


def solution(mesh):
    tokens = P("dp", "seq", None)
    rows = P(("dp", "seq"), None)
    vector = P(("dp", "seq"))
    return jax.shard_map(
        local,
        mesh=mesh,
        in_specs=(tokens, P("dp", None), tokens) + (P(),) * 14,
        out_specs=(
            tokens, tokens, vector, rows, rows, rows, rows, rows, P(None, ("dp", "seq")), vector,
            vector, rows, vector, rows, rows, rows,
        ),
        check_vma=False,
    )
```

```python
import functools

import jax
import jax.numpy as jnp
from jax import lax
from jax.experimental import pallas as pl
from jax.experimental.pallas import tpu as pltpu
from jax.sharding import PartitionSpec as P

HEADS = 4
EPS = 1e-06
MIB = 1 << 20
BF = jnp.bfloat16
F32 = jnp.float32
HIGHEST = lax.Precision.HIGHEST


def nn(a, b, precision=None):
    return lax.dot_general(
        a, b, (((1,), (0,)), ((), ())), precision=precision, preferred_element_type=F32
    )


def nt(a, b):
    return lax.dot_general(a, b, (((1,), (1,)), ((), ())), preferred_element_type=F32)


def tn(a, b):
    return lax.dot_general(a, b, (((0,), (0,)), ((), ())), preferred_element_type=F32)


def shape(dims, dtype):
    return jax.ShapeDtypeStruct(dims, dtype)


def call(body, out_shape, grid, in_specs, out_specs, prefetch=0, scratch=(), flops=0, moved=0):
    return pl.pallas_call(
        body,
        out_shape=out_shape,
        grid_spec=pltpu.PrefetchScalarGridSpec(
            num_scalar_prefetch=prefetch,
            grid=grid,
            in_specs=in_specs,
            out_specs=out_specs,
            scratch_shapes=list(scratch),
        ),
        compiler_params=pltpu.CompilerParams(vmem_limit_bytes=56 * MIB),
        cost_estimate=pl.CostEstimate(flops=1, bytes_accessed=1, transcendentals=0),
    )


def block(dims, index):
    return pl.BlockSpec(dims, index)


def whole(dims):
    zero = (0,) * len(dims)
    return pl.BlockSpec(dims, lambda *_: zero)


def reset_masks(docs_ref, row, docs, length):
    at_i = lax.broadcasted_iota(jnp.int32, (length, length), 0)
    at_j = lax.broadcasted_iota(jnp.int32, (length, length), 1)
    token = lax.broadcasted_iota(jnp.int32, (length, 1), 0)
    visible = at_i >= at_j
    alive = token >= 0
    tail = token >= 0
    whole_alive = jnp.float32(1.0)
    for n in range(docs):
        start = docs_ref[row * docs + n]
        visible = visible & jnp.logical_not((at_j < start) & (start <= at_i))
        inside = (start >= 0) & (start < length)
        first = jnp.where(start >= 0, start, length)
        alive = alive & (token < first)
        last = jnp.where(start < length, start, -1)
        tail = tail & (token >= last)
        whole_alive = whole_alive * jnp.where(inside, 0.0, 1.0)
    return visible, alive.astype(F32), tail.astype(F32), whole_alive


def lower_ones(length, strict=False):
    at_i = lax.broadcasted_iota(jnp.int32, (length, length), 0)
    at_j = lax.broadcasted_iota(jnp.int32, (length, length), 1)
    return (at_i > at_j if strict else at_i >= at_j).astype(F32)


def project_body(
    rows, docs, length, hk, hv, parts,
    docs_ref, table_ref, x_ref, gain_ref, wq_ref, wk_ref, wv_ref, wog_ref, wrd_ref, wru_ref, bias_ref,
    normed_ref, q_ref, k_ref, v_ref, og_ref, ra_ref, gp_ref, cum_ref, keep_ref, send_ref, decay_ref,
    hold,
):
    x = x_ref[...].astype(F32)
    inv = lax.rsqrt(jnp.mean(x * x, axis=-1, keepdims=True) + EPS)
    normed = (x * inv * gain_ref[...]).astype(BF)
    normed_ref[...] = normed
    rank = nt(normed, wrd_ref[...]).astype(BF)
    ra_ref[...] = rank
    gate = nn(rank, wru_ref[...]) + bias_ref[...]
    gp_ref[...] = gate
    q_ref[...] = nn(normed, wq_ref[...]).astype(BF)
    key = nn(normed, wk_ref[...]).astype(BF)
    k_ref[...] = key
    value = nn(normed, wv_ref[...]).astype(BF)
    v_ref[...] = value
    og_ref[...] = nn(normed, wog_ref[...])
    log_decay = (jnp.minimum(gate, 0.0) - jnp.log1p(jnp.exp(-jnp.abs(gate)))) * (1.0 / 16.0)
    tri = lower_ones(length)
    size = hv // parts
    for r in range(rows):
        at = slice(r * length, (r + 1) * length)
        row = pl.program_id(0) * rows + r
        cum = nn(tri, log_decay[at], HIGHEST)
        cum_ref[at, :] = cum
        _, _, tail, whole_alive = reset_masks(docs_ref, row, docs, length)
        last = cum[length - 1 :, :]
        decay_ref[r] = jnp.exp(last) * whole_alive
        weighted = (key[at].astype(F32) * jnp.exp(last - cum) * tail).astype(BF)
        for h in range(HEADS):
            hold[...] = tn(value[at, h * hv : (h + 1) * hv], weighted[:, h * hk : (h + 1) * hk])
            for j in range(parts // 2):
                first = pl.multiple_of(table_ref[j] * size, size)
                keep_ref[j, r, h] = hold[pl.ds(first, size), :]
                second = pl.multiple_of(table_ref[parts // 2 + j] * size, size)
                send_ref[j, r, h] = hold[pl.ds(second, size), :]


def project_all(x, docs, table, gain, wq, wk, wv, wog, wrd, wru, bias, dims):
    row_count, length, width, kw, vw, ndocs, parts = dims
    tokens = row_count * length
    rows = 2 if row_count % 2 == 0 else 1
    tm = rows * length
    hk, hv = kw // HEADS, vw // HEADS
    rank = wrd.shape[0]
    size = hv // parts
    tile = lambda n: block((tm, n), lambda i, *_: (i, 0))
    half = (parts // 2, row_count, HEADS, size, hk)
    half_block = block((parts // 2, rows, HEADS, size, hk), lambda i, *_: (0, i, 0, 0, 0))
    body = functools.partial(project_body, rows, ndocs, length, hk, hv, parts)
    return call(
        body,
        (
            shape((tokens, width), BF),
            shape((tokens, kw), BF),
            shape((tokens, kw), BF),
            shape((tokens, vw), BF),
            shape((tokens, vw), F32),
            shape((tokens, rank), BF),
            shape((tokens, kw), F32),
            shape((tokens, kw), F32),
            shape(half, F32),
            shape(half, F32),
            shape((row_count, 1, kw), F32),
        ),
        (row_count // rows,),
        [
            tile(width), whole((1, width)), whole(wq.shape), whole(wk.shape), whole(wv.shape),
            whole(wog.shape), whole(wrd.shape), whole(wru.shape), whole((1, kw)),
        ],
        (
            tile(width), tile(kw), tile(kw), tile(vw), tile(vw), tile(rank), tile(kw), tile(kw),
            half_block, half_block, block((rows, 1, kw), lambda i, *_: (i, 0, 0)),
        ),
        prefetch=2,
        scratch=[pltpu.VMEM((hv, hk), F32)],
        flops=2 * tokens * width * (2 * kw + 2 * vw),
        moved=20 * MIB,
    )(docs, table, x, gain.reshape(1, -1), wq, wk, wv, wog, wrd, wru, bias.reshape(1, -1))


def span_factors(cum, length):
    middle = cum[length // 2 - 1 : length // 2, :]
    return jnp.exp(cum - middle), jnp.exp(middle - cum)


def inner_body(docs, length, hk, hv, docs_ref, q_ref, k_ref, v_ref, cum_ref, inner_ref):
    visible, _, _, _ = reset_masks(docs_ref, pl.program_id(0), docs, length)
    up, down = span_factors(cum_ref[...], length)
    q = (q_ref[...].astype(F32) * up).astype(BF)
    k = (k_ref[...].astype(F32) * down).astype(BF)
    for h in range(HEADS):
        kk = slice(h * hk, (h + 1) * hk)
        vv = slice(h * hv, (h + 1) * hv)
        scores = jnp.where(visible, nt(q[:, kk], k[:, kk]), 0.0).astype(BF)
        inner_ref[:, vv] = nn(scores, v_ref[:, vv])


def inner_all(q, k, v, cum, docs, dims):
    row_count, length, width, kw, vw, ndocs, parts = dims
    tokens = row_count * length
    tile = lambda n: block((length, n), lambda i, *_: (i, 0))
    return call(
        functools.partial(inner_body, ndocs, length, kw // HEADS, vw // HEADS),
        shape((tokens, vw), F32),
        (row_count,),
        [tile(kw), tile(kw), tile(vw), tile(kw)],
        tile(vw),
        prefetch=1,
        flops=2 * tokens * length * (kw + vw),
        moved=8 * MIB,
    )(docs, q, k, v, cum)


def gather_state(near_ref, far_ref, table_ref, h, parts):
    half = parts // 2
    pieces = []
    for p in range(parts):
        place = table_ref[parts + p]
        near = near_ref[jnp.minimum(place, half - 1), 0, h]
        far = far_ref[jnp.maximum(place - half, 0), 0, h]
        pieces.append(jnp.where(place < half, near, far))
    return jnp.concatenate(pieces, axis=0)


def mix_body(
    docs, length, hk, hv, parts,
    docs_ref, table_ref, q_ref, cum_ref, inner_ref, og_ref, near_ref, far_ref, gain_ref,
    mixed_ref, gated_ref, kept_ref,
):
    _, alive, _, _ = reset_masks(docs_ref, pl.program_id(0), docs, length)
    reach = (q_ref[...].astype(F32) * jnp.exp(cum_ref[...]) * alive).astype(BF)
    scale = hk ** (-0.5)
    for h in range(HEADS):
        kk = slice(h * hk, (h + 1) * hk)
        vv = slice(h * hv, (h + 1) * hv)
        state = gather_state(near_ref, far_ref, table_ref, h, parts).astype(BF)
        kept_ref[0, h] = state
        mixed = scale * (inner_ref[:, vv] + nt(reach[:, kk], state))
        mixed_ref[:, vv] = mixed
        inv = lax.rsqrt(jnp.mean(mixed * mixed, axis=-1, keepdims=True) + EPS)
        og = og_ref[:, vv]
        gated_ref[:, vv] = (mixed * inv * gain_ref[...] * og * jax.nn.sigmoid(og)).astype(BF)


def mix_all(q, cum, inner, og, near, far, gain, docs, table, dims):
    row_count, length, width, kw, vw, ndocs, parts = dims
    tokens = row_count * length
    hk, hv = kw // HEADS, vw // HEADS
    tile = lambda n: block((length, n), lambda i, *_: (i, 0))
    half = block((parts // 2, 1, HEADS, hv // parts, hk), lambda i, *_: (0, i, 0, 0, 0))
    return call(
        functools.partial(mix_body, ndocs, length, hk, hv, parts),
        (
            shape((tokens, vw), F32),
            shape((tokens, vw), BF),
            shape((row_count, HEADS, hv, hk), BF),
        ),
        (row_count,),
        [
            tile(kw), tile(kw), tile(vw), tile(vw), half, half, whole((1, hv)),
        ],
        (tile(vw), tile(vw), block((1, HEADS, hv, hk), lambda i, *_: (i, 0, 0, 0))),
        prefetch=2,
        flops=2 * tokens * hk * vw,
        moved=18 * MIB,
    )(docs, table, q, cum, inner, og, near, far, gain.reshape(1, -1))


def ff_body(
    steps,
    x_ref, cot_ref, gated_ref, wo_ref, gain_ref, wg_ref, wu_ref, wd_ref, dh_ref,
    hidden_ref, dg_ref, du_ref, normed2_ref, out_ref, dmid_ref, dout_ref, dgated_ref, gnorm_ref,
    middle, total, back,
):
    step = pl.program_id(0)

    @pl.when(step == 0)
    def _():
        mid = x_ref[...].astype(F32) + nn(gated_ref[...], wo_ref[...])
        middle[...] = mid
        inv = lax.rsqrt(jnp.mean(mid * mid, axis=-1, keepdims=True) + EPS)
        normed2_ref[...] = (mid * inv * gain_ref[...]).astype(BF)

    normed2 = normed2_ref[...]
    gate = nn(normed2, wg_ref[...])
    up = nn(normed2, wu_ref[...])
    d_hidden = dh_ref[...]
    sig = jax.nn.sigmoid(gate)
    act = gate * sig
    hidden = (act * up).astype(BF)
    dg = (d_hidden * up * sig * (1.0 + gate * (1.0 - sig))).astype(BF)
    du = (d_hidden * act).astype(BF)
    hidden_ref[...] = hidden
    dg_ref[...] = dg
    du_ref[...] = du
    more = nn(hidden, wd_ref[...])
    more_back = nt(dg, wg_ref[...]) + nt(du, wu_ref[...])

    @pl.when(step == 0)
    def _():
        total[...] = more
        back[...] = more_back

    @pl.when(step > 0)
    def _():
        total[...] += more
        back[...] += more_back

    @pl.when(step == steps - 1)
    def _():
        mid = middle[...]
        out_ref[...] = (mid + total[...]).astype(BF)
        inv = lax.rsqrt(jnp.mean(mid * mid, axis=-1, keepdims=True) + EPS)
        d_normed2 = back[...]
        gnorm_ref[...] = jnp.sum(d_normed2 * mid * inv, axis=0, keepdims=True)
        scaled = d_normed2 * gain_ref[...]
        d_middle = (
            cot_ref[...].astype(F32)
            + inv * scaled
            - mid * (inv * inv * inv) * jnp.mean(scaled * mid, axis=-1, keepdims=True)
        )
        dmid_ref[...] = d_middle
        d_out = d_middle.astype(BF)
        dout_ref[...] = d_out
        dgated_ref[...] = nt(d_out, wo_ref[...])


def hidden_back_body(cot_ref, wd_ref, dh_ref):
    dh_ref[...] = nt(cot_ref[...], wd_ref[...])


def hidden_back_all(cot, wd):
    tokens, width = cot.shape
    ff, tile = wd.shape[0], 256
    return call(
        hidden_back_body,
        shape((tokens, ff), F32),
        (ff // tile,),
        [whole((tokens, width)), block((tile, width), lambda i: (i, 0))],
        block((tokens, tile), lambda i: (0, i)),
        flops=2 * tokens * width * ff,
        moved=16 * MIB,
    )(cot, wd)


def ff_all(x, cot, gated, wo, gain, wg, wu, wd, dh):
    tokens, width = x.shape
    vw = gated.shape[1]
    ff = wg.shape[1]
    tile = 256
    steps = ff // tile
    col = lambda n: block((n, tile), lambda i: (0, i))
    once = lambda dims: pl.BlockSpec(dims, lambda i: (0, 0), pipeline_mode=pl.Buffered(1))
    return call(
        functools.partial(ff_body, steps),
        (
            shape((tokens, ff), BF), shape((tokens, ff), BF), shape((tokens, ff), BF),
            shape((tokens, width), BF), shape((tokens, width), BF), shape((tokens, width), F32),
            shape((tokens, width), BF), shape((tokens, vw), F32), shape((1, width), F32),
        ),
        (steps,),
        [
            once((tokens, width)), once((tokens, width)), once((tokens, vw)), once(wo.shape),
            once((1, width)), col(width), col(width), block((tile, width), lambda i: (i, 0)), col(tokens),
        ],
        (
            col(tokens), col(tokens), col(tokens),
            whole((tokens, width)), whole((tokens, width)), whole((tokens, width)),
            whole((tokens, width)), whole((tokens, vw)), whole((1, width)),
        ),
        scratch=[pltpu.VMEM((tokens, width), F32)] * 3,
        flops=10 * tokens * width * ff,
        moved=45 * MIB,
    )(x, cot, gated, wo, gain.reshape(1, -1), wg, wu, wd, dh)


def head_back_body(
    docs, length, hk, hv, parts,
    docs_ref, table_ref, dgated_ref, og_ref, mixed_ref, q_ref, cum_ref, gain_ref,
    dmix_ref, dog_ref, keep_ref, send_ref, ggroup_ref,
    hold,
):
    row = pl.program_id(0)
    _, alive, _, _ = reset_masks(docs_ref, row, docs, length)
    reach = (q_ref[...].astype(F32) * jnp.exp(cum_ref[...]) * alive).astype(BF)
    scale = hk ** (-0.5)
    size = hv // parts
    ggroup = jnp.zeros((1, hv), F32)
    for h in range(HEADS):
        kk = slice(h * hk, (h + 1) * hk)
        vv = slice(h * hv, (h + 1) * hv)
        mixed = mixed_ref[:, vv]
        inv = lax.rsqrt(jnp.mean(mixed * mixed, axis=-1, keepdims=True) + EPS)
        og = og_ref[:, vv]
        sig = jax.nn.sigmoid(og)
        dgated = dgated_ref[:, vv]
        unit = mixed * inv
        dog_ref[:, vv] = (
            dgated * unit * gain_ref[...] * sig * (1.0 + og * (1.0 - sig))
        ).astype(BF)
        d_heads = dgated * og * sig
        ggroup = ggroup + jnp.sum(d_heads * unit, axis=0, keepdims=True)
        scaled = d_heads * gain_ref[...]
        d_mixed = inv * scaled - mixed * (inv * inv * inv) * jnp.mean(
            scaled * mixed, axis=-1, keepdims=True
        )
        d_mixed = (scale * d_mixed).astype(BF)
        dmix_ref[:, vv] = d_mixed
        hold[...] = tn(d_mixed, reach[:, kk])
        for j in range(parts // 2):
            first = pl.multiple_of(table_ref[j] * size, size)
            keep_ref[j, 0, h] = hold[pl.ds(first, size), :]
            second = pl.multiple_of(table_ref[parts // 2 + j] * size, size)
            send_ref[j, 0, h] = hold[pl.ds(second, size), :]

    @pl.when(row == 0)
    def _():
        ggroup_ref[...] = ggroup

    @pl.when(row > 0)
    def _():
        ggroup_ref[...] += ggroup


def head_back_all(dgated, og, mixed, q, cum, gain, docs, table, dims):
    row_count, length, width, kw, vw, ndocs, parts = dims
    tokens = row_count * length
    hk, hv = kw // HEADS, vw // HEADS
    size = hv // parts
    tile = lambda n: block((length, n), lambda i, *_: (i, 0))
    half = (parts // 2, row_count, HEADS, size, hk)
    half_block = block((parts // 2, 1, HEADS, size, hk), lambda i, *_: (0, i, 0, 0, 0))
    return call(
        functools.partial(head_back_body, ndocs, length, hk, hv, parts),
        (
            shape((tokens, vw), BF), shape((tokens, vw), BF),
            shape(half, F32), shape(half, F32), shape((1, hv), F32),
        ),
        (row_count,),
        [tile(vw), tile(vw), tile(vw), tile(kw), tile(kw), whole((1, hv))],
        (tile(vw), tile(vw), half_block, half_block, whole((1, hv))),
        prefetch=2,
        scratch=[pltpu.VMEM((hv, hk), F32)],
        flops=2 * tokens * hk * vw,
        moved=20 * MIB,
    )(docs, table, dgated, og, mixed, q, cum, gain.reshape(1, -1))


def mix_back_body(
    docs, length, hk, hv, parts,
    docs_ref, table_ref, q_ref, k_ref, v_ref, cum_ref, gp_ref, ra_ref, dmix_ref, state_ref, near_ref,
    far_ref, wru_ref,
    dqkv_ref, drank_ref, grup_ref, gbias_ref,
):
    row = pl.program_id(0)
    kw = HEADS * hk
    visible, alive, tail, whole_alive = reset_masks(docs_ref, row, docs, length)
    cum = cum_ref[...]
    last = cum[length - 1 :, :]
    up, down = span_factors(cum, length)
    from_start = jnp.exp(cum) * alive
    to_end = jnp.exp(last - cum) * tail
    total = jnp.exp(last) * whole_alive
    q = q_ref[...].astype(F32)
    k = k_ref[...].astype(F32)
    q_span = (q * up).astype(BF)
    k_span = (k * down).astype(BF)
    reach = (q * from_start).astype(BF)
    weighted = (k * to_end).astype(BF)
    later, earlier, crossing = [], [], []
    for h in range(HEADS):
        kk = slice(h * hk, (h + 1) * hk)
        vv = slice(h * hv, (h + 1) * hv)
        qs, ks = q_span[:, kk], k_span[:, kk]
        d_mix = dmix_ref[:, vv]
        value = v_ref[:, vv]
        state = state_ref[0, h]
        grad32 = gather_state(near_ref, far_ref, table_ref, h, parts)
        grad = grad32.astype(BF)
        scores = jnp.where(visible, nt(qs, ks), 0.0).astype(BF)
        d_scores = jnp.where(visible, nt(d_mix, value), 0.0).astype(BF)
        dq_in = nn(d_scores, ks)
        dk_in = tn(d_scores, qs)
        dq_out = nn(d_mix, state)
        dk_out = nn(value, grad)
        dqkv_ref[:, kk] = (dq_in * up[:, kk] + dq_out * from_start[:, kk]).astype(BF)
        dqkv_ref[:, kw + h * hk : kw + (h + 1) * hk] = (
            dk_in * down[:, kk] + dk_out * to_end[:, kk]
        ).astype(BF)
        dqkv_ref[:, 2 * kw + h * hv : 2 * kw + (h + 1) * hv] = (
            tn(scores, d_mix) + nt(weighted[:, kk], grad)
        ).astype(BF)
        later.append(
            qs.astype(F32) * dq_in - ks.astype(F32) * dk_in + reach[:, kk].astype(F32) * dq_out
        )
        earlier.append(weighted[:, kk].astype(F32) * dk_out)
        crossing.append(jnp.sum(state.astype(F32) * grad32, axis=0, keepdims=True))
    later = jnp.concatenate(later, axis=1)
    earlier = jnp.concatenate(earlier, axis=1)
    crossing = jnp.concatenate(crossing, axis=1)
    at_i = lax.broadcasted_iota(jnp.int32, (length, length), 0)
    at_j = lax.broadcasted_iota(jnp.int32, (length, length), 1)
    after = (at_i <= at_j).astype(F32)
    before = (at_i > at_j).astype(F32)
    d_decay = nn(after, later, HIGHEST) + nn(before, earlier, HIGHEST) + total * crossing
    d_gate = (d_decay * jax.nn.sigmoid(-gp_ref[...]) * (1.0 / 16.0)).astype(BF)
    drank_ref[...] = nt(d_gate, wru_ref[...]).astype(BF)
    grup = tn(ra_ref[...], d_gate)
    gbias = jnp.sum(d_gate.astype(F32), axis=0, keepdims=True)

    @pl.when(row == 0)
    def _():
        grup_ref[...] = grup
        gbias_ref[...] = gbias

    @pl.when(row > 0)
    def _():
        grup_ref[...] += grup
        gbias_ref[...] += gbias


def mix_back_all(q, k, v, cum, gp, ra, dmix, state, near, far, wru, docs, table, dims):
    row_count, length, width, kw, vw, ndocs, parts = dims
    tokens = row_count * length
    hk, hv = kw // HEADS, vw // HEADS
    rank = wru.shape[0]
    tile = lambda n: block((length, n), lambda i, *_: (i, 0))
    half = block((parts // 2, 1, HEADS, hv // parts, hk), lambda i, *_: (0, i, 0, 0, 0))
    return call(
        functools.partial(mix_back_body, ndocs, length, hk, hv, parts),
        (
            shape((tokens, 2 * kw + vw), BF), shape((tokens, rank), BF),
            shape((rank, kw), F32), shape((1, kw), F32),
        ),
        (row_count,),
        [
            tile(kw), tile(kw), tile(vw), tile(kw), tile(kw), tile(rank), tile(vw),
            block((1, HEADS, hv, hk), lambda i, *_: (i, 0, 0, 0)),
            half, half, whole((rank, kw)),
        ],
        (tile(2 * kw + vw), tile(rank), whole((rank, kw)), whole((1, kw))),
        prefetch=2,
        flops=16 * tokens * length * vw,
        moved=16 * MIB,
    )(docs, table, q, k, v, cum, gp, ra, dmix, state, near, far, wru)


def input_back_body(
    kw, vw,
    x_ref, dmid_ref, dqkv_ref, dog_ref, drank_ref, gain_ref, wq_ref, wk_ref, wv_ref, wog_ref, wrd_ref,
    gin_ref, gnorm_ref,
):
    step = pl.program_id(0)
    d_normed = (
        nt(dqkv_ref[:, :kw], wq_ref[...])
        + nt(dqkv_ref[:, kw : 2 * kw], wk_ref[...])
        + nt(dqkv_ref[:, 2 * kw :], wv_ref[...])
        + nt(dog_ref[...], wog_ref[...])
        + nn(drank_ref[...], wrd_ref[...])
    )
    x = x_ref[...].astype(F32)
    inv = lax.rsqrt(jnp.mean(x * x, axis=-1, keepdims=True) + EPS)
    gnorm = jnp.sum(d_normed * x * inv, axis=0, keepdims=True)
    scaled = d_normed * gain_ref[...]
    gin_ref[...] = (
        dmid_ref[...]
        + inv * scaled
        - x * (inv * inv * inv) * jnp.mean(scaled * x, axis=-1, keepdims=True)
    )

    @pl.when(step == 0)
    def _():
        gnorm_ref[...] = gnorm

    @pl.when(step > 0)
    def _():
        gnorm_ref[...] += gnorm


def input_back_all(x, dmid, dqkv, dog, drank, gain, wq, wk, wv, wog, wrd):
    tokens, width = x.shape
    kw, vw = wq.shape[1], wv.shape[1]
    tm = 256 if tokens % 256 == 0 else 128
    tile = lambda n: block((tm, n), lambda i: (i, 0))
    return call(
        functools.partial(input_back_body, kw, vw),
        (shape((tokens, width), F32), shape((1, width), F32)),
        (tokens // tm,),
        [
            tile(width), tile(width), tile(2 * kw + vw), tile(vw), tile(drank.shape[1]),
            whole((1, width)), whole(wq.shape), whole(wk.shape), whole(wv.shape), whole(wog.shape),
            whole(wrd.shape),
        ],
        (tile(width), whole((1, width))),
        flops=2 * tokens * width * (2 * kw + 2 * vw),
        moved=20 * MIB,
    )(x, dmid, dqkv, dog, drank, gain.reshape(1, -1), wq, wk, wv, wog, wrd)


def weight_body(count, pieces, per, table_ref, *refs):
    lefts, rights = refs[:count], refs[count : 2 * count]
    keep_ref, send_ref, hold = refs[2 * count : 2 * count + 3]
    turned = refs[2 * count + 3 :]

    @pl.when(pl.program_id(0) == 0)
    def _():
        for n in range(count):
            turned[n][...] = lefts[n][...].T

    for n in range(count):
        hold[...] = nn(turned[n][...], rights[n][...])
        at = slice(n * per, (n + 1) * per)
        for j in range(pieces // 2):
            first = pl.multiple_of(table_ref[j] * per, per)
            keep_ref[j, at, :] = hold[pl.ds(first, per), :]
            second = pl.multiple_of(table_ref[pieces // 2 + j] * per, per)
            send_ref[j, at, :] = hold[pl.ds(second, per), :]


def weight_grads(pairs, table):
    count, pieces = len(pairs), table.shape[0]
    tokens, rows = pairs[0][0].shape
    per = rows // pieces
    cols = pairs[0][1].shape[1]
    if per % 8:
        both = [tn(left, right) for left, right in pairs]
        parts = jnp.concatenate([part.reshape(pieces, per, cols) for part in both], axis=1)[table]
        return parts[: pieces // 2], parts[pieces // 2 :]
    tile = next(n for n in (1408, 512, 256, 128) if cols % n == 0)
    half = shape((pieces // 2, count * per, cols), F32)
    half_block = block((pieces // 2, count * per, tile), lambda i, *_: (0, 0, i))
    return call(
        functools.partial(weight_body, count, pieces, per),
        (half, half),
        (cols // tile,),
        [whole((tokens, rows))] * count
        + [block((tokens, tile), lambda i, *_: (0, i))] * count,
        (half_block, half_block),
        prefetch=1,
        scratch=[pltpu.VMEM((rows, tile), F32)] + [pltpu.VMEM((rows, tokens), BF)] * count,
        flops=2 * tokens * rows * cols * count,
        moved=4 * rows * cols * count,
    )(table, *[left for left, _ in pairs], *[right for _, right in pairs])


def bits_of(n):
    return n.bit_length() - 1


class Links:
    def __init__(self):
        self.n_dp, self.n_seq = lax.axis_size("dp"), lax.axis_size("seq")
        self.seq_bits, self.dp_bits = bits_of(self.n_seq), bits_of(self.n_dp)
        self.at_seq = lax.axis_index("seq")
        self.me = lax.axis_index("dp") * self.n_seq + self.at_seq

    def swap(self, value, bit):
        name, n, flip = "seq", self.n_seq, 1 << bit
        if bit >= self.seq_bits:
            name, n, flip = "dp", self.n_dp, 1 << (bit - self.seq_bits)
        return lax.ppermute(value, name, [(i, i ^ flip) for i in range(n)])

    def table(self, order):
        n = 1 << len(order)
        places = [
            sum(((at >> (len(order) - 1 - k)) & 1) << bit for k, bit in enumerate(order))
            for at in range(n)
        ]
        here = self.me if n == self.n_dp * self.n_seq else self.at_seq
        return jnp.array(places, jnp.int32) ^ here

    def order(self, *names):
        across = tuple(range(self.seq_bits, self.seq_bits + self.dp_bits))
        bits = [0]
        for name in names:
            bits.extend(across if name == "x" else [{"y": 1, "z0": 2, "z1": 3}[name]])
        return tuple(bits) + tuple(b for b in range(self.seq_bits) if b not in bits)


class Turns:
    def __init__(self):
        self.last = ()

    def after(self, value):
        return lax.optimization_barrier((value,) + self.last)[0]

    def done(self, *values):
        self.last = values


class Task:
    def __init__(self, steps):
        self.steps, self.wanted, self.got, self.begun, self.over = steps, [], None, False, False

    def advance(self, turns):
        if self.over:
            return
        if self.wanted:
            start([self], turns)
        try:
            self.wanted = self.steps.send(self.got) if self.begun else next(self.steps)
            self.begun = True
        except StopIteration:
            self.wanted, self.over = [], True

    def finish(self, turns):
        while not self.over:
            self.advance(turns)


def start(tasks, turns):
    tasks = [task for task in tasks if task.wanted]
    values = [value for task in tasks for value, _ in task.wanted]
    if not values:
        return
    tied = lax.optimization_barrier(tuple(values) + turns.last)[: len(values)]
    turns.done(tied[0])
    tied = iter(tied)
    for task in tasks:
        task.got = [move(next(tied)) for _, move in task.wanted]
        task.wanted = []


def reduce_steps(links, turns, make, order, out, name, halves=False):
    keep, send = make()
    turns.done(keep, send)
    for k, bit in enumerate(order):
        swap = functools.partial(links.swap, bit=bit)
        half = keep.shape[0] // 2
        if halves and k == 0:
            near, far = yield [(send[:half], swap), (send[half:], swap)]
        else:
            (got,) = yield [(send, swap)]
            near, far = got[:half], got[half:]
        keep = turns.after(keep)
        if k == len(order) - 1:
            out[name] = keep + got
            turns.done(out[name])
            return
        send = keep[half:] + far
        keep = keep[:half] + near
        turns.done(keep, send)


def scan_steps(links, turns, make, decays, backwards, out):
    keep, send, decay = make()
    bits = links.seq_bits
    levels = []
    kept = [] if decays is None else decays
    turns.done(keep, send)
    for bit in range(bits - 1):
        swap = functools.partial(links.swap, bit=bit)
        if decays is None:
            got, got_d = yield [(send, swap), (decay, swap)]
            kept.append((decay, got_d))
            decay = decay * got_d
        else:
            (got,) = yield [(send, swap)]
        mine_d, got_d = kept[bit]
        keep = turns.after(keep)
        odd = (links.at_seq >> bit) & 1
        second = (odd == 0) if backwards else (odd == 1)
        levels.append((second, keep, got, mine_d, got_d))
        total = jnp.where(second, mine_d * got + keep, got_d * keep + got)
        half = total.shape[0] // 2
        if bit < bits - 2:
            keep, send = total[:half], total[half:]
            turns.done(keep, send)
        else:
            send = total
            turns.done(send)
    flip = 1 << (bits - 1)
    pairs = [(i, i ^ flip) for i in range(links.n_seq) if ((i >> (bits - 1)) & 1) == int(backwards)]
    (state,) = yield [(send, lambda value: lax.ppermute(value, "seq", pairs))]
    for bit in reversed(range(bits - 1)):
        second, keep, got, mine_d, got_d = levels[bit]
        keep = turns.after(keep)
        theirs = jnp.where(second, state, mine_d * state + keep)
        mine = jnp.where(second, got_d * state + got, state)
        turns.done(theirs, mine)
        (far,) = yield [(theirs, functools.partial(links.swap, bit=bit))]
        if bit == 0:
            out["near"], out["far"], out["decays"] = mine, far, kept
        else:
            mine = turns.after(mine)
            state = jnp.concatenate([mine, far], axis=0)


ROUTES = {
    "gate": ("x", "y", "z0", "z1"),
    "up": ("y", "z0", "x", "z1"),
    "down": ("z0", "x", "y", "z1"),
    "mid": ("x", "y", "z0", "z1"),
    "qkv": ("y", "x", "z0", "z1"),
    "small": ("x", "y", "z0", "z1"),
}
SCHEDULE = (
    "scan", ("scan",), "gate", "scan", ("scan", "gate"), "up", "gate", "scan", ("scan", "up"),
    "down", "up", "scan", ("scan", "down"), "mid", "down", "scan", ("scan", "mid", "gate"),
    "mid", "scan", ("scan", "down"), "scan", ("scan", "up"), "scan", "qkv", "gate", ("qkv",
    "mid"), "up", "down", "qkv", ("up", "qkv", "down"), "small", ("small",), "mid", "small",
    ("small", "gate"), "up", ("up",), "small", ("small",), "down", ("mid",), "qkv", ("down",),
    "small", ("small",), "gate", ("qkv",), "up", ("gate",), "small", ("small",), "mid", ("up",),
    "down", ("mid",), "small", "qkv", ("down",), "gate", ("qkv",), "up", ("gate",), "mid",
    ("mid",), "down", "qkv", ("qkv",), "gate", "mid", "qkv",
)


def local(
    block_in, doc_starts, cotangent, norm1_gain, w_query, w_key, w_value, w_outgate, w_rank_down,
    w_rank_up, decay_bias, group_gain, w_output, norm2_gain, w_ffgate, w_ffup, w_ffdown,
):
    row_count, length, width = block_in.shape
    tokens = row_count * length
    kw, vw = w_query.shape[1], w_value.shape[1]
    links, turns = Links(), Turns()
    parts = links.n_seq
    everyone = links.n_dp * links.n_seq
    dims = (row_count, length, width, kw, vw, doc_starts.shape[1], parts)
    x = block_in.reshape(tokens, width)
    cot = cotangent.reshape(tokens, width)
    docs = (doc_starts - links.at_seq * length).reshape(-1)
    rank_down_t = w_rank_down.T

    levels = range(links.seq_bits - 1)
    step = 1 << len(levels)
    size = parts // step
    low = links.at_seq & (step - 1)
    reverse = jnp.array(
        [sum(((p >> b) & 1) << (len(levels) - 1 - b) for b in levels) for p in range(step)], jnp.int32
    )
    spread = jnp.arange(size)
    to_piece = ((reverse ^ low)[:, None] * size + spread).reshape(-1)
    to_place = (reverse[jnp.arange(step) ^ low][:, None] * size + spread).reshape(-1)
    state_table = jnp.concatenate([to_piece, to_place]).astype(jnp.int32)

    normed, q, k, v, og, ra, gp, cum, keep, send, decay = project_all(
        x, docs, state_table, norm1_gain, w_query, w_key, w_value, w_outgate, rank_down_t, w_rank_up,
        decay_bias, dims,
    )
    decay = decay.reshape(1, row_count, HEADS, 1, kw // HEADS)
    fwd = {}
    scan = Task(scan_steps(links, turns, lambda: (keep, send, decay), None, False, fwd))
    scan.advance(turns)
    scan.advance(turns)
    start([scan], turns)
    dh = hidden_back_all(turns.after(cot), w_ffdown)
    turns.done(dh)
    scan.advance(turns)
    start([scan], turns)
    inner = inner_all(q, k, v, cum, turns.after(docs), dims)
    turns.done(inner)
    scan.finish(turns)
    mixed, gated, state_kept = mix_all(
        q, cum, inner, og, fwd["near"], fwd["far"], group_gain, turns.after(docs), state_table, dims
    )
    hidden, dg, du, normed2, block_out, d_middle, d_out, d_gated, gnorm2 = ff_all(
        x, cot, gated, w_output, norm2_gain, w_ffgate, w_ffup, w_ffdown, dh
    )

    routes = {name: links.order(*route) for name, route in ROUTES.items()}
    tables = {route: links.table(route) for route in set(routes.values())}
    back, grads, held = {}, {}, {}
    ff = w_ffgate.shape[1]

    def head_back():
        d_mix, d_og, keep, send, ggroup = head_back_all(
            d_gated, og, mixed, q, cum, group_gain, turns.after(docs), state_table, dims
        )
        held.update(d_mix=d_mix, d_og=d_og, ggroup=ggroup)
        return keep, send, None

    def all_back():
        yield from scan_steps(links, turns, head_back, fwd["decays"], True, back)
        held["d_qkv"], held["d_rank"], held["grup"], held["gbias"] = mix_back_all(
            q, k, v, cum, gp, ra, held["d_mix"], state_kept, back["near"], back["far"], w_rank_up,
            turns.after(docs), state_table, dims,
        )
        turns.done(held["d_rank"])

    def weights(name, pairs, halves=False):
        order = routes[name]
        make = lambda: weight_grads(pairs(), turns.after(tables[order]))
        return reduce_steps(links, turns, make, order, grads, name, halves)

    def small_steps():
        grad_in, gnorm1 = input_back_all(
            x, d_middle, held["d_qkv"], held["d_og"], held["d_rank"], turns.after(norm1_gain), w_query,
            w_key, w_value, w_outgate, rank_down_t,
        )
        held["grad_in"] = grad_in
        by_device = lambda value: value.reshape(everyone, -1)
        small = [
            by_device(tn(normed, held["d_rank"])),
            held["grup"].reshape(rank, everyone, -1).transpose(1, 0, 2).reshape(everyone, -1),
            by_device(gnorm1), by_device(gnorm2), by_device(held["gbias"]), by_device(held["ggroup"]),
        ]
        held["widths"] = [part.shape[1] for part in small]
        packed = jnp.concatenate(small, axis=1)
        packed = jnp.pad(packed, ((0, 0), (0, -packed.shape[1] % 128)))[tables[routes["small"]]]
        packed = packed.reshape(everyone, 1, -1)
        make = lambda: (packed[: everyone // 2], packed[everyone // 2 :])
        yield from reduce_steps(links, turns, make, routes["small"], grads, "small")

    rank = w_rank_up.shape[0]
    work = {
        "scan": all_back(),
        "gate": weights("gate", lambda: [(normed2, dg)]),
        "up": weights("up", lambda: [(normed2, du)]),
        "down": weights("down", lambda: [(hidden, cot)]),
        "mid": weights("mid", lambda: [(gated, d_out), (normed, held["d_og"])]),
        "qkv": weights("qkv", lambda: [(normed, held["d_qkv"])], True),
        "small": small_steps(),
    }
    work = {name: Task(steps) for name, steps in work.items()}
    for name in SCHEDULE + tuple(work) * (2 * len(routes["gate"])):
        if isinstance(name, tuple):
            start([work[each] for each in name], turns)
            continue
        if name in ("qkv", "small"):
            work["scan"].finish(turns)
        work[name].advance(turns)

    packed = grads["small"].reshape(-1)
    out_small, at = [], 0
    for n in held["widths"]:
        out_small.append(packed[at : at + n])
        at += n
    s_down, s_up, s_norm1, s_norm2, s_bias, s_group = out_small
    per = width // everyone
    mid, qkv = grads["mid"][0], grads["qkv"][0]
    return (
        block_out.reshape(row_count, length, width),
        held["grad_in"].reshape(row_count, length, width),
        s_norm1,
        qkv[:, :kw],
        qkv[:, kw : 2 * kw],
        qkv[:, 2 * kw :],
        mid[per:],
        s_down.reshape(-1, rank),
        s_up.reshape(rank, -1),
        s_bias,
        s_group,
        mid[:per],
        s_norm2,
        grads["gate"][0],
        grads["up"][0],
        grads["down"][0],
    )


def solution(mesh):
    tokens = P("dp", "seq", None)
    rows = P(("dp", "seq"), None)
    vector = P(("dp", "seq"))
    return jax.shard_map(
        local,
        mesh=mesh,
        in_specs=(tokens, P("dp", None), tokens) + (P(),) * 14,
        out_specs=(
            tokens, tokens, vector, rows, rows, rows, rows, rows, P(None, ("dp", "seq")), vector,
            vector, rows, vector, rows, rows, rows,
        ),
        check_vma=False,
    )
```

```python
import functools

import jax
import jax.numpy as jnp
from jax import lax
from jax.experimental import pallas as pl
from jax.experimental.pallas import tpu as pltpu
from jax.sharding import PartitionSpec as P

HEADS = 4
EPS = 1e-06
MIB = 1 << 20
BF = jnp.bfloat16
F32 = jnp.float32
HIGHEST = lax.Precision.HIGHEST


def nn(a, b, precision=None):
    return lax.dot_general(
        a, b, (((1,), (0,)), ((), ())), precision=precision, preferred_element_type=F32
    )


def nt(a, b):
    return lax.dot_general(a, b, (((1,), (1,)), ((), ())), preferred_element_type=F32)


def tn(a, b):
    return lax.dot_general(a, b, (((0,), (0,)), ((), ())), preferred_element_type=F32)


def shape(dims, dtype):
    return jax.ShapeDtypeStruct(dims, dtype)


def call(body, out_shape, grid, in_specs, out_specs, prefetch=0, scratch=()):
    return pl.pallas_call(
        body,
        out_shape=out_shape,
        grid_spec=pltpu.PrefetchScalarGridSpec(
            num_scalar_prefetch=prefetch,
            grid=grid,
            in_specs=in_specs,
            out_specs=out_specs,
            scratch_shapes=list(scratch),
        ),
        compiler_params=pltpu.CompilerParams(vmem_limit_bytes=60 * MIB),
        cost_estimate=pl.CostEstimate(flops=1, bytes_accessed=1, transcendentals=0),
    )


def block(dims, index):
    return pl.BlockSpec(dims, index)


def whole(dims):
    zero = (0,) * len(dims)
    return pl.BlockSpec(dims, lambda *_: zero)


def reset_masks(docs_ref, row, docs, length):
    at_i = lax.broadcasted_iota(jnp.int32, (length, length), 0)
    at_j = lax.broadcasted_iota(jnp.int32, (length, length), 1)
    token = lax.broadcasted_iota(jnp.int32, (length, 1), 0)
    visible = at_i >= at_j
    alive = token >= 0
    tail = token >= 0
    whole_alive = jnp.float32(1.0)
    for n in range(docs):
        start = docs_ref[row * docs + n]
        visible = visible & jnp.logical_not((at_j < start) & (start <= at_i))
        inside = (start >= 0) & (start < length)
        first = jnp.where(start >= 0, start, length)
        alive = alive & (token < first)
        last = jnp.where(start < length, start, -1)
        tail = tail & (token >= last)
        whole_alive = whole_alive * jnp.where(inside, 0.0, 1.0)
    return visible, alive.astype(F32), tail.astype(F32), whole_alive


def lower_ones(length, strict=False):
    at_i = lax.broadcasted_iota(jnp.int32, (length, length), 0)
    at_j = lax.broadcasted_iota(jnp.int32, (length, length), 1)
    return (at_i > at_j if strict else at_i >= at_j).astype(F32)


def project_body(
    rows, docs, length, hk, hv, parts,
    docs_ref, table_ref, x_ref, gain_ref, wq_ref, wk_ref, wv_ref, wog_ref, wrd_ref, wru_ref, bias_ref,
    normed_ref, q_ref, k_ref, v_ref, og_ref, ra_ref, gp_ref, cum_ref, keep_a_ref, send_a_ref, keep_b_ref,
    send_b_ref, decay_ref,
    hold,
):
    x = x_ref[...].astype(F32)
    inv = lax.rsqrt(jnp.mean(x * x, axis=-1, keepdims=True) + EPS)
    normed = (x * inv * gain_ref[...]).astype(BF)
    normed_ref[...] = normed
    rank = nt(normed, wrd_ref[...]).astype(BF)
    ra_ref[...] = rank
    gate = nn(rank, wru_ref[...]) + bias_ref[...]
    gp_ref[...] = gate
    q_ref[...] = nn(normed, wq_ref[...]).astype(BF)
    key = nn(normed, wk_ref[...]).astype(BF)
    k_ref[...] = key
    value = nn(normed, wv_ref[...]).astype(BF)
    v_ref[...] = value
    og_ref[...] = nn(normed, wog_ref[...])
    log_decay = (jnp.minimum(gate, 0.0) - jnp.log1p(jnp.exp(-jnp.abs(gate)))) * (1.0 / 16.0)
    tri = lower_ones(length)
    size = hv // parts
    for r in range(rows):
        at = slice(r * length, (r + 1) * length)
        row = pl.program_id(0) * rows + r
        cum = nn(tri, log_decay[at], HIGHEST)
        cum_ref[at, :] = cum
        _, _, tail, whole_alive = reset_masks(docs_ref, row, docs, length)
        last = cum[length - 1 :, :]
        decay_ref[r] = jnp.exp(last) * whole_alive
        weighted = (key[at].astype(F32) * jnp.exp(last - cum) * tail).astype(BF)
        for h in range(HEADS):
            hold[...] = tn(value[at, h * hv : (h + 1) * hv], weighted[:, h * hk : (h + 1) * hk])
            keep_ref, send_ref = (keep_a_ref, send_a_ref) if h < HEADS // 2 else (keep_b_ref, send_b_ref)
            for j in range(parts // 2):
                first = pl.multiple_of(table_ref[j] * size, size)
                keep_ref[j, r, h % (HEADS // 2)] = hold[pl.ds(first, size), :]
                second = pl.multiple_of(table_ref[parts // 2 + j] * size, size)
                send_ref[j, r, h % (HEADS // 2)] = hold[pl.ds(second, size), :]


def project_all(x, docs, table, gain, wq, wk, wv, wog, wrd, wru, bias, dims):
    row_count, length, width, kw, vw, ndocs, parts = dims
    tokens = row_count * length
    rows = 2 if row_count % 2 == 0 else 1
    tm = rows * length
    hk, hv = kw // HEADS, vw // HEADS
    rank = wrd.shape[0]
    size = hv // parts
    tile = lambda n: block((tm, n), lambda i, *_: (i, 0))
    half = (parts // 2, row_count, HEADS // 2, size, hk)
    half_block = block((parts // 2, rows, HEADS // 2, size, hk), lambda i, *_: (0, i, 0, 0, 0))
    body = functools.partial(project_body, rows, ndocs, length, hk, hv, parts)
    return call(
        body,
        (
            shape((tokens, width), BF),
            shape((tokens, kw), BF),
            shape((tokens, kw), BF),
            shape((tokens, vw), BF),
            shape((tokens, vw), F32),
            shape((tokens, rank), BF),
            shape((tokens, kw), F32),
            shape((tokens, kw), F32),
            shape(half, F32),
            shape(half, F32),
            shape(half, F32),
            shape(half, F32),
            shape((row_count, 1, kw), F32),
        ),
        (row_count // rows,),
        [
            tile(width), whole((1, width)), whole(wq.shape), whole(wk.shape), whole(wv.shape),
            whole(wog.shape), whole(wrd.shape), whole(wru.shape), whole((1, kw)),
        ],
        (
            tile(width), tile(kw), tile(kw), tile(vw), tile(vw), tile(rank), tile(kw), tile(kw),
            half_block, half_block, half_block, half_block,
            block((rows, 1, kw), lambda i, *_: (i, 0, 0)),
        ),
        prefetch=2,
        scratch=[pltpu.VMEM((hv, hk), F32)],
    )(docs, table, x, gain.reshape(1, -1), wq, wk, wv, wog, wrd, wru, bias.reshape(1, -1))


def span_factors(cum, length):
    middle = cum[length // 2 - 1 : length // 2, :]
    return jnp.exp(cum - middle), jnp.exp(middle - cum)


def inner_body(docs, length, hk, hv, docs_ref, q_ref, k_ref, v_ref, cum_ref, inner_ref):
    visible, _, _, _ = reset_masks(docs_ref, pl.program_id(0), docs, length)
    up, down = span_factors(cum_ref[...], length)
    q = (q_ref[...].astype(F32) * up).astype(BF)
    k = (k_ref[...].astype(F32) * down).astype(BF)
    for h in range(HEADS):
        kk = slice(h * hk, (h + 1) * hk)
        vv = slice(h * hv, (h + 1) * hv)
        scores = jnp.where(visible, nt(q[:, kk], k[:, kk]), 0.0).astype(BF)
        inner_ref[:, vv] = nn(scores, v_ref[:, vv])


def inner_all(q, k, v, cum, docs, dims):
    row_count, length, width, kw, vw, ndocs, parts = dims
    tokens = row_count * length
    tile = lambda n: block((length, n), lambda i, *_: (i, 0))
    return call(
        functools.partial(inner_body, ndocs, length, kw // HEADS, vw // HEADS),
        shape((tokens, vw), F32),
        (row_count,),
        [tile(kw), tile(kw), tile(vw), tile(kw)],
        tile(vw),
        prefetch=1,
    )(docs, q, k, v, cum)


def gather_state(near_ref, far_ref, table_ref, h, parts):
    half = parts // 2
    pieces = []
    for p in range(parts):
        place = table_ref[parts + p]
        near = near_ref[jnp.minimum(place, half - 1), 0, h]
        far = far_ref[jnp.maximum(place - half, 0), 0, h]
        pieces.append(jnp.where(place < half, near, far))
    return jnp.concatenate(pieces, axis=0)


def mix_body(
    docs, length, hk, hv, parts,
    docs_ref, table_ref, q_ref, cum_ref, inner_ref, og_ref, near_a_ref, far_a_ref, near_b_ref, far_b_ref,
    gain_ref,
    mixed_ref, gated_ref, kept_ref,
):
    _, alive, _, _ = reset_masks(docs_ref, pl.program_id(0), docs, length)
    reach = (q_ref[...].astype(F32) * jnp.exp(cum_ref[...]) * alive).astype(BF)
    scale = hk ** (-0.5)
    for h in range(HEADS):
        kk = slice(h * hk, (h + 1) * hk)
        vv = slice(h * hv, (h + 1) * hv)
        near_ref, far_ref = (near_a_ref, far_a_ref) if h < HEADS // 2 else (near_b_ref, far_b_ref)
        state = gather_state(near_ref, far_ref, table_ref, h % (HEADS // 2), parts).astype(BF)
        kept_ref[0, h] = state
        mixed = scale * (inner_ref[:, vv] + nt(reach[:, kk], state))
        mixed_ref[:, vv] = mixed
        inv = lax.rsqrt(jnp.mean(mixed * mixed, axis=-1, keepdims=True) + EPS)
        og = og_ref[:, vv]
        gated_ref[:, vv] = (mixed * inv * gain_ref[...] * og * jax.nn.sigmoid(og)).astype(BF)


def mix_all(q, cum, inner, og, states, gain, docs, table, dims):
    row_count, length, width, kw, vw, ndocs, parts = dims
    tokens = row_count * length
    hk, hv = kw // HEADS, vw // HEADS
    tile = lambda n: block((length, n), lambda i, *_: (i, 0))
    half = block((parts // 2, 1, HEADS // 2, hv // parts, hk), lambda i, *_: (0, i, 0, 0, 0))
    return call(
        functools.partial(mix_body, ndocs, length, hk, hv, parts),
        (
            shape((tokens, vw), F32),
            shape((tokens, vw), BF),
            shape((row_count, HEADS, hv, hk), BF),
        ),
        (row_count,),
        [
            tile(kw), tile(kw), tile(vw), tile(vw), half, half, half, half, whole((1, hv)),
        ],
        (tile(vw), tile(vw), block((1, HEADS, hv, hk), lambda i, *_: (i, 0, 0, 0))),
        prefetch=2,
    )(docs, table, q, cum, inner, og, *states, gain.reshape(1, -1))


def hidden_back_body(cot_ref, wd_ref, dh_ref):
    dh_ref[...] = nt(cot_ref[...], wd_ref[...])


def hidden_back_all(cot, wd):
    tokens, width = cot.shape
    ff, tile = wd.shape[0], 256
    return call(
        hidden_back_body,
        shape((tokens, ff), F32),
        (ff // tile,),
        [whole((tokens, width)), block((tile, width), lambda i: (i, 0))],
        block((tokens, tile), lambda i: (0, i)),
    )(cot, wd)


def ff_body(
    x_ref, gated_ref, wo_ref, gain_ref, wg_ref, wu_ref, dh_ref,
    hidden_ref, dg_ref, du_ref, normed2_ref, middle_ref,
):
    @pl.when(pl.program_id(0) == 0)
    def _():
        mid = x_ref[...].astype(F32) + nn(gated_ref[...], wo_ref[...])
        middle_ref[...] = mid
        inv = lax.rsqrt(jnp.mean(mid * mid, axis=-1, keepdims=True) + EPS)
        normed2_ref[...] = (mid * inv * gain_ref[...]).astype(BF)

    normed2 = normed2_ref[...]
    gate = nn(normed2, wg_ref[...])
    up = nn(normed2, wu_ref[...])
    d_hidden = dh_ref[...]
    sig = jax.nn.sigmoid(gate)
    act = gate * sig
    hidden_ref[...] = (act * up).astype(BF)
    dg_ref[...] = (d_hidden * up * sig * (1.0 + gate * (1.0 - sig))).astype(BF)
    du_ref[...] = (d_hidden * act).astype(BF)


def ff_all(x, gated, wo, gain, wg, wu, dh):
    tokens, width = x.shape
    ff = wg.shape[1]
    tile = 256
    col = lambda n: block((n, tile), lambda i: (0, i))
    once = lambda dims: pl.BlockSpec(dims, lambda i: (0, 0), pipeline_mode=pl.Buffered(1))
    return call(
        ff_body,
        (
            shape((tokens, ff), BF), shape((tokens, ff), BF), shape((tokens, ff), BF),
            shape((tokens, width), BF), shape((tokens, width), F32),
        ),
        (ff // tile,),
        [
            once((tokens, width)), once(gated.shape), once(wo.shape), once((1, width)),
            col(width), col(width), col(tokens),
        ],
        (
            col(tokens), col(tokens), col(tokens), whole((tokens, width)), whole((tokens, width)),
        ),
    )(x, gated, wo, gain.reshape(1, -1), wg, wu, dh)


def ff_back_body(
    steps,
    hidden_ref, dg_ref, du_ref, wd_ref, wg_ref, wu_ref, middle_ref, cot_ref, wo_ref, gain_ref,
    out_ref, dmid_ref, dout_ref, dgated_ref, gnorm_ref,
):
    total, back = dgated_ref, dmid_ref
    step = pl.program_id(0)
    tokens = middle_ref.shape[0]
    rows = 256 if tokens % 256 == 0 else tokens
    for first in range(0, tokens, rows):
        at = slice(first, first + rows)
        more = nn(hidden_ref[at, :], wd_ref[...])
        more_back = nt(dg_ref[at, :], wg_ref[...]) + nt(du_ref[at, :], wu_ref[...])

        @pl.when(step == 0)
        def _(at=at, more=more, more_back=more_back):
            total[at, :] = more
            back[at, :] = more_back

        @pl.when(step > 0)
        def _(at=at, more=more, more_back=more_back):
            total[at, :] += more
            back[at, :] += more_back

    @pl.when(step == steps - 1)
    def _():
        gnorm = jnp.zeros((1, middle_ref.shape[1]), F32)
        for first in range(0, tokens, rows):
            at = slice(first, first + rows)
            mid = middle_ref[at, :]
            out_ref[at, :] = (mid + total[at, :]).astype(BF)
            inv = lax.rsqrt(jnp.mean(mid * mid, axis=-1, keepdims=True) + EPS)
            d_normed2 = back[at, :]
            gnorm = gnorm + jnp.sum(d_normed2 * mid * inv, axis=0, keepdims=True)
            scaled = d_normed2 * gain_ref[...]
            d_middle = (
                cot_ref[at, :].astype(F32)
                + inv * scaled
                - mid * (inv * inv * inv) * jnp.mean(scaled * mid, axis=-1, keepdims=True)
            )
            dmid_ref[at, :] = d_middle
            d_out = d_middle.astype(BF)
            dout_ref[at, :] = d_out
            dgated_ref[at, :] = nt(d_out, wo_ref[...])
        gnorm_ref[...] = gnorm


def ff_back_all(hidden, dg, du, wd, wg, wu, middle, cot, wo, gain):
    tokens, width = middle.shape
    vw, ff = wo.shape[0], wg.shape[1]
    tile = 1408 if ff % 1408 == 0 else 256
    steps = ff // tile
    col = lambda n: block((n, tile), lambda i: (0, i))
    once = lambda dims: pl.BlockSpec(dims, lambda i: (0, 0), pipeline_mode=pl.Buffered(1))
    return call(
        functools.partial(ff_back_body, steps),
        (
            shape((tokens, width), BF), shape((tokens, width), F32), shape((tokens, width), BF),
            shape((tokens, vw), F32), shape((1, width), F32),
        ),
        (steps,),
        [
            col(tokens), col(tokens), col(tokens), block((tile, width), lambda i: (i, 0)),
            col(width), col(width), once((tokens, width)), once((tokens, width)), once(wo.shape),
            once((1, width)),
        ],
        (
            whole((tokens, width)), whole((tokens, width)), whole((tokens, width)),
            whole((tokens, vw)), whole((1, width)),
        ),
    )(hidden, dg, du, wd, wg, wu, middle, cot, wo, gain.reshape(1, -1))


def head_back_body(
    docs, length, hk, hv, parts,
    docs_ref, table_ref, dgated_ref, og_ref, mixed_ref, q_ref, cum_ref, gain_ref,
    dmix_ref, dog_ref, keep_ref, send_ref, ggroup_ref,
    hold,
):
    row = pl.program_id(0)
    _, alive, _, _ = reset_masks(docs_ref, row, docs, length)
    reach = (q_ref[...].astype(F32) * jnp.exp(cum_ref[...]) * alive).astype(BF)
    scale = hk ** (-0.5)
    size = hv // parts
    ggroup = jnp.zeros((1, hv), F32)
    for h in range(HEADS):
        kk = slice(h * hk, (h + 1) * hk)
        vv = slice(h * hv, (h + 1) * hv)
        mixed = mixed_ref[:, vv]
        inv = lax.rsqrt(jnp.mean(mixed * mixed, axis=-1, keepdims=True) + EPS)
        og = og_ref[:, vv]
        sig = jax.nn.sigmoid(og)
        dgated = dgated_ref[:, vv]
        unit = mixed * inv
        dog_ref[:, vv] = (
            dgated * unit * gain_ref[...] * sig * (1.0 + og * (1.0 - sig))
        ).astype(BF)
        d_heads = dgated * og * sig
        ggroup = ggroup + jnp.sum(d_heads * unit, axis=0, keepdims=True)
        scaled = d_heads * gain_ref[...]
        d_mixed = inv * scaled - mixed * (inv * inv * inv) * jnp.mean(
            scaled * mixed, axis=-1, keepdims=True
        )
        d_mixed = (scale * d_mixed).astype(BF)
        dmix_ref[:, vv] = d_mixed
        hold[...] = tn(d_mixed, reach[:, kk])
        for j in range(parts // 2):
            first = pl.multiple_of(table_ref[j] * size, size)
            keep_ref[j, 0, h] = hold[pl.ds(first, size), :]
            second = pl.multiple_of(table_ref[parts // 2 + j] * size, size)
            send_ref[j, 0, h] = hold[pl.ds(second, size), :]

    @pl.when(row == 0)
    def _():
        ggroup_ref[...] = ggroup

    @pl.when(row > 0)
    def _():
        ggroup_ref[...] += ggroup


def head_back_all(dgated, og, mixed, q, cum, gain, docs, table, dims):
    row_count, length, width, kw, vw, ndocs, parts = dims
    tokens = row_count * length
    hk, hv = kw // HEADS, vw // HEADS
    size = hv // parts
    tile = lambda n: block((length, n), lambda i, *_: (i, 0))
    half = (parts // 2, row_count, HEADS, size, hk)
    half_block = block((parts // 2, 1, HEADS, size, hk), lambda i, *_: (0, i, 0, 0, 0))
    return call(
        functools.partial(head_back_body, ndocs, length, hk, hv, parts),
        (
            shape((tokens, vw), BF), shape((tokens, vw), BF),
            shape(half, F32), shape(half, F32), shape((1, hv), F32),
        ),
        (row_count,),
        [tile(vw), tile(vw), tile(vw), tile(kw), tile(kw), whole((1, hv))],
        (tile(vw), tile(vw), half_block, half_block, whole((1, hv))),
        prefetch=2,
        scratch=[pltpu.VMEM((hv, hk), F32)],
    )(docs, table, dgated, og, mixed, q, cum, gain.reshape(1, -1))


def mix_back_body(
    docs, length, hk, hv, parts,
    docs_ref, table_ref, q_ref, k_ref, v_ref, cum_ref, gp_ref, ra_ref, dmix_ref, state_ref, near_ref,
    far_ref, wru_ref,
    dqkv_ref, drank_ref, grup_ref, gbias_ref,
):
    row = pl.program_id(0)
    kw = HEADS * hk
    visible, alive, tail, whole_alive = reset_masks(docs_ref, row, docs, length)
    cum = cum_ref[...]
    last = cum[length - 1 :, :]
    up, down = span_factors(cum, length)
    from_start = jnp.exp(cum) * alive
    to_end = jnp.exp(last - cum) * tail
    total = jnp.exp(last) * whole_alive
    q = q_ref[...].astype(F32)
    k = k_ref[...].astype(F32)
    q_span = (q * up).astype(BF)
    k_span = (k * down).astype(BF)
    reach = (q * from_start).astype(BF)
    weighted = (k * to_end).astype(BF)
    later, earlier, crossing = [], [], []
    for h in range(HEADS):
        kk = slice(h * hk, (h + 1) * hk)
        vv = slice(h * hv, (h + 1) * hv)
        qs, ks = q_span[:, kk], k_span[:, kk]
        d_mix = dmix_ref[:, vv]
        value = v_ref[:, vv]
        state = state_ref[0, h]
        grad32 = gather_state(near_ref, far_ref, table_ref, h, parts)
        grad = grad32.astype(BF)
        scores = jnp.where(visible, nt(qs, ks), 0.0).astype(BF)
        d_scores = jnp.where(visible, nt(d_mix, value), 0.0).astype(BF)
        dq_in = nn(d_scores, ks)
        dk_in = tn(d_scores, qs)
        dq_out = nn(d_mix, state)
        dk_out = nn(value, grad)
        dqkv_ref[:, kk] = (dq_in * up[:, kk] + dq_out * from_start[:, kk]).astype(BF)
        dqkv_ref[:, kw + h * hk : kw + (h + 1) * hk] = (
            dk_in * down[:, kk] + dk_out * to_end[:, kk]
        ).astype(BF)
        dqkv_ref[:, 2 * kw + h * hv : 2 * kw + (h + 1) * hv] = (
            tn(scores, d_mix) + nt(weighted[:, kk], grad)
        ).astype(BF)
        later.append(
            qs.astype(F32) * dq_in - ks.astype(F32) * dk_in + reach[:, kk].astype(F32) * dq_out
        )
        earlier.append(weighted[:, kk].astype(F32) * dk_out)
        crossing.append(jnp.sum(state.astype(F32) * grad32, axis=0, keepdims=True))
    later = jnp.concatenate(later, axis=1)
    earlier = jnp.concatenate(earlier, axis=1)
    crossing = jnp.concatenate(crossing, axis=1)
    at_i = lax.broadcasted_iota(jnp.int32, (length, length), 0)
    at_j = lax.broadcasted_iota(jnp.int32, (length, length), 1)
    after = (at_i <= at_j).astype(F32)
    before = (at_i > at_j).astype(F32)
    d_decay = nn(after, later, HIGHEST) + nn(before, earlier, HIGHEST) + total * crossing
    d_gate = (d_decay * jax.nn.sigmoid(-gp_ref[...]) * (1.0 / 16.0)).astype(BF)
    drank_ref[...] = nt(d_gate, wru_ref[...]).astype(BF)
    grup = tn(ra_ref[...], d_gate)
    gbias = jnp.sum(d_gate.astype(F32), axis=0, keepdims=True)

    @pl.when(row == 0)
    def _():
        grup_ref[...] = grup
        gbias_ref[...] = gbias

    @pl.when(row > 0)
    def _():
        grup_ref[...] += grup
        gbias_ref[...] += gbias


def mix_back_all(q, k, v, cum, gp, ra, dmix, state, near, far, wru, docs, table, dims):
    row_count, length, width, kw, vw, ndocs, parts = dims
    tokens = row_count * length
    hk, hv = kw // HEADS, vw // HEADS
    rank = wru.shape[0]
    tile = lambda n: block((length, n), lambda i, *_: (i, 0))
    half = block((parts // 2, 1, HEADS, hv // parts, hk), lambda i, *_: (0, i, 0, 0, 0))
    return call(
        functools.partial(mix_back_body, ndocs, length, hk, hv, parts),
        (
            shape((tokens, 2 * kw + vw), BF), shape((tokens, rank), BF),
            shape((rank, kw), F32), shape((1, kw), F32),
        ),
        (row_count,),
        [
            tile(kw), tile(kw), tile(vw), tile(kw), tile(kw), tile(rank), tile(vw),
            block((1, HEADS, hv, hk), lambda i, *_: (i, 0, 0, 0)),
            half, half, whole((rank, kw)),
        ],
        (tile(2 * kw + vw), tile(rank), whole((rank, kw)), whole((1, kw))),
        prefetch=2,
    )(docs, table, q, k, v, cum, gp, ra, dmix, state, near, far, wru)


def input_back_body(
    kw, vw,
    x_ref, dmid_ref, dqkv_ref, dog_ref, drank_ref, gain_ref, wq_ref, wk_ref, wv_ref, wog_ref, wrd_ref,
    gin_ref, gnorm_ref,
):
    step = pl.program_id(0)
    d_normed = (
        nt(dqkv_ref[:, :kw], wq_ref[...])
        + nt(dqkv_ref[:, kw : 2 * kw], wk_ref[...])
        + nt(dqkv_ref[:, 2 * kw :], wv_ref[...])
        + nt(dog_ref[...], wog_ref[...])
        + nn(drank_ref[...], wrd_ref[...])
    )
    x = x_ref[...].astype(F32)
    inv = lax.rsqrt(jnp.mean(x * x, axis=-1, keepdims=True) + EPS)
    gnorm = jnp.sum(d_normed * x * inv, axis=0, keepdims=True)
    scaled = d_normed * gain_ref[...]
    gin_ref[...] = (
        dmid_ref[...]
        + inv * scaled
        - x * (inv * inv * inv) * jnp.mean(scaled * x, axis=-1, keepdims=True)
    )

    @pl.when(step == 0)
    def _():
        gnorm_ref[...] = gnorm

    @pl.when(step > 0)
    def _():
        gnorm_ref[...] += gnorm


def input_back_all(x, dmid, dqkv, dog, drank, gain, wq, wk, wv, wog, wrd):
    tokens, width = x.shape
    kw, vw = wq.shape[1], wv.shape[1]
    tm = 256 if tokens % 256 == 0 else 128
    tile = lambda n: block((tm, n), lambda i: (i, 0))
    return call(
        functools.partial(input_back_body, kw, vw),
        (shape((tokens, width), F32), shape((1, width), F32)),
        (tokens // tm,),
        [
            tile(width), tile(width), tile(2 * kw + vw), tile(vw), tile(drank.shape[1]),
            whole((1, width)), whole(wq.shape), whole(wk.shape), whole(wv.shape), whole(wog.shape),
            whole(wrd.shape),
        ],
        (tile(width), whole((1, width))),
    )(x, dmid, dqkv, dog, drank, gain.reshape(1, -1), wq, wk, wv, wog, wrd)


def weight_body(count, pieces, per, table_ref, *refs):
    lefts, rights = refs[:count], refs[count : 2 * count]
    keep_ref, send_ref, hold = refs[2 * count : 2 * count + 3]
    turned = refs[2 * count + 3 :]

    @pl.when(pl.program_id(0) == 0)
    def _():
        for n in range(count):
            turned[n][...] = lefts[n][...].T

    for n in range(count):
        hold[...] = nn(turned[n][...], rights[n][...])
        at = slice(n * per, (n + 1) * per)
        for j in range(pieces // 2):
            first = pl.multiple_of(table_ref[j] * per, per)
            keep_ref[j, at, :] = hold[pl.ds(first, per), :]
            second = pl.multiple_of(table_ref[pieces // 2 + j] * per, per)
            send_ref[j, at, :] = hold[pl.ds(second, per), :]


def weight_grads(pairs, table, columns=None):
    count, pieces = len(pairs), table.shape[0]
    tokens, rows = pairs[0][0].shape
    per = rows // pieces
    start, cols = columns or (0, pairs[0][1].shape[1])
    if per % 8:
        both = [tn(left, right[:, start : start + cols]) for left, right in pairs]
        parts = jnp.concatenate([part.reshape(pieces, per, cols) for part in both], axis=1)[table]
        return parts[: pieces // 2], parts[pieces // 2 :]
    tile = next(n for n in (1408, 512, 256, 128) if cols % n == 0 and start % n == 0)
    skip = start // tile
    half = shape((pieces // 2, count * per, cols), F32)
    half_block = block((pieces // 2, count * per, tile), lambda i, *_: (0, 0, i))
    return call(
        functools.partial(weight_body, count, pieces, per),
        (half, half),
        (cols // tile,),
        [whole((tokens, rows))] * count
        + [block((tokens, tile), lambda i, *_: (0, i + skip))] * count,
        (half_block, half_block),
        prefetch=1,
        scratch=[pltpu.VMEM((rows, tile), F32)] + [pltpu.VMEM((rows, tokens), BF)] * count,
    )(table, *[left for left, _ in pairs], *[right for _, right in pairs])


def small_body(
    pieces,
    table_ref, normed_ref, drank_ref, gnorm1_ref, gnorm2_ref, grup_ref, gbias_ref, ggroup_ref,
    keep_ref, send_ref,
    hold,
):
    width, kw, hv = gnorm1_ref.shape[1], gbias_ref.shape[1], ggroup_ref.shape[1]
    rank = grup_ref.shape[0]

    def stand(rows):
        have = sum(row.shape[0] for row in rows)
        return jnp.concatenate(rows + [jnp.zeros((128 - have, rows[0].shape[1]), F32)], axis=0).T

    spread = jnp.zeros((normed_ref.shape[0], 128 - rank), BF)
    hold[:width, :] = tn(normed_ref[...], jnp.concatenate([drank_ref[...], spread], axis=1)) + stand(
        [jnp.zeros((rank, width), F32), gnorm1_ref[...], gnorm2_ref[...]]
    )
    hold[width : width + kw, :] = stand([grup_ref[...], gbias_ref[...]])
    hold[width + kw :, :] = stand([ggroup_ref[...]])
    first, place = 0, 0
    for rows in (width, kw, hv):
        per = rows // pieces
        for j in range(pieces // 2):
            keep = pl.multiple_of(first + table_ref[j] * per, per)
            keep_ref[j, place : place + per, :] = hold[pl.ds(keep, per), :]
            send = pl.multiple_of(first + table_ref[pieces // 2 + j] * per, per)
            send_ref[j, place : place + per, :] = hold[pl.ds(send, per), :]
        first, place = first + rows, place + per


def small_grads(normed, drank, gnorm1, gnorm2, grup, gbias, ggroup, table):
    pieces, rank = table.shape[0], grup.shape[0]
    width, kw, hv = gnorm1.shape[1], gbias.shape[1], ggroup.shape[1]
    rows = (width + kw + hv) // pieces
    if hv // pieces % 8:
        wide = lambda value: jnp.pad(value, ((0, 0), (0, 128 - value.shape[1])))
        cut = lambda value: wide(value).reshape(pieces, -1, 128)
        both = jnp.concatenate(
            [
                cut(jnp.concatenate([tn(normed, drank), gnorm1.T, gnorm2.T], axis=1)),
                cut(jnp.concatenate([grup.T, gbias.T], axis=1)),
                cut(ggroup.T),
            ],
            axis=1,
        )[table]
        return both[: pieces // 2], both[pieces // 2 :]
    half = shape((pieces // 2, rows, 128), F32)
    operands = (normed, drank, gnorm1, gnorm2, grup, gbias, ggroup)
    return call(
        functools.partial(small_body, pieces),
        (half, half),
        (1,),
        [whole(value.shape) for value in operands],
        (whole(half.shape), whole(half.shape)),
        prefetch=1,
        scratch=[pltpu.VMEM((width + kw + hv, 128), F32)],
    )(table, *operands)


def bits_of(n):
    return n.bit_length() - 1


class Links:
    def __init__(self):
        self.n_dp, self.n_seq = lax.axis_size("dp"), lax.axis_size("seq")
        self.seq_bits, self.dp_bits = bits_of(self.n_seq), bits_of(self.n_dp)
        self.at_seq = lax.axis_index("seq")
        self.me = lax.axis_index("dp") * self.n_seq + self.at_seq

    def swap(self, value, bit):
        name, n, flip = "seq", self.n_seq, 1 << bit
        if bit >= self.seq_bits:
            name, n, flip = "dp", self.n_dp, 1 << (bit - self.seq_bits)
        return lax.ppermute(value, name, [(i, i ^ flip) for i in range(n)])

    def table(self, order):
        n = 1 << len(order)
        places = [
            sum(((at >> (len(order) - 1 - k)) & 1) << bit for k, bit in enumerate(order))
            for at in range(n)
        ]
        here = self.me if n == self.n_dp * self.n_seq else self.at_seq
        return jnp.array(places, jnp.int32) ^ here

    def order(self, *names):
        across = tuple(range(self.seq_bits, self.seq_bits + self.dp_bits))
        bits = [0]
        for name in names:
            bits.extend(across if name == "x" else [{"y": 1, "z0": 2, "z1": 3}[name]])
        return tuple(bits) + tuple(b for b in range(self.seq_bits) if b not in bits)


class Turns:
    def __init__(self):
        self.last = ()

    def after(self, value):
        return lax.optimization_barrier((value,) + self.last)[0]

    def done(self, *values):
        self.last = values


class Task:
    def __init__(self, steps):
        self.steps, self.wanted, self.got, self.begun, self.over = steps, [], None, False, False

    def advance(self, turns):
        if self.over:
            return
        if self.wanted:
            start([self], turns)
        try:
            self.wanted = self.steps.send(self.got) if self.begun else next(self.steps)
            self.begun = True
        except StopIteration:
            self.wanted, self.over = [], True

    def finish(self, turns):
        while not self.over:
            self.advance(turns)


def start(tasks, turns):
    tasks = [task for task in tasks if task.wanted]
    values = [value for task in tasks for value, _ in task.wanted]
    if not values:
        return
    tied = lax.optimization_barrier(tuple(values) + turns.last)[: len(values)]
    turns.done(tied[0])
    tied = iter(tied)
    for task in tasks:
        task.got = [move(next(tied)) for _, move in task.wanted]
        task.wanted = []


def reduce_steps(links, turns, make, order, out, name):
    keep, send = make()
    turns.done(keep, send)
    for k, bit in enumerate(order):
        (got,) = yield [(send, functools.partial(links.swap, bit=bit))]
        keep = turns.after(keep)
        if k == len(order) - 1:
            out[name] = keep + got
            turns.done(out[name])
            return
        half = keep.shape[0] // 2
        send = keep[half:] + got[half:]
        keep = keep[:half] + got[:half]
        turns.done(keep, send)


def scan_steps(links, turns, make, decays, backwards, out):
    keep, send, decay = make()
    bits = links.seq_bits
    levels = []
    kept = [] if decays is None else decays
    turns.done(keep, send)
    for bit in range(bits - 1):
        swap = functools.partial(links.swap, bit=bit)
        if decays is None:
            got, got_d = yield [(send, swap), (decay, swap)]
            kept.append((decay, got_d))
            decay = decay * got_d
        else:
            (got,) = yield [(send, swap)]
        mine_d, got_d = kept[bit]
        keep = turns.after(keep)
        odd = (links.at_seq >> bit) & 1
        second = (odd == 0) if backwards else (odd == 1)
        levels.append((second, keep, got, mine_d, got_d))
        total = jnp.where(second, mine_d * got + keep, got_d * keep + got)
        half = total.shape[0] // 2
        if bit < bits - 2:
            keep, send = total[:half], total[half:]
            turns.done(keep, send)
        else:
            send = total
            turns.done(send)
    flip = 1 << (bits - 1)
    pairs = [(i, i ^ flip) for i in range(links.n_seq) if ((i >> (bits - 1)) & 1) == int(backwards)]
    (state,) = yield [(send, lambda value: lax.ppermute(value, "seq", pairs))]
    for bit in reversed(range(bits - 1)):
        second, keep, got, mine_d, got_d = levels[bit]
        keep = turns.after(keep)
        theirs = jnp.where(second, state, mine_d * state + keep)
        mine = jnp.where(second, got_d * state + got, state)
        turns.done(theirs, mine)
        (far,) = yield [(theirs, functools.partial(links.swap, bit=bit))]
        if bit == 0:
            out["near"], out["far"], out["decays"] = mine, far, kept
        else:
            mine = turns.after(mine)
            state = jnp.concatenate([mine, far], axis=0)


ROUTES = {
    "gate": ("x", "y", "z0", "z1"),
    "up": ("y", "x", "z0", "z1"),
    "down": ("z0", "y", "x", "z1"),
    "mid": ("x", "y", "z0", "z1"),
    "qk": ("x", "y", "z0", "z1"),
    "v": ("y", "x", "z0", "z1"),
    "small": ("x", "y", "z0", "z1"),
}
SCHEDULE = (
    "gate", ("gate",), "up", ("up",), "down", ("down",), "gate", ("gate",), "up", ("up",),
    "down", ("down",), "ff", "scan", ("scan",), "gate", "up", "down", "scan", ("scan", "up"),
    "mid", "scan", ("scan", "gate", "mid"), "mid", "scan", ("scan", "mid", "down"), "up",
    "gate", "scan", ("scan",), "scan", ("scan",), "down", "mid", "scan", ("scan", "gate", "up",
    "down", "mid"), "scan", "qk", "v", "gate", "up", "down", "mid", ("qk", "v", "gate", "up",
    "mid"), "qk", "v", ("qk", "v"), "small", "small", "qk", "v", ("qk", "v"), "gate", "up",
    ("small", "down"), "mid", "qk", "v", "small", ("qk", "v", "small"), "small", ("mid",),
    "down", "qk", "v", ("small", "qk", "v"), "small", ("small",), "small", ("small",), "mid",
    "qk", "v", "small",
)


def local(
    block_in, doc_starts, cotangent, norm1_gain, w_query, w_key, w_value, w_outgate, w_rank_down,
    w_rank_up, decay_bias, group_gain, w_output, norm2_gain, w_ffgate, w_ffup, w_ffdown,
):
    row_count, length, width = block_in.shape
    tokens = row_count * length
    kw, vw = w_query.shape[1], w_value.shape[1]
    links, turns = Links(), Turns()
    parts = links.n_seq
    everyone = links.n_dp * links.n_seq
    dims = (row_count, length, width, kw, vw, doc_starts.shape[1], parts)
    x = block_in.reshape(tokens, width)
    cot = cotangent.reshape(tokens, width)
    docs = (doc_starts - links.at_seq * length).reshape(-1)
    rank_down_t = w_rank_down.T

    levels = range(links.seq_bits - 1)
    step = 1 << len(levels)
    size = parts // step
    low = links.at_seq & (step - 1)
    reverse = jnp.array(
        [sum(((p >> b) & 1) << (len(levels) - 1 - b) for b in levels) for p in range(step)], jnp.int32
    )
    spread = jnp.arange(size)
    to_piece = ((reverse ^ low)[:, None] * size + spread).reshape(-1)
    to_place = (reverse[jnp.arange(step) ^ low][:, None] * size + spread).reshape(-1)
    state_table = jnp.concatenate([to_piece, to_place]).astype(jnp.int32)

    normed, q, k, v, og, ra, gp, cum, keep_a, send_a, keep_b, send_b, decay = project_all(
        x, docs, state_table, norm1_gain, w_query, w_key, w_value, w_outgate, rank_down_t, w_rank_up,
        decay_bias, dims,
    )
    decay = decay.reshape(1, row_count, HEADS, 1, kw // HEADS)
    fwd_a, fwd_b = {}, {}
    one = Task(scan_steps(
        links, turns, lambda: (keep_a, send_a, decay[:, :, : HEADS // 2]), None, False, fwd_a
    ))
    two = Task(scan_steps(
        links, turns, lambda: (keep_b, send_b, decay[:, :, HEADS // 2 :]), None, False, fwd_b
    ))
    one.advance(turns)
    start([one], turns)
    two.advance(turns)
    start([two], turns)
    one.advance(turns)
    start([one], turns)
    two.advance(turns)
    start([two], turns)
    dh = hidden_back_all(turns.after(cot), w_ffdown)
    turns.done(dh)
    one.advance(turns)
    start([one], turns)
    two.advance(turns)
    start([two], turns)
    inner = inner_all(q, k, v, cum, turns.after(docs), dims)
    turns.done(inner)
    while not two.over:
        one.advance(turns)
        start([one], turns)
        two.advance(turns)
        start([two], turns)
    decays = [
        tuple(jnp.concatenate(pair, axis=2) for pair in zip(*both))
        for both in zip(fwd_a["decays"], fwd_b["decays"])
    ]
    states = (fwd_a["near"], fwd_a["far"], fwd_b["near"], fwd_b["far"])
    mixed, gated, state_kept = mix_all(
        q, cum, inner, og, states, group_gain, turns.after(docs), state_table, dims
    )
    hidden, dg, du, normed2, middle = ff_all(
        x, gated, w_output, norm2_gain, w_ffgate, w_ffup, dh
    )
    turns.done(normed2)

    routes = {name: links.order(*route) for name, route in ROUTES.items()}
    tables = {route: links.table(route) for route in set(routes.values())}
    back, grads, held = {}, {}, {}
    ff = w_ffgate.shape[1]

    def ff_steps():
        out, d_middle, d_out, d_gated, gnorm2 = ff_back_all(
            hidden, dg, du, w_ffdown, w_ffgate, w_ffup, middle, turns.after(cot), w_output, norm2_gain
        )
        held.update(out=out, d_middle=d_middle, d_out=d_out, d_gated=d_gated, gnorm2=gnorm2)
        turns.done(d_out)
        return
        yield

    def head_back():
        d_mix, d_og, keep, send, ggroup = head_back_all(
            held["d_gated"], og, mixed, q, cum, group_gain, turns.after(docs), state_table, dims
        )
        held.update(d_mix=d_mix, d_og=d_og, ggroup=ggroup)
        return keep, send, None

    def all_back():
        yield from scan_steps(links, turns, head_back, decays, True, back)
        held["d_qkv"], held["d_rank"], held["grup"], held["gbias"] = mix_back_all(
            q, k, v, cum, gp, ra, held["d_mix"], state_kept, back["near"], back["far"], w_rank_up,
            turns.after(docs), state_table, dims,
        )
        turns.done(held["d_rank"])

    def weights(name, pairs, columns=None):
        order = routes[name]
        make = lambda: weight_grads(pairs(), turns.after(tables[order]), columns)
        return reduce_steps(links, turns, make, order, grads, name)

    def small_steps():
        grad_in, gnorm1 = input_back_all(
            x, held["d_middle"], held["d_qkv"], held["d_og"], held["d_rank"], turns.after(norm1_gain),
            w_query, w_key, w_value, w_outgate, rank_down_t,
        )
        held["grad_in"] = grad_in
        turns.done(gnorm1)
        yield []
        make = lambda: small_grads(
            normed, held["d_rank"], gnorm1, held["gnorm2"], held["grup"], held["gbias"],
            held["ggroup"], turns.after(tables[routes["small"]]),
        )
        yield from reduce_steps(links, turns, make, routes["small"], grads, "small")

    rank = w_rank_up.shape[0]
    work = {
        "ff": ff_steps(),
        "scan": all_back(),
        "gate": weights("gate", lambda: [(normed2, dg)]),
        "up": weights("up", lambda: [(normed2, du)]),
        "down": weights("down", lambda: [(hidden, cot)]),
        "mid": weights("mid", lambda: [(gated, held["d_out"]), (normed, held["d_og"])]),
        "qk": weights("qk", lambda: [(normed, held["d_qkv"])], (0, 2 * kw)),
        "v": weights("v", lambda: [(normed, held["d_qkv"])], (2 * kw, vw)),
        "small": small_steps(),
    }
    work = {name: Task(steps) for name, steps in work.items()}
    for name in SCHEDULE + tuple(work) * (2 * len(routes["gate"])):
        if isinstance(name, tuple):
            start([work[each] for each in name], turns)
            continue
        if name in ("scan", "mid"):
            work["ff"].finish(turns)
        if name in ("qk", "v", "small"):
            work["scan"].finish(turns)
        work[name].advance(turns)

    per, per_k = width // everyone, kw // everyone
    small = grads["small"][0]
    first, second, third = small[:per], small[per : per + per_k], small[per + per_k :]
    mid, qk = grads["mid"][0], grads["qk"][0]
    return (
        held["out"].reshape(row_count, length, width),
        held["grad_in"].reshape(row_count, length, width),
        first[:, rank],
        qk[:, :kw],
        qk[:, kw:],
        grads["v"][0],
        mid[per:],
        first[:, :rank],
        second[:, :rank].T,
        second[:, rank],
        third[:, 0],
        mid[:per],
        first[:, rank + 1],
        grads["gate"][0],
        grads["up"][0],
        grads["down"][0],
    )


def solution(mesh):
    tokens = P("dp", "seq", None)
    rows = P(("dp", "seq"), None)
    vector = P(("dp", "seq"))
    return jax.shard_map(
        local,
        mesh=mesh,
        in_specs=(tokens, P("dp", None), tokens) + (P(),) * 14,
        out_specs=(
            tokens, tokens, vector, rows, rows, rows, rows, rows, P(None, ("dp", "seq")), vector,
            vector, rows, vector, rows, rows, rows,
        ),
        check_vma=False,
    )
```

```python
import functools

import jax
import jax.numpy as jnp
from jax import lax
from jax.experimental import pallas as pl
from jax.experimental.pallas import tpu as pltpu
from jax.sharding import PartitionSpec as P

HEADS = 4
EPS = 1e-06
MIB = 1 << 20
BF = jnp.bfloat16
F32 = jnp.float32
HIGHEST = lax.Precision.HIGHEST


def nn(a, b, precision=None):
    return lax.dot_general(
        a, b, (((1,), (0,)), ((), ())), precision=precision, preferred_element_type=F32
    )


def nt(a, b):
    return lax.dot_general(a, b, (((1,), (1,)), ((), ())), preferred_element_type=F32)


def tn(a, b):
    return lax.dot_general(a, b, (((0,), (0,)), ((), ())), preferred_element_type=F32)


def shape(dims, dtype):
    return jax.ShapeDtypeStruct(dims, dtype)


def call(body, out_shape, grid, in_specs, out_specs, prefetch=0, scratch=()):
    return pl.pallas_call(
        body,
        out_shape=out_shape,
        grid_spec=pltpu.PrefetchScalarGridSpec(
            num_scalar_prefetch=prefetch,
            grid=grid,
            in_specs=in_specs,
            out_specs=out_specs,
            scratch_shapes=list(scratch),
        ),
        compiler_params=pltpu.CompilerParams(vmem_limit_bytes=60 * MIB),
        cost_estimate=pl.CostEstimate(flops=1, bytes_accessed=1, transcendentals=0),
    )


def block(dims, index):
    return pl.BlockSpec(dims, index)


def whole(dims):
    zero = (0,) * len(dims)
    return pl.BlockSpec(dims, lambda *_: zero)


def reset_masks(docs_ref, row, docs, length):
    at_i = lax.broadcasted_iota(jnp.int32, (length, length), 0)
    at_j = lax.broadcasted_iota(jnp.int32, (length, length), 1)
    token = lax.broadcasted_iota(jnp.int32, (length, 1), 0)
    visible = at_i >= at_j
    alive = token >= 0
    tail = token >= 0
    whole_alive = jnp.float32(1.0)
    for n in range(docs):
        start = docs_ref[row * docs + n]
        visible = visible & jnp.logical_not((at_j < start) & (start <= at_i))
        inside = (start >= 0) & (start < length)
        first = jnp.where(start >= 0, start, length)
        alive = alive & (token < first)
        last = jnp.where(start < length, start, -1)
        tail = tail & (token >= last)
        whole_alive = whole_alive * jnp.where(inside, 0.0, 1.0)
    return visible, alive.astype(F32), tail.astype(F32), whole_alive


def lower_ones(length, strict=False):
    at_i = lax.broadcasted_iota(jnp.int32, (length, length), 0)
    at_j = lax.broadcasted_iota(jnp.int32, (length, length), 1)
    return (at_i > at_j if strict else at_i >= at_j).astype(F32)


def project_body(
    rows, docs, length, hk, hv, parts,
    docs_ref, table_ref, x_ref, gain_ref, wk_ref, wv_ref, wrd_ref, wru_ref, bias_ref,
    normed_ref, k_ref, v_ref, ra_ref, gp_ref, cum_ref, keep_a_ref, send_a_ref, keep_b_ref,
    send_b_ref, decay_ref,
    hold,
):
    x = x_ref[...].astype(F32)
    inv = lax.rsqrt(jnp.mean(x * x, axis=-1, keepdims=True) + EPS)
    normed = (x * inv * gain_ref[...]).astype(BF)
    normed_ref[...] = normed
    rank = nt(normed, wrd_ref[...]).astype(BF)
    ra_ref[...] = rank
    gate = nn(rank, wru_ref[...]) + bias_ref[...]
    gp_ref[...] = gate
    key = nn(normed, wk_ref[...]).astype(BF)
    k_ref[...] = key
    value = nn(normed, wv_ref[...]).astype(BF)
    v_ref[...] = value
    log_decay = (jnp.minimum(gate, 0.0) - jnp.log1p(jnp.exp(-jnp.abs(gate)))) * (1.0 / 16.0)
    tri = lower_ones(length)
    size = hv // parts
    for r in range(rows):
        at = slice(r * length, (r + 1) * length)
        row = pl.program_id(0) * rows + r
        cum = nn(tri, log_decay[at], HIGHEST)
        cum_ref[at, :] = cum
        _, _, tail, whole_alive = reset_masks(docs_ref, row, docs, length)
        last = cum[length - 1 :, :]
        decay_ref[r] = jnp.exp(last) * whole_alive
        weighted = (key[at].astype(F32) * jnp.exp(last - cum) * tail).astype(BF)
        for h in range(HEADS):
            hold[...] = tn(value[at, h * hv : (h + 1) * hv], weighted[:, h * hk : (h + 1) * hk])
            keep_ref, send_ref = (keep_a_ref, send_a_ref) if h < HEADS // 2 else (keep_b_ref, send_b_ref)
            for j in range(parts // 2):
                first = pl.multiple_of(table_ref[j] * size, size)
                keep_ref[j, r, h % (HEADS // 2)] = hold[pl.ds(first, size), :]
                second = pl.multiple_of(table_ref[parts // 2 + j] * size, size)
                send_ref[j, r, h % (HEADS // 2)] = hold[pl.ds(second, size), :]


def project_all(x, docs, table, gain, wk, wv, wrd, wru, bias, dims):
    row_count, length, width, kw, vw, ndocs, parts = dims
    tokens = row_count * length
    rows = 2 if row_count % 2 == 0 else 1
    tm = rows * length
    hk, hv = kw // HEADS, vw // HEADS
    rank = wrd.shape[0]
    size = hv // parts
    tile = lambda n: block((tm, n), lambda i, *_: (i, 0))
    half = (parts // 2, row_count, HEADS // 2, size, hk)
    half_block = block((parts // 2, rows, HEADS // 2, size, hk), lambda i, *_: (0, i, 0, 0, 0))
    body = functools.partial(project_body, rows, ndocs, length, hk, hv, parts)
    return call(
        body,
        (
            shape((tokens, width), BF),
            shape((tokens, kw), BF),
            shape((tokens, vw), BF),
            shape((tokens, rank), BF),
            shape((tokens, kw), F32),
            shape((tokens, kw), F32),
            shape(half, F32),
            shape(half, F32),
            shape(half, F32),
            shape(half, F32),
            shape((row_count, 1, kw), F32),
        ),
        (row_count // rows,),
        [
            tile(width), whole((1, width)), whole(wk.shape), whole(wv.shape), whole(wrd.shape),
            whole(wru.shape), whole((1, kw)),
        ],
        (
            tile(width), tile(kw), tile(vw), tile(rank), tile(kw), tile(kw),
            half_block, half_block, half_block, half_block,
            block((rows, 1, kw), lambda i, *_: (i, 0, 0)),
        ),
        prefetch=2,
        scratch=[pltpu.VMEM((hv, hk), F32)],
    )(docs, table, x, gain.reshape(1, -1), wk, wv, wrd, wru, bias.reshape(1, -1))


def readers_body(normed_ref, wq_ref, wog_ref, q_ref, og_ref):
    q_ref[...] = nn(normed_ref[...], wq_ref[...]).astype(BF)
    og_ref[...] = nn(normed_ref[...], wog_ref[...])


def readers_all(normed, wq, wog):
    tokens, width = normed.shape
    tm = 256 if tokens % 256 == 0 else 128
    tile = lambda n: block((tm, n), lambda i: (i, 0))
    return call(
        readers_body,
        (shape((tokens, wq.shape[1]), BF), shape((tokens, wog.shape[1]), F32)),
        (tokens // tm,),
        [tile(width), whole(wq.shape), whole(wog.shape)],
        (tile(wq.shape[1]), tile(wog.shape[1])),
    )(normed, wq, wog)


def span_factors(cum, length):
    middle = cum[length // 2 - 1 : length // 2, :]
    return jnp.exp(cum - middle), jnp.exp(middle - cum)


def inner_body(docs, length, hk, hv, docs_ref, q_ref, k_ref, v_ref, cum_ref, inner_ref):
    visible, _, _, _ = reset_masks(docs_ref, pl.program_id(0), docs, length)
    up, down = span_factors(cum_ref[...], length)
    q = (q_ref[...].astype(F32) * up).astype(BF)
    k = (k_ref[...].astype(F32) * down).astype(BF)
    for h in range(HEADS):
        kk = slice(h * hk, (h + 1) * hk)
        vv = slice(h * hv, (h + 1) * hv)
        scores = jnp.where(visible, nt(q[:, kk], k[:, kk]), 0.0).astype(BF)
        inner_ref[:, vv] = nn(scores, v_ref[:, vv])


def inner_all(q, k, v, cum, docs, dims):
    row_count, length, width, kw, vw, ndocs, parts = dims
    tokens = row_count * length
    tile = lambda n: block((length, n), lambda i, *_: (i, 0))
    return call(
        functools.partial(inner_body, ndocs, length, kw // HEADS, vw // HEADS),
        shape((tokens, vw), F32),
        (row_count,),
        [tile(kw), tile(kw), tile(vw), tile(kw)],
        tile(vw),
        prefetch=1,
    )(docs, q, k, v, cum)


def gather_state(near_ref, far_ref, table_ref, h, parts):
    half = parts // 2
    pieces = []
    for p in range(parts):
        place = table_ref[parts + p]
        near = near_ref[jnp.minimum(place, half - 1), 0, h]
        far = far_ref[jnp.maximum(place - half, 0), 0, h]
        pieces.append(jnp.where(place < half, near, far))
    return jnp.concatenate(pieces, axis=0)


def mix_body(
    docs, length, hk, hv, parts,
    docs_ref, table_ref, q_ref, cum_ref, inner_ref, og_ref, near_a_ref, far_a_ref, near_b_ref, far_b_ref,
    gain_ref,
    mixed_ref, gated_ref, kept_ref,
):
    _, alive, _, _ = reset_masks(docs_ref, pl.program_id(0), docs, length)
    reach = (q_ref[...].astype(F32) * jnp.exp(cum_ref[...]) * alive).astype(BF)
    scale = hk ** (-0.5)
    for h in range(HEADS):
        kk = slice(h * hk, (h + 1) * hk)
        vv = slice(h * hv, (h + 1) * hv)
        near_ref, far_ref = (near_a_ref, far_a_ref) if h < HEADS // 2 else (near_b_ref, far_b_ref)
        state = gather_state(near_ref, far_ref, table_ref, h % (HEADS // 2), parts).astype(BF)
        kept_ref[0, h] = state
        mixed = scale * (inner_ref[:, vv] + nt(reach[:, kk], state))
        mixed_ref[:, vv] = mixed
        inv = lax.rsqrt(jnp.mean(mixed * mixed, axis=-1, keepdims=True) + EPS)
        og = og_ref[:, vv]
        gated_ref[:, vv] = (mixed * inv * gain_ref[...] * og * jax.nn.sigmoid(og)).astype(BF)


def mix_all(q, cum, inner, og, states, gain, docs, table, dims):
    row_count, length, width, kw, vw, ndocs, parts = dims
    tokens = row_count * length
    hk, hv = kw // HEADS, vw // HEADS
    tile = lambda n: block((length, n), lambda i, *_: (i, 0))
    half = block((parts // 2, 1, HEADS // 2, hv // parts, hk), lambda i, *_: (0, i, 0, 0, 0))
    return call(
        functools.partial(mix_body, ndocs, length, hk, hv, parts),
        (
            shape((tokens, vw), F32),
            shape((tokens, vw), BF),
            shape((row_count, HEADS, hv, hk), BF),
        ),
        (row_count,),
        [
            tile(kw), tile(kw), tile(vw), tile(vw), half, half, half, half, whole((1, hv)),
        ],
        (tile(vw), tile(vw), block((1, HEADS, hv, hk), lambda i, *_: (i, 0, 0, 0))),
        prefetch=2,
    )(docs, table, q, cum, inner, og, *states, gain.reshape(1, -1))


def hidden_back_body(cot_ref, wd_ref, dh_ref):
    dh_ref[...] = nt(cot_ref[...], wd_ref[...])


def hidden_back_all(cot, wd):
    tokens, width = cot.shape
    ff, tile = wd.shape[0], 256
    return call(
        hidden_back_body,
        shape((tokens, ff), F32),
        (ff // tile,),
        [whole((tokens, width)), block((tile, width), lambda i: (i, 0))],
        block((tokens, tile), lambda i: (0, i)),
    )(cot, wd)


def ff_body(
    x_ref, gated_ref, wo_ref, gain_ref, wg_ref, wu_ref, dh_ref,
    hidden_ref, dg_ref, du_ref, normed2_ref, middle_ref,
):
    @pl.when(pl.program_id(0) == 0)
    def _():
        mid = x_ref[...].astype(F32) + nn(gated_ref[...], wo_ref[...])
        middle_ref[...] = mid
        inv = lax.rsqrt(jnp.mean(mid * mid, axis=-1, keepdims=True) + EPS)
        normed2_ref[...] = (mid * inv * gain_ref[...]).astype(BF)

    normed2 = normed2_ref[...]
    gate = nn(normed2, wg_ref[...])
    up = nn(normed2, wu_ref[...])
    d_hidden = dh_ref[...]
    sig = jax.nn.sigmoid(gate)
    act = gate * sig
    hidden_ref[...] = (act * up).astype(BF)
    dg_ref[...] = (d_hidden * up * sig * (1.0 + gate * (1.0 - sig))).astype(BF)
    du_ref[...] = (d_hidden * act).astype(BF)


def ff_all(x, gated, wo, gain, wg, wu, dh):
    tokens, width = x.shape
    ff = wg.shape[1]
    tile = 256
    col = lambda n: block((n, tile), lambda i: (0, i))
    once = lambda dims: pl.BlockSpec(dims, lambda i: (0, 0), pipeline_mode=pl.Buffered(1))
    return call(
        ff_body,
        (
            shape((tokens, ff), BF), shape((tokens, ff), BF), shape((tokens, ff), BF),
            shape((tokens, width), BF), shape((tokens, width), F32),
        ),
        (ff // tile,),
        [
            once((tokens, width)), once(gated.shape), once(wo.shape), once((1, width)),
            col(width), col(width), col(tokens),
        ],
        (
            col(tokens), col(tokens), col(tokens), whole((tokens, width)), whole((tokens, width)),
        ),
    )(x, gated, wo, gain.reshape(1, -1), wg, wu, dh)


def ff_back_body(
    steps,
    hidden_ref, dg_ref, du_ref, wd_ref, wg_ref, wu_ref, middle_ref, cot_ref, wo_ref, gain_ref,
    out_ref, dmid_ref, dout_ref, dgated_ref, gnorm_ref,
):
    total, back = dgated_ref, dmid_ref
    step = pl.program_id(0)
    tokens = middle_ref.shape[0]
    rows = 256 if tokens % 256 == 0 else tokens
    for first in range(0, tokens, rows):
        at = slice(first, first + rows)
        more = nn(hidden_ref[at, :], wd_ref[...])
        more_back = nt(dg_ref[at, :], wg_ref[...]) + nt(du_ref[at, :], wu_ref[...])

        @pl.when(step == 0)
        def _(at=at, more=more, more_back=more_back):
            total[at, :] = more
            back[at, :] = more_back

        @pl.when(step > 0)
        def _(at=at, more=more, more_back=more_back):
            total[at, :] += more
            back[at, :] += more_back

    @pl.when(step == steps - 1)
    def _():
        gnorm = jnp.zeros((1, middle_ref.shape[1]), F32)
        for first in range(0, tokens, rows):
            at = slice(first, first + rows)
            mid = middle_ref[at, :]
            out_ref[at, :] = (mid + total[at, :]).astype(BF)
            inv = lax.rsqrt(jnp.mean(mid * mid, axis=-1, keepdims=True) + EPS)
            d_normed2 = back[at, :]
            gnorm = gnorm + jnp.sum(d_normed2 * mid * inv, axis=0, keepdims=True)
            scaled = d_normed2 * gain_ref[...]
            d_middle = (
                cot_ref[at, :].astype(F32)
                + inv * scaled
                - mid * (inv * inv * inv) * jnp.mean(scaled * mid, axis=-1, keepdims=True)
            )
            dmid_ref[at, :] = d_middle
            d_out = d_middle.astype(BF)
            dout_ref[at, :] = d_out
            dgated_ref[at, :] = nt(d_out, wo_ref[...])
        gnorm_ref[...] = gnorm


def ff_back_all(hidden, dg, du, wd, wg, wu, middle, cot, wo, gain):
    tokens, width = middle.shape
    vw, ff = wo.shape[0], wg.shape[1]
    tile = 1408 if ff % 1408 == 0 else 256
    steps = ff // tile
    col = lambda n: block((n, tile), lambda i: (0, i))
    once = lambda dims: pl.BlockSpec(dims, lambda i: (0, 0), pipeline_mode=pl.Buffered(1))
    return call(
        functools.partial(ff_back_body, steps),
        (
            shape((tokens, width), BF), shape((tokens, width), F32), shape((tokens, width), BF),
            shape((tokens, vw), F32), shape((1, width), F32),
        ),
        (steps,),
        [
            col(tokens), col(tokens), col(tokens), block((tile, width), lambda i: (i, 0)),
            col(width), col(width), once((tokens, width)), once((tokens, width)), once(wo.shape),
            once((1, width)),
        ],
        (
            whole((tokens, width)), whole((tokens, width)), whole((tokens, width)),
            whole((tokens, vw)), whole((1, width)),
        ),
    )(hidden, dg, du, wd, wg, wu, middle, cot, wo, gain.reshape(1, -1))


def head_back_body(
    docs, length, hk, hv, parts,
    docs_ref, table_ref, dgated_ref, og_ref, mixed_ref, q_ref, cum_ref, gain_ref,
    dmix_ref, dog_ref, keep_ref, send_ref, ggroup_ref,
    hold,
):
    row = pl.program_id(0)
    _, alive, _, _ = reset_masks(docs_ref, row, docs, length)
    reach = (q_ref[...].astype(F32) * jnp.exp(cum_ref[...]) * alive).astype(BF)
    scale = hk ** (-0.5)
    size = hv // parts
    ggroup = jnp.zeros((1, hv), F32)
    for h in range(HEADS):
        kk = slice(h * hk, (h + 1) * hk)
        vv = slice(h * hv, (h + 1) * hv)
        mixed = mixed_ref[:, vv]
        inv = lax.rsqrt(jnp.mean(mixed * mixed, axis=-1, keepdims=True) + EPS)
        og = og_ref[:, vv]
        sig = jax.nn.sigmoid(og)
        dgated = dgated_ref[:, vv]
        unit = mixed * inv
        dog_ref[:, vv] = (
            dgated * unit * gain_ref[...] * sig * (1.0 + og * (1.0 - sig))
        ).astype(BF)
        d_heads = dgated * og * sig
        ggroup = ggroup + jnp.sum(d_heads * unit, axis=0, keepdims=True)
        scaled = d_heads * gain_ref[...]
        d_mixed = inv * scaled - mixed * (inv * inv * inv) * jnp.mean(
            scaled * mixed, axis=-1, keepdims=True
        )
        d_mixed = (scale * d_mixed).astype(BF)
        dmix_ref[:, vv] = d_mixed
        hold[...] = tn(d_mixed, reach[:, kk])
        for j in range(parts // 2):
            first = pl.multiple_of(table_ref[j] * size, size)
            keep_ref[j, 0, h] = hold[pl.ds(first, size), :]
            second = pl.multiple_of(table_ref[parts // 2 + j] * size, size)
            send_ref[j, 0, h] = hold[pl.ds(second, size), :]

    @pl.when(row == 0)
    def _():
        ggroup_ref[...] = ggroup

    @pl.when(row > 0)
    def _():
        ggroup_ref[...] += ggroup


def head_back_all(dgated, og, mixed, q, cum, gain, docs, table, dims):
    row_count, length, width, kw, vw, ndocs, parts = dims
    tokens = row_count * length
    hk, hv = kw // HEADS, vw // HEADS
    size = hv // parts
    tile = lambda n: block((length, n), lambda i, *_: (i, 0))
    half = (parts // 2, row_count, HEADS, size, hk)
    half_block = block((parts // 2, 1, HEADS, size, hk), lambda i, *_: (0, i, 0, 0, 0))
    return call(
        functools.partial(head_back_body, ndocs, length, hk, hv, parts),
        (
            shape((tokens, vw), BF), shape((tokens, vw), BF),
            shape(half, F32), shape(half, F32), shape((1, hv), F32),
        ),
        (row_count,),
        [tile(vw), tile(vw), tile(vw), tile(kw), tile(kw), whole((1, hv))],
        (tile(vw), tile(vw), half_block, half_block, whole((1, hv))),
        prefetch=2,
        scratch=[pltpu.VMEM((hv, hk), F32)],
    )(docs, table, dgated, og, mixed, q, cum, gain.reshape(1, -1))


def mix_local_body(
    docs, length, hk, hv,
    docs_ref, q_ref, k_ref, v_ref, cum_ref, dmix_ref, state_ref,
    dq_ref, dk_ref, dv_ref, decay_ref,
):
    visible, alive, _, _ = reset_masks(docs_ref, pl.program_id(0), docs, length)
    cum = cum_ref[...]
    up, down = span_factors(cum, length)
    from_start = jnp.exp(cum) * alive
    q = q_ref[...].astype(F32)
    q_span = (q * up).astype(BF)
    k_span = (k_ref[...].astype(F32) * down).astype(BF)
    reach = (q * from_start).astype(BF)
    later = []
    for h in range(HEADS):
        kk = slice(h * hk, (h + 1) * hk)
        vv = slice(h * hv, (h + 1) * hv)
        qs, ks = q_span[:, kk], k_span[:, kk]
        d_mix = dmix_ref[:, vv]
        scores = jnp.where(visible, nt(qs, ks), 0.0).astype(BF)
        d_scores = jnp.where(visible, nt(d_mix, v_ref[:, vv]), 0.0).astype(BF)
        dq_in = nn(d_scores, ks)
        dk_in = tn(d_scores, qs)
        dq_out = nn(d_mix, state_ref[0, h])
        dq_ref[:, kk] = (dq_in * up[:, kk] + dq_out * from_start[:, kk]).astype(BF)
        dk_ref[:, kk] = dk_in * down[:, kk]
        dv_ref[:, vv] = tn(scores, d_mix)
        later.append(
            qs.astype(F32) * dq_in - ks.astype(F32) * dk_in + reach[:, kk].astype(F32) * dq_out
        )
    at_i = lax.broadcasted_iota(jnp.int32, (length, length), 0)
    at_j = lax.broadcasted_iota(jnp.int32, (length, length), 1)
    decay_ref[...] = nn((at_i <= at_j).astype(F32), jnp.concatenate(later, axis=1), HIGHEST)


def mix_local_all(q, k, v, cum, dmix, state, docs, dims):
    row_count, length, width, kw, vw, ndocs, parts = dims
    tokens = row_count * length
    hk, hv = kw // HEADS, vw // HEADS
    tile = lambda n: block((length, n), lambda i, *_: (i, 0))
    return call(
        functools.partial(mix_local_body, ndocs, length, hk, hv),
        (
            shape((tokens, kw), BF), shape((tokens, kw), F32), shape((tokens, vw), F32),
            shape((tokens, kw), F32),
        ),
        (row_count,),
        [
            tile(kw), tile(kw), tile(vw), tile(kw), tile(vw),
            block((1, HEADS, hv, hk), lambda i, *_: (i, 0, 0, 0)),
        ],
        (tile(kw), tile(kw), tile(vw), tile(kw)),
        prefetch=1,
    )(docs, q, k, v, cum, dmix, state)


def mix_back_body(
    docs, length, hk, hv, parts,
    docs_ref, table_ref, k_ref, v_ref, cum_ref, gp_ref, ra_ref, state_ref, dk_ref, dv_ref, decay_ref,
    near_ref, far_ref, wru_ref,
    dk_out_ref, dv_out_ref, drank_ref, grup_ref, gbias_ref,
):
    row = pl.program_id(0)
    _, _, tail, whole_alive = reset_masks(docs_ref, row, docs, length)
    cum = cum_ref[...]
    last = cum[length - 1 :, :]
    to_end = jnp.exp(last - cum) * tail
    weighted = (k_ref[...].astype(F32) * to_end).astype(BF)
    earlier, crossing = [], []
    for h in range(HEADS):
        kk = slice(h * hk, (h + 1) * hk)
        vv = slice(h * hv, (h + 1) * hv)
        grad32 = gather_state(near_ref, far_ref, table_ref, h, parts)
        grad = grad32.astype(BF)
        dk_out = nn(v_ref[:, vv], grad)
        dk_out_ref[:, kk] = (dk_ref[:, kk] + dk_out * to_end[:, kk]).astype(BF)
        dv_out_ref[:, vv] = (
            dv_ref[:, vv] + nt(weighted[:, kk], grad)
        ).astype(BF)
        earlier.append(weighted[:, kk].astype(F32) * dk_out)
        crossing.append(jnp.sum(state_ref[0, h].astype(F32) * grad32, axis=0, keepdims=True))
    d_decay = (
        decay_ref[...]
        + nn(lower_ones(length, True), jnp.concatenate(earlier, axis=1), HIGHEST)
        + jnp.exp(last) * whole_alive * jnp.concatenate(crossing, axis=1)
    )
    d_gate = (d_decay * jax.nn.sigmoid(-gp_ref[...]) * (1.0 / 16.0)).astype(BF)
    drank_ref[...] = nt(d_gate, wru_ref[...]).astype(BF)
    grup = tn(ra_ref[...], d_gate)
    gbias = jnp.sum(d_gate.astype(F32), axis=0, keepdims=True)

    @pl.when(row == 0)
    def _():
        grup_ref[...] = grup
        gbias_ref[...] = gbias

    @pl.when(row > 0)
    def _():
        grup_ref[...] += grup
        gbias_ref[...] += gbias


def mix_back_all(k, v, cum, gp, ra, state, dk, dv, decay, near, far, wru, docs, table, dims):
    row_count, length, width, kw, vw, ndocs, parts = dims
    tokens = row_count * length
    hk, hv = kw // HEADS, vw // HEADS
    rank = wru.shape[0]
    tile = lambda n: block((length, n), lambda i, *_: (i, 0))
    half = block((parts // 2, 1, HEADS, hv // parts, hk), lambda i, *_: (0, i, 0, 0, 0))
    return call(
        functools.partial(mix_back_body, ndocs, length, hk, hv, parts),
        (
            shape((tokens, kw), BF), shape((tokens, vw), BF), shape((tokens, rank), BF),
            shape((rank, kw), F32), shape((1, kw), F32),
        ),
        (row_count,),
        [
            tile(kw), tile(vw), tile(kw), tile(kw), tile(rank),
            block((1, HEADS, hv, hk), lambda i, *_: (i, 0, 0, 0)),
            tile(kw), tile(vw), tile(kw), half, half, whole((rank, kw)),
        ],
        (tile(kw), tile(vw), tile(rank), whole((rank, kw)), whole((1, kw))),
        prefetch=2,
    )(docs, table, k, v, cum, gp, ra, state, dk, dv, decay, near, far, wru)


def input_back_body(
    x_ref, dmid_ref, dq_ref, dk_ref, dv_ref, dog_ref, drank_ref, gain_ref, wq_ref, wk_ref, wv_ref, wog_ref, wrd_ref,
    gin_ref, gnorm_ref,
):
    step = pl.program_id(0)
    d_normed = (
        nt(dq_ref[...], wq_ref[...])
        + nt(dk_ref[...], wk_ref[...])
        + nt(dv_ref[...], wv_ref[...])
        + nt(dog_ref[...], wog_ref[...])
        + nn(drank_ref[...], wrd_ref[...])
    )
    x = x_ref[...].astype(F32)
    inv = lax.rsqrt(jnp.mean(x * x, axis=-1, keepdims=True) + EPS)
    gnorm = jnp.sum(d_normed * x * inv, axis=0, keepdims=True)
    scaled = d_normed * gain_ref[...]
    gin_ref[...] = (
        dmid_ref[...]
        + inv * scaled
        - x * (inv * inv * inv) * jnp.mean(scaled * x, axis=-1, keepdims=True)
    )

    @pl.when(step == 0)
    def _():
        gnorm_ref[...] = gnorm

    @pl.when(step > 0)
    def _():
        gnorm_ref[...] += gnorm


def input_back_all(x, dmid, dq, dk, dv, dog, drank, gain, wq, wk, wv, wog, wrd):
    tokens, width = x.shape
    kw, vw = wq.shape[1], wv.shape[1]
    tm = 256 if tokens % 256 == 0 else 128
    tile = lambda n: block((tm, n), lambda i: (i, 0))
    return call(
        input_back_body,
        (shape((tokens, width), F32), shape((1, width), F32)),
        (tokens // tm,),
        [
            tile(width), tile(width), tile(kw), tile(kw), tile(vw), tile(vw), tile(drank.shape[1]),
            whole((1, width)), whole(wq.shape), whole(wk.shape), whole(wv.shape), whole(wog.shape),
            whole(wrd.shape),
        ],
        (tile(width), whole((1, width))),
    )(x, dmid, dq, dk, dv, dog, drank, gain.reshape(1, -1), wq, wk, wv, wog, wrd)


def weight_body(groups, lefts, pieces, *refs):
    tables = refs[: len(groups)]
    refs = refs[len(groups) :]
    left_refs, refs = refs[:lefts], refs[lefts:]
    count = sum(len(group) for group in groups)
    rights, refs = refs[:count], refs[count:]
    outs, refs = refs[: 2 * len(groups)], refs[2 * len(groups) :]
    turned, holds = refs[:lefts], refs[lefts:]

    @pl.when(pl.program_id(0) == 0)
    def _():
        for n in range(lefts):
            turned[n][...] = left_refs[n][...].T

    at = 0
    for g, group in enumerate(groups):
        keep_ref, send_ref = outs[2 * g], outs[2 * g + 1]
        place = 0
        for left in group:
            hold = holds[g]
            hold[...] = nn(turned[left][...], rights[at][...])
            per = hold.shape[0] // pieces
            rows = slice(place, place + per)
            for j in range(pieces // 2):
                first = pl.multiple_of(tables[g][j] * per, per)
                keep_ref[j, rows, :] = hold[pl.ds(first, per), :]
                second = pl.multiple_of(tables[g][pieces // 2 + j] * per, per)
                send_ref[j, rows, :] = hold[pl.ds(second, per), :]
            at, place = at + 1, place + per


def weight_grads(groups, tables, steps=2):
    pieces = tables[0].shape[0]
    tokens = groups[0][0][0].shape[0]
    out = []
    if any(left.shape[1] // pieces % 8 for group in groups for left, _ in group):
        for group, table in zip(groups, tables):
            parts = [tn(left, right) for left, right in group]
            parts = [part.reshape(pieces, -1, part.shape[1]) for part in parts]
            parts = jnp.concatenate(parts, axis=1)[table]
            out.append((parts[: pieces // 2], parts[pieces // 2 :]))
        return out
    lefts, index = [], []
    for group in groups:
        index.append([])
        for left, _ in group:
            known = [n for n, other in enumerate(lefts) if other is left]
            if not known:
                lefts.append(left)
            index[-1].append(known[0] if known else len(lefts) - 1)
    rights = [right for group in groups for _, right in group]
    column = lambda n: block((tokens, n // steps), lambda i, *_: (0, i))
    shapes, blocks, holds = [], [], []
    for group in groups:
        rows, cols = group[0][0].shape[1], group[0][1].shape[1]
        dims = (pieces // 2, len(group) * rows // pieces, cols)
        shapes += [shape(dims, F32)] * 2
        blocks += [block(dims[:2] + (cols // steps,), lambda i, *_: (0, 0, i))] * 2
        holds.append(pltpu.VMEM((rows, cols // steps), F32))
    flat = call(
        functools.partial(weight_body, index, len(lefts), pieces),
        tuple(shapes),
        (steps,),
        [whole(left.shape) for left in lefts] + [column(right.shape[1]) for right in rights],
        tuple(blocks),
        prefetch=len(groups),
        scratch=[pltpu.VMEM(left.shape[::-1], BF) for left in lefts] + holds,
    )(*tables, *lefts, *rights)
    return [(flat[2 * g], flat[2 * g + 1]) for g in range(len(groups))]


def small_body(
    pieces,
    table_ref, normed_ref, drank_ref, gnorm1_ref, gnorm2_ref, grup_ref, gbias_ref, ggroup_ref,
    keep_ref, send_ref,
    hold,
):
    width, kw, hv = gnorm1_ref.shape[1], gbias_ref.shape[1], ggroup_ref.shape[1]
    rank = grup_ref.shape[0]

    def stand(rows):
        have = sum(row.shape[0] for row in rows)
        return jnp.concatenate(rows + [jnp.zeros((128 - have, rows[0].shape[1]), F32)], axis=0).T

    spread = jnp.zeros((normed_ref.shape[0], 128 - rank), BF)
    hold[:width, :] = tn(normed_ref[...], jnp.concatenate([drank_ref[...], spread], axis=1)) + stand(
        [jnp.zeros((rank, width), F32), gnorm1_ref[...], gnorm2_ref[...]]
    )
    hold[width : width + kw, :] = stand([grup_ref[...], gbias_ref[...]])
    hold[width + kw :, :] = stand([ggroup_ref[...]])
    first, place = 0, 0
    for rows in (width, kw, hv):
        per = rows // pieces
        for j in range(pieces // 2):
            keep = pl.multiple_of(first + table_ref[j] * per, per)
            keep_ref[j, place : place + per, :] = hold[pl.ds(keep, per), :]
            send = pl.multiple_of(first + table_ref[pieces // 2 + j] * per, per)
            send_ref[j, place : place + per, :] = hold[pl.ds(send, per), :]
        first, place = first + rows, place + per


def small_grads(normed, drank, gnorm1, gnorm2, grup, gbias, ggroup, table):
    pieces, rank = table.shape[0], grup.shape[0]
    width, kw, hv = gnorm1.shape[1], gbias.shape[1], ggroup.shape[1]
    rows = (width + kw + hv) // pieces
    if hv // pieces % 8:
        wide = lambda value: jnp.pad(value, ((0, 0), (0, 128 - value.shape[1])))
        cut = lambda value: wide(value).reshape(pieces, -1, 128)
        both = jnp.concatenate(
            [
                cut(jnp.concatenate([tn(normed, drank), gnorm1.T, gnorm2.T], axis=1)),
                cut(jnp.concatenate([grup.T, gbias.T], axis=1)),
                cut(ggroup.T),
            ],
            axis=1,
        )[table]
        return both[: pieces // 2], both[pieces // 2 :]
    half = shape((pieces // 2, rows, 128), F32)
    operands = (normed, drank, gnorm1, gnorm2, grup, gbias, ggroup)
    return call(
        functools.partial(small_body, pieces),
        (half, half),
        (1,),
        [whole(value.shape) for value in operands],
        (whole(half.shape), whole(half.shape)),
        prefetch=1,
        scratch=[pltpu.VMEM((width + kw + hv, 128), F32)],
    )(table, *operands)


def bits_of(n):
    return n.bit_length() - 1


class Links:
    def __init__(self):
        self.n_dp, self.n_seq = lax.axis_size("dp"), lax.axis_size("seq")
        self.seq_bits, self.dp_bits = bits_of(self.n_seq), bits_of(self.n_dp)
        self.at_seq = lax.axis_index("seq")
        self.me = lax.axis_index("dp") * self.n_seq + self.at_seq

    def swap(self, value, bit):
        name, n, flip = "seq", self.n_seq, 1 << bit
        if bit >= self.seq_bits:
            name, n, flip = "dp", self.n_dp, 1 << (bit - self.seq_bits)
        return lax.ppermute(value, name, [(i, i ^ flip) for i in range(n)])

    def table(self, order):
        n = 1 << len(order)
        places = [
            sum(((at >> (len(order) - 1 - k)) & 1) << bit for k, bit in enumerate(order))
            for at in range(n)
        ]
        here = self.me if n == self.n_dp * self.n_seq else self.at_seq
        return jnp.array(places, jnp.int32) ^ here

    def order(self, *names):
        across = tuple(range(self.seq_bits, self.seq_bits + self.dp_bits))
        bits = [0]
        for name in names:
            bits.extend(across if name == "x" else [{"y": 1, "z0": 2, "z1": 3}[name]])
        return tuple(bits) + tuple(b for b in range(self.seq_bits) if b not in bits)


class Turns:
    def __init__(self):
        self.last = ()

    def after(self, value):
        return lax.optimization_barrier((value,) + self.last)[0]

    def done(self, *values):
        self.last = values


class Task:
    def __init__(self, steps):
        self.steps, self.wanted, self.got, self.begun, self.over = steps, [], None, False, False

    def advance(self, turns):
        if self.over:
            return
        if self.wanted:
            start([self], turns)
        try:
            self.wanted = self.steps.send(self.got) if self.begun else next(self.steps)
            self.begun = True
        except StopIteration:
            self.wanted, self.over = [], True

    def finish(self, turns):
        while not self.over:
            self.advance(turns)


def start(tasks, turns):
    tasks = [task for task in tasks if task.wanted]
    values = [value for task in tasks for value, _ in task.wanted]
    if not values:
        return
    tied = lax.optimization_barrier(tuple(values) + turns.last)[: len(values)]
    turns.done(tied[0])
    tied = iter(tied)
    for task in tasks:
        task.got = [move(next(tied)) for _, move in task.wanted]
        task.wanted = []


def reduce_steps(links, turns, make, order, out, name):
    keep, send = make()
    turns.done(keep, send)
    for k, bit in enumerate(order):
        (got,) = yield [(send, functools.partial(links.swap, bit=bit))]
        keep = turns.after(keep)
        if k == len(order) - 1:
            out[name] = keep + got
            turns.done(out[name])
            return
        half = keep.shape[0] // 2
        send = keep[half:] + got[half:]
        keep = keep[:half] + got[:half]
        turns.done(keep, send)


def scan_steps(links, turns, make, decays, backwards, out):
    keep, send, decay = make()
    bits = links.seq_bits
    levels = []
    kept = [] if decays is None else decays
    turns.done(keep, send)
    for bit in range(bits - 1):
        swap = functools.partial(links.swap, bit=bit)
        if decays is None:
            got, got_d = yield [(send, swap), (decay, swap)]
            kept.append((decay, got_d))
            decay = decay * got_d
        else:
            (got,) = yield [(send, swap)]
        mine_d, got_d = kept[bit]
        keep = turns.after(keep)
        odd = (links.at_seq >> bit) & 1
        second = (odd == 0) if backwards else (odd == 1)
        levels.append((second, keep, got, mine_d, got_d))
        total = jnp.where(second, mine_d * got + keep, got_d * keep + got)
        half = total.shape[0] // 2
        if bit < bits - 2:
            keep, send = total[:half], total[half:]
            turns.done(keep, send)
        else:
            send = total
            turns.done(send)
    flip = 1 << (bits - 1)
    pairs = [(i, i ^ flip) for i in range(links.n_seq) if ((i >> (bits - 1)) & 1) == int(backwards)]
    (state,) = yield [(send, lambda value: lax.ppermute(value, "seq", pairs))]
    for bit in reversed(range(bits - 1)):
        second, keep, got, mine_d, got_d = levels[bit]
        keep = turns.after(keep)
        theirs = jnp.where(second, state, mine_d * state + keep)
        mine = jnp.where(second, got_d * state + got, state)
        turns.done(theirs, mine)
        (far,) = yield [(theirs, functools.partial(links.swap, bit=bit))]
        if bit == 0:
            out["near"], out["far"], out["decays"] = mine, far, kept
        else:
            mine = turns.after(mine)
            state = jnp.concatenate([mine, far], axis=0)


ROUTES = {
    "gate": ("x", "y", "z0", "z1"),
    "up": ("y", "x", "z0", "z1"),
    "down": ("z0", "x", "y", "z1"),
    "mid": ("x", "y", "z0", "z1"),
    "qk": ("x", "y", "z0", "z1"),
    "v": ("y", "x", "z0", "z1"),
    "small": ("x", "y", "z0", "z1"),
}
SCHEDULE = (
    "gate", "up", ("gate", "up"), "down", ("down",), "gate", ("gate",), "up", ("up",), "down",
    ("down",), "ff", "scan", ("scan",), "mid", "gate", "up", "down", "scan", ("scan", "up",
    "mid"), "mid", "scan", ("scan", "gate"), "up", "scan", ("scan", "mid"), "local", "gate",
    "scan", ("scan",), "scan", ("scan",), "mid", "scan", ("scan", "gate", "up", "down", "mid"),
    "scan", "qk", "v", "gate", "up", "down", "mid", ("qk", "v", "gate", "up", "mid"), "qk", "v",
    ("qk", "v"), "small", "small", "qk", "v", ("qk", "v"), "gate", "up", ("small", "down"),
    "mid", ("mid",), "qk", "v", ("qk", "v"), "small", ("small",), "qk", "v", ("qk", "v"),
    "down", ("down",), "small", ("small",), "mid", "small", ("small",), "qk", "v", "small",
    ("small",), "down", "small",
)


def local(
    block_in, doc_starts, cotangent, norm1_gain, w_query, w_key, w_value, w_outgate, w_rank_down,
    w_rank_up, decay_bias, group_gain, w_output, norm2_gain, w_ffgate, w_ffup, w_ffdown,
):
    row_count, length, width = block_in.shape
    tokens = row_count * length
    kw, vw = w_query.shape[1], w_value.shape[1]
    links, turns = Links(), Turns()
    parts = links.n_seq
    everyone = links.n_dp * links.n_seq
    dims = (row_count, length, width, kw, vw, doc_starts.shape[1], parts)
    x = block_in.reshape(tokens, width)
    cot = cotangent.reshape(tokens, width)
    docs = (doc_starts - links.at_seq * length).reshape(-1)
    rank_down_t = w_rank_down.T

    levels = range(links.seq_bits - 1)
    step = 1 << len(levels)
    size = parts // step
    low = links.at_seq & (step - 1)
    turn = lambda p: sum(((p >> b) & 1) << (len(levels) - 1 - b) for b in levels)
    reverse = jnp.array([turn(p) for p in range(step)], jnp.int32)
    spread = jnp.arange(size)
    to_piece = ((reverse ^ low)[:, None] * size + spread).reshape(-1)
    to_place = ((reverse ^ turn(low))[:, None] * size + spread).reshape(-1)
    state_table = jnp.concatenate([to_piece, to_place]).astype(jnp.int32)

    normed, k, v, ra, gp, cum, keep_a, send_a, keep_b, send_b, decay = project_all(
        x, docs, state_table, norm1_gain, w_key, w_value, rank_down_t, w_rank_up, decay_bias, dims
    )
    decay = decay.reshape(1, row_count, HEADS, 1, kw // HEADS)
    fwd_a, fwd_b = {}, {}
    one = Task(scan_steps(
        links, turns, lambda: (keep_a, send_a, decay[:, :, : HEADS // 2]), None, False, fwd_a
    ))
    two = Task(scan_steps(
        links, turns, lambda: (keep_b, send_b, decay[:, :, HEADS // 2 :]), None, False, fwd_b
    ))
    one.advance(turns)
    start([one], turns)
    two.advance(turns)
    start([two], turns)
    one.advance(turns)
    start([one], turns)
    two.advance(turns)
    start([two], turns)
    dh = hidden_back_all(turns.after(cot), w_ffdown)
    turns.done(dh)
    one.advance(turns)
    start([one], turns)
    two.advance(turns)
    start([two], turns)
    q, og = readers_all(turns.after(normed), w_query, w_outgate)
    turns.done(q)
    one.advance(turns)
    start([one], turns)
    two.advance(turns)
    start([two], turns)
    inner = inner_all(q, k, v, cum, turns.after(docs), dims)
    turns.done(inner)
    while not two.over:
        one.advance(turns)
        start([one], turns)
        two.advance(turns)
        start([two], turns)
    decays = [
        tuple(jnp.concatenate(pair, axis=2) for pair in zip(*both))
        for both in zip(fwd_a["decays"], fwd_b["decays"])
    ]
    states = (fwd_a["near"], fwd_a["far"], fwd_b["near"], fwd_b["far"])
    mixed, gated, state_kept = mix_all(
        q, cum, inner, og, states, group_gain, turns.after(docs), state_table, dims
    )
    hidden, dg, du, normed2, middle = ff_all(
        x, gated, w_output, norm2_gain, w_ffgate, w_ffup, dh
    )
    turns.done(normed2)

    routes = {name: links.order(*route) for name, route in ROUTES.items()}
    tables = {route: links.table(route) for route in set(routes.values())}
    back, grads, held = {}, {}, {}
    ff = w_ffgate.shape[1]

    def ff_steps():
        out, d_middle, d_out, d_gated, gnorm2 = ff_back_all(
            hidden, dg, du, w_ffdown, w_ffgate, w_ffup, middle, turns.after(cot), w_output, norm2_gain
        )
        held.update(out=out, d_middle=d_middle, d_out=d_out, d_gated=d_gated, gnorm2=gnorm2)
        turns.done(d_out)
        return
        yield

    def head_back():
        d_mix, d_og, keep, send, ggroup = head_back_all(
            held["d_gated"], og, mixed, q, cum, group_gain, turns.after(docs), state_table, dims
        )
        held.update(d_mix=d_mix, d_og=d_og, ggroup=ggroup)
        return keep, send, None

    def local_steps():
        held["d_q"], held["own_k"], held["own_v"], held["decay"] = mix_local_all(
            q, k, v, cum, held["d_mix"], state_kept, turns.after(docs), dims
        )
        turns.done(held["d_q"])
        return
        yield

    def all_back():
        yield from scan_steps(links, turns, head_back, decays, True, back)
        held["d_k"], held["d_v"], held["d_rank"], held["grup"], held["gbias"] = mix_back_all(
            k, v, cum, gp, ra, state_kept, held["own_k"], held["own_v"], held["decay"], back["near"],
            back["far"], w_rank_up, turns.after(docs), state_table, dims,
        )
        turns.done(held["d_rank"])

    operands = {
        "gate": lambda: [(normed2, dg)],
        "up": lambda: [(normed2, du)],
        "down": lambda: [(hidden, cot)],
        "mid": lambda: [(gated, held["d_out"]), (normed, held["d_og"])],
        "qk": lambda: [(normed, held["d_q"]), (normed, held["d_k"])],
        "v": lambda: [(normed, held["d_v"])],
    }
    made = {}

    def weights(name, *names):
        def make():
            if name not in made:
                ordered = [tables[routes[each]] for each in names]
                ordered[0] = turns.after(ordered[0])
                groups = weight_grads([operands[each]() for each in names], ordered)
                made.update(zip(names, groups))
            return made[name]

        return reduce_steps(links, turns, make, routes[name], grads, name)

    def small_steps():
        grad_in, gnorm1 = input_back_all(
            x, held["d_middle"], held["d_q"], held["d_k"], held["d_v"], held["d_og"], held["d_rank"],
            turns.after(norm1_gain), w_query, w_key, w_value, w_outgate, rank_down_t,
        )
        held["grad_in"] = grad_in
        turns.done(gnorm1)
        yield []
        make = lambda: small_grads(
            normed, held["d_rank"], gnorm1, held["gnorm2"], held["grup"], held["gbias"],
            held["ggroup"], turns.after(tables[routes["small"]]),
        )
        yield from reduce_steps(links, turns, make, routes["small"], grads, "small")

    rank = w_rank_up.shape[0]
    work = {
        "ff": ff_steps(),
        "scan": all_back(),
        "gate": weights("gate", "gate", "up"),
        "up": weights("up", "gate", "up"),
        "down": weights("down", "down"),
        "mid": weights("mid", "mid"),
        "local": local_steps(),
        "qk": weights("qk", "qk", "v"),
        "v": weights("v", "qk", "v"),
        "small": small_steps(),
    }
    work = {name: Task(steps) for name, steps in work.items()}
    for name in SCHEDULE + tuple(work) * (2 * len(routes["gate"])):
        if isinstance(name, tuple):
            start([work[each] for each in name], turns)
            continue
        if name in ("scan", "mid", "local"):
            work["ff"].finish(turns)
        if name in ("qk", "v", "small"):
            work["local"].finish(turns)
            work["scan"].finish(turns)
        work[name].advance(turns)

    per, per_k = width // everyone, kw // everyone
    small = grads["small"][0]
    first, second, third = small[:per], small[per : per + per_k], small[per + per_k :]
    mid, qk = grads["mid"][0], grads["qk"][0]
    return (
        held["out"].reshape(row_count, length, width),
        held["grad_in"].reshape(row_count, length, width),
        first[:, rank],
        qk[:per],
        qk[per:],
        grads["v"][0],
        mid[per:],
        first[:, :rank],
        second[:, :rank].T,
        second[:, rank],
        third[:, 0],
        mid[:per],
        first[:, rank + 1],
        grads["gate"][0],
        grads["up"][0],
        grads["down"][0],
    )


def solution(mesh):
    tokens = P("dp", "seq", None)
    rows = P(("dp", "seq"), None)
    vector = P(("dp", "seq"))
    return jax.shard_map(
        local,
        mesh=mesh,
        in_specs=(tokens, P("dp", None), tokens) + (P(),) * 14,
        out_specs=(
            tokens, tokens, vector, rows, rows, rows, rows, rows, P(None, ("dp", "seq")), vector,
            vector, rows, vector, rows, rows, rows,
        ),
        check_vma=False,
    )
```

```python
import functools

import jax
import jax.numpy as jnp
from jax import lax
from jax.experimental import pallas as pl
from jax.experimental.pallas import tpu as pltpu
from jax.sharding import PartitionSpec as P

HEADS = 4
EPS = 1e-06
MIB = 1 << 20
BF = jnp.bfloat16
F32 = jnp.float32
HIGHEST = lax.Precision.HIGHEST


def nn(a, b, precision=None):
    return lax.dot_general(
        a, b, (((1,), (0,)), ((), ())), precision=precision, preferred_element_type=F32
    )


def nt(a, b):
    return lax.dot_general(a, b, (((1,), (1,)), ((), ())), preferred_element_type=F32)


def tn(a, b):
    return lax.dot_general(a, b, (((0,), (0,)), ((), ())), preferred_element_type=F32)


def shape(dims, dtype):
    return jax.ShapeDtypeStruct(dims, dtype)


def call(body, out_shape, grid, in_specs, out_specs, prefetch=0, scratch=(), room=60):
    return pl.pallas_call(
        body,
        out_shape=out_shape,
        grid_spec=pltpu.PrefetchScalarGridSpec(
            num_scalar_prefetch=prefetch,
            grid=grid,
            in_specs=in_specs,
            out_specs=out_specs,
            scratch_shapes=list(scratch),
        ),
        compiler_params=pltpu.CompilerParams(vmem_limit_bytes=room * MIB),
        cost_estimate=pl.CostEstimate(flops=1, bytes_accessed=1, transcendentals=0),
    )


def block(dims, index):
    return pl.BlockSpec(dims, index)


def whole(dims):
    zero = (0,) * len(dims)
    return pl.BlockSpec(dims, lambda *_: zero)


def reset_masks(docs_ref, row, docs, length):
    at_i = lax.broadcasted_iota(jnp.int32, (length, length), 0)
    at_j = lax.broadcasted_iota(jnp.int32, (length, length), 1)
    token = lax.broadcasted_iota(jnp.int32, (length, 1), 0)
    visible = at_i >= at_j
    alive = token >= 0
    tail = token >= 0
    whole_alive = jnp.float32(1.0)
    for n in range(docs):
        start = docs_ref[row * docs + n]
        visible = visible & jnp.logical_not((at_j < start) & (start <= at_i))
        inside = (start >= 0) & (start < length)
        first = jnp.where(start >= 0, start, length)
        alive = alive & (token < first)
        last = jnp.where(start < length, start, -1)
        tail = tail & (token >= last)
        whole_alive = whole_alive * jnp.where(inside, 0.0, 1.0)
    return visible, alive.astype(F32), tail.astype(F32), whole_alive


def lower_ones(length, strict=False):
    at_i = lax.broadcasted_iota(jnp.int32, (length, length), 0)
    at_j = lax.broadcasted_iota(jnp.int32, (length, length), 1)
    return (at_i > at_j if strict else at_i >= at_j).astype(F32)


def project_body(
    rows, docs, length, hk, hv, parts,
    docs_ref, table_ref, x_ref, gain_ref, wk_ref, wv_ref, wrd_ref, wru_ref, bias_ref,
    normed_ref, k_ref, v_ref, ra_ref, gp_ref, cum_ref, keep_a_ref, send_a_ref, keep_b_ref,
    send_b_ref, decay_ref,
    hold,
):
    x = x_ref[...].astype(F32)
    inv = lax.rsqrt(jnp.mean(x * x, axis=-1, keepdims=True) + EPS)
    normed = (x * inv * gain_ref[...]).astype(BF)
    normed_ref[...] = normed
    rank = nt(normed, wrd_ref[...]).astype(BF)
    ra_ref[...] = rank
    gate = nn(rank, wru_ref[...]) + bias_ref[...]
    gp_ref[...] = gate
    key = nn(normed, wk_ref[...]).astype(BF)
    k_ref[...] = key
    value = nn(normed, wv_ref[...]).astype(BF)
    v_ref[...] = value
    log_decay = (jnp.minimum(gate, 0.0) - jnp.log1p(jnp.exp(-jnp.abs(gate)))) * (1.0 / 16.0)
    tri = lower_ones(length)
    size = hv // parts
    for r in range(rows):
        at = slice(r * length, (r + 1) * length)
        row = pl.program_id(0) * rows + r
        cum = nn(tri, log_decay[at], HIGHEST)
        cum_ref[at, :] = cum
        _, _, tail, whole_alive = reset_masks(docs_ref, row, docs, length)
        last = cum[length - 1 :, :]
        decay_ref[r] = jnp.exp(last) * whole_alive
        weighted = (key[at].astype(F32) * jnp.exp(last - cum) * tail).astype(BF)
        for h in range(HEADS):
            hold[...] = tn(value[at, h * hv : (h + 1) * hv], weighted[:, h * hk : (h + 1) * hk])
            keep_ref, send_ref = (keep_a_ref, send_a_ref) if h < HEADS // 2 else (keep_b_ref, send_b_ref)
            for j in range(parts // 2):
                first = pl.multiple_of(table_ref[j] * size, size)
                keep_ref[j, r, h % (HEADS // 2)] = hold[pl.ds(first, size), :]
                second = pl.multiple_of(table_ref[parts // 2 + j] * size, size)
                send_ref[j, r, h % (HEADS // 2)] = hold[pl.ds(second, size), :]


def project_all(x, docs, table, gain, wk, wv, wrd, wru, bias, dims):
    row_count, length, width, kw, vw, ndocs, parts = dims
    tokens = row_count * length
    rows = 2 if row_count % 2 == 0 else 1
    tm = rows * length
    hk, hv = kw // HEADS, vw // HEADS
    rank = wrd.shape[0]
    size = hv // parts
    tile = lambda n: block((tm, n), lambda i, *_: (i, 0))
    half = (parts // 2, row_count, HEADS // 2, size, hk)
    half_block = block((parts // 2, rows, HEADS // 2, size, hk), lambda i, *_: (0, i, 0, 0, 0))
    body = functools.partial(project_body, rows, ndocs, length, hk, hv, parts)
    return call(
        body,
        (
            shape((tokens, width), BF),
            shape((tokens, kw), BF),
            shape((tokens, vw), BF),
            shape((tokens, rank), BF),
            shape((tokens, kw), F32),
            shape((tokens, kw), F32),
            shape(half, F32),
            shape(half, F32),
            shape(half, F32),
            shape(half, F32),
            shape((row_count, 1, kw), F32),
        ),
        (row_count // rows,),
        [
            tile(width), whole((1, width)), whole(wk.shape), whole(wv.shape), whole(wrd.shape),
            whole(wru.shape), whole((1, kw)),
        ],
        (
            tile(width), tile(kw), tile(vw), tile(rank), tile(kw), tile(kw),
            half_block, half_block, half_block, half_block,
            block((rows, 1, kw), lambda i, *_: (i, 0, 0)),
        ),
        prefetch=2,
        scratch=[pltpu.VMEM((hv, hk), F32)],
    )(docs, table, x, gain.reshape(1, -1), wk, wv, wrd, wru, bias.reshape(1, -1))


def readers_body(normed_ref, wq_ref, wog_ref, q_ref, og_ref):
    q_ref[...] = nn(normed_ref[...], wq_ref[...]).astype(BF)
    og_ref[...] = nn(normed_ref[...], wog_ref[...])


def readers_all(normed, wq, wog):
    tokens, width = normed.shape
    tm = 256 if tokens % 256 == 0 else 128
    tile = lambda n: block((tm, n), lambda i: (i, 0))
    return call(
        readers_body,
        (shape((tokens, wq.shape[1]), BF), shape((tokens, wog.shape[1]), F32)),
        (tokens // tm,),
        [tile(width), whole(wq.shape), whole(wog.shape)],
        (tile(wq.shape[1]), tile(wog.shape[1])),
    )(normed, wq, wog)


def span_factors(cum, length):
    middle = cum[length // 2 - 1 : length // 2, :]
    return jnp.exp(cum - middle), jnp.exp(middle - cum)


def inner_body(docs, length, hk, hv, docs_ref, q_ref, k_ref, v_ref, cum_ref, inner_ref):
    visible, _, _, _ = reset_masks(docs_ref, pl.program_id(0), docs, length)
    up, down = span_factors(cum_ref[...], length)
    q = (q_ref[...].astype(F32) * up).astype(BF)
    k = (k_ref[...].astype(F32) * down).astype(BF)
    for h in range(HEADS):
        kk = slice(h * hk, (h + 1) * hk)
        vv = slice(h * hv, (h + 1) * hv)
        scores = jnp.where(visible, nt(q[:, kk], k[:, kk]), 0.0).astype(BF)
        inner_ref[:, vv] = nn(scores, v_ref[:, vv])


def inner_all(q, k, v, cum, docs, dims):
    row_count, length, width, kw, vw, ndocs, parts = dims
    tokens = row_count * length
    tile = lambda n: block((length, n), lambda i, *_: (i, 0))
    return call(
        functools.partial(inner_body, ndocs, length, kw // HEADS, vw // HEADS),
        shape((tokens, vw), F32),
        (row_count,),
        [tile(kw), tile(kw), tile(vw), tile(kw)],
        tile(vw),
        prefetch=1,
    )(docs, q, k, v, cum)


def gather_state(near_ref, far_ref, table_ref, h, parts):
    half = parts // 2
    pieces = []
    for p in range(parts):
        place = table_ref[parts + p]
        near = near_ref[jnp.minimum(place, half - 1), 0, h]
        far = far_ref[jnp.maximum(place - half, 0), 0, h]
        pieces.append(jnp.where(place < half, near, far))
    return jnp.concatenate(pieces, axis=0)


def mix_body(
    docs, length, hk, hv, parts,
    docs_ref, table_ref, q_ref, cum_ref, inner_ref, og_ref, near_a_ref, far_a_ref, near_b_ref, far_b_ref,
    gain_ref,
    mixed_ref, gated_ref, kept_ref,
):
    _, alive, _, _ = reset_masks(docs_ref, pl.program_id(0), docs, length)
    reach = (q_ref[...].astype(F32) * jnp.exp(cum_ref[...]) * alive).astype(BF)
    scale = hk ** (-0.5)
    for h in range(HEADS):
        kk = slice(h * hk, (h + 1) * hk)
        vv = slice(h * hv, (h + 1) * hv)
        near_ref, far_ref = (near_a_ref, far_a_ref) if h < HEADS // 2 else (near_b_ref, far_b_ref)
        state = gather_state(near_ref, far_ref, table_ref, h % (HEADS // 2), parts).astype(BF)
        kept_ref[0, h] = state
        mixed = scale * (inner_ref[:, vv] + nt(reach[:, kk], state))
        mixed_ref[:, vv] = mixed
        inv = lax.rsqrt(jnp.mean(mixed * mixed, axis=-1, keepdims=True) + EPS)
        og = og_ref[:, vv]
        gated_ref[:, vv] = (mixed * inv * gain_ref[...] * og * jax.nn.sigmoid(og)).astype(BF)


def mix_all(q, cum, inner, og, states, gain, docs, table, dims):
    row_count, length, width, kw, vw, ndocs, parts = dims
    tokens = row_count * length
    hk, hv = kw // HEADS, vw // HEADS
    tile = lambda n: block((length, n), lambda i, *_: (i, 0))
    half = block((parts // 2, 1, HEADS // 2, hv // parts, hk), lambda i, *_: (0, i, 0, 0, 0))
    return call(
        functools.partial(mix_body, ndocs, length, hk, hv, parts),
        (
            shape((tokens, vw), F32),
            shape((tokens, vw), BF),
            shape((row_count, HEADS, hv, hk), BF),
        ),
        (row_count,),
        [
            tile(kw), tile(kw), tile(vw), tile(vw), half, half, half, half, whole((1, hv)),
        ],
        (tile(vw), tile(vw), block((1, HEADS, hv, hk), lambda i, *_: (i, 0, 0, 0))),
        prefetch=2,
    )(docs, table, q, cum, inner, og, *states, gain.reshape(1, -1))


def hidden_back_body(cot_ref, wd_ref, dh_ref):
    dh_ref[...] = nt(cot_ref[...], wd_ref[...])


def hidden_back_all(cot, wd):
    tokens, width = cot.shape
    ff, tile = wd.shape[0], 256
    return call(
        hidden_back_body,
        shape((tokens, ff), F32),
        (ff // tile,),
        [whole((tokens, width)), block((tile, width), lambda i: (i, 0))],
        block((tokens, tile), lambda i: (0, i)),
    )(cot, wd)


def ff_body(
    x_ref, gated_ref, wo_ref, gain_ref, wg_ref, wu_ref, dh_ref,
    hidden_ref, dg_ref, du_ref, normed2_ref, middle_ref,
):
    @pl.when(pl.program_id(0) == 0)
    def _():
        mid = x_ref[...].astype(F32) + nn(gated_ref[...], wo_ref[...])
        middle_ref[...] = mid
        inv = lax.rsqrt(jnp.mean(mid * mid, axis=-1, keepdims=True) + EPS)
        normed2_ref[...] = (mid * inv * gain_ref[...]).astype(BF)

    normed2 = normed2_ref[...]
    gate = nn(normed2, wg_ref[...])
    up = nn(normed2, wu_ref[...])
    d_hidden = dh_ref[...]
    sig = jax.nn.sigmoid(gate)
    act = gate * sig
    hidden_ref[...] = (act * up).astype(BF)
    dg_ref[...] = (d_hidden * up * sig * (1.0 + gate * (1.0 - sig))).astype(BF)
    du_ref[...] = (d_hidden * act).astype(BF)


def ff_all(x, gated, wo, gain, wg, wu, dh):
    tokens, width = x.shape
    ff = wg.shape[1]
    tile = 256
    col = lambda n: block((n, tile), lambda i: (0, i))
    once = lambda dims: pl.BlockSpec(dims, lambda i: (0, 0), pipeline_mode=pl.Buffered(1))
    return call(
        ff_body,
        (
            shape((tokens, ff), BF), shape((tokens, ff), BF), shape((tokens, ff), BF),
            shape((tokens, width), BF), shape((tokens, width), F32),
        ),
        (ff // tile,),
        [
            once((tokens, width)), once(gated.shape), once(wo.shape), once((1, width)),
            col(width), col(width), col(tokens),
        ],
        (
            col(tokens), col(tokens), col(tokens), whole((tokens, width)), whole((tokens, width)),
        ),
    )(x, gated, wo, gain.reshape(1, -1), wg, wu, dh)


def ff_back_body(
    steps,
    hidden_ref, dg_ref, du_ref, wd_ref, wg_ref, wu_ref, middle_ref, cot_ref, wo_ref, gain_ref,
    out_ref, dmid_ref, dout_ref, dgated_ref, gnorm_ref,
):
    total, back = dgated_ref, dmid_ref
    step = pl.program_id(0)
    tokens = middle_ref.shape[0]
    rows = 256 if tokens % 256 == 0 else tokens
    for first in range(0, tokens, rows):
        at = slice(first, first + rows)
        more = nn(hidden_ref[at, :], wd_ref[...])
        more_back = nt(dg_ref[at, :], wg_ref[...]) + nt(du_ref[at, :], wu_ref[...])

        @pl.when(step == 0)
        def _(at=at, more=more, more_back=more_back):
            total[at, :] = more
            back[at, :] = more_back

        @pl.when(step > 0)
        def _(at=at, more=more, more_back=more_back):
            total[at, :] += more
            back[at, :] += more_back

    @pl.when(step == steps - 1)
    def _():
        gnorm = jnp.zeros((1, middle_ref.shape[1]), F32)
        for first in range(0, tokens, rows):
            at = slice(first, first + rows)
            mid = middle_ref[at, :]
            out_ref[at, :] = (mid + total[at, :]).astype(BF)
            inv = lax.rsqrt(jnp.mean(mid * mid, axis=-1, keepdims=True) + EPS)
            d_normed2 = back[at, :]
            gnorm = gnorm + jnp.sum(d_normed2 * mid * inv, axis=0, keepdims=True)
            scaled = d_normed2 * gain_ref[...]
            d_middle = (
                cot_ref[at, :].astype(F32)
                + inv * scaled
                - mid * (inv * inv * inv) * jnp.mean(scaled * mid, axis=-1, keepdims=True)
            )
            dmid_ref[at, :] = d_middle
            d_out = d_middle.astype(BF)
            dout_ref[at, :] = d_out
            dgated_ref[at, :] = nt(d_out, wo_ref[...])
        gnorm_ref[...] = gnorm


def ff_back_all(hidden, dg, du, wd, wg, wu, middle, cot, wo, gain):
    tokens, width = middle.shape
    vw, ff = wo.shape[0], wg.shape[1]
    tile = 1408 if ff % 1408 == 0 else 256
    steps = ff // tile
    col = lambda n: block((n, tile), lambda i: (0, i))
    once = lambda dims: pl.BlockSpec(dims, lambda i: (0, 0), pipeline_mode=pl.Buffered(1))
    return call(
        functools.partial(ff_back_body, steps),
        (
            shape((tokens, width), BF), shape((tokens, width), F32), shape((tokens, width), BF),
            shape((tokens, vw), F32), shape((1, width), F32),
        ),
        (steps,),
        [
            col(tokens), col(tokens), col(tokens), block((tile, width), lambda i: (i, 0)),
            col(width), col(width), once((tokens, width)), once((tokens, width)), once(wo.shape),
            once((1, width)),
        ],
        (
            whole((tokens, width)), whole((tokens, width)), whole((tokens, width)),
            whole((tokens, vw)), whole((1, width)),
        ),
    )(hidden, dg, du, wd, wg, wu, middle, cot, wo, gain.reshape(1, -1))


def head_back_body(
    docs, length, hk, hv, parts,
    docs_ref, table_ref, dgated_ref, og_ref, mixed_ref, q_ref, cum_ref, gain_ref,
    dmix_ref, dog_ref, keep_ref, send_ref, ggroup_ref,
    hold,
):
    row = pl.program_id(0)
    _, alive, _, _ = reset_masks(docs_ref, row, docs, length)
    reach = (q_ref[...].astype(F32) * jnp.exp(cum_ref[...]) * alive).astype(BF)
    scale = hk ** (-0.5)
    size = hv // parts
    ggroup = jnp.zeros((1, hv), F32)
    for h in range(HEADS):
        kk = slice(h * hk, (h + 1) * hk)
        vv = slice(h * hv, (h + 1) * hv)
        mixed = mixed_ref[:, vv]
        inv = lax.rsqrt(jnp.mean(mixed * mixed, axis=-1, keepdims=True) + EPS)
        og = og_ref[:, vv]
        sig = jax.nn.sigmoid(og)
        dgated = dgated_ref[:, vv]
        unit = mixed * inv
        dog_ref[:, vv] = (
            dgated * unit * gain_ref[...] * sig * (1.0 + og * (1.0 - sig))
        ).astype(BF)
        d_heads = dgated * og * sig
        ggroup = ggroup + jnp.sum(d_heads * unit, axis=0, keepdims=True)
        scaled = d_heads * gain_ref[...]
        d_mixed = inv * scaled - mixed * (inv * inv * inv) * jnp.mean(
            scaled * mixed, axis=-1, keepdims=True
        )
        d_mixed = (scale * d_mixed).astype(BF)
        dmix_ref[:, vv] = d_mixed
        hold[...] = tn(d_mixed, reach[:, kk])
        for j in range(parts // 2):
            first = pl.multiple_of(table_ref[j] * size, size)
            keep_ref[j, 0, h] = hold[pl.ds(first, size), :]
            second = pl.multiple_of(table_ref[parts // 2 + j] * size, size)
            send_ref[j, 0, h] = hold[pl.ds(second, size), :]

    @pl.when(row == 0)
    def _():
        ggroup_ref[...] = ggroup

    @pl.when(row > 0)
    def _():
        ggroup_ref[...] += ggroup


def head_back_all(dgated, og, mixed, q, cum, gain, docs, table, dims):
    row_count, length, width, kw, vw, ndocs, parts = dims
    tokens = row_count * length
    hk, hv = kw // HEADS, vw // HEADS
    size = hv // parts
    tile = lambda n: block((length, n), lambda i, *_: (i, 0))
    half = (parts // 2, row_count, HEADS, size, hk)
    half_block = block((parts // 2, 1, HEADS, size, hk), lambda i, *_: (0, i, 0, 0, 0))
    return call(
        functools.partial(head_back_body, ndocs, length, hk, hv, parts),
        (
            shape((tokens, vw), BF), shape((tokens, vw), BF),
            shape(half, F32), shape(half, F32), shape((1, hv), F32),
        ),
        (row_count,),
        [tile(vw), tile(vw), tile(vw), tile(kw), tile(kw), whole((1, hv))],
        (tile(vw), tile(vw), half_block, half_block, whole((1, hv))),
        prefetch=2,
        scratch=[pltpu.VMEM((hv, hk), F32)],
    )(docs, table, dgated, og, mixed, q, cum, gain.reshape(1, -1))


def mix_local_body(
    docs, length, hk, hv,
    docs_ref, q_ref, k_ref, v_ref, cum_ref, dmix_ref, state_ref,
    dq_ref, dk_ref, dv_ref, decay_ref,
):
    visible, alive, _, _ = reset_masks(docs_ref, pl.program_id(0), docs, length)
    cum = cum_ref[...]
    up, down = span_factors(cum, length)
    from_start = jnp.exp(cum) * alive
    q = q_ref[...].astype(F32)
    q_span = (q * up).astype(BF)
    k_span = (k_ref[...].astype(F32) * down).astype(BF)
    reach = (q * from_start).astype(BF)
    later = []
    for h in range(HEADS):
        kk = slice(h * hk, (h + 1) * hk)
        vv = slice(h * hv, (h + 1) * hv)
        qs, ks = q_span[:, kk], k_span[:, kk]
        d_mix = dmix_ref[:, vv]
        scores = jnp.where(visible, nt(qs, ks), 0.0).astype(BF)
        d_scores = jnp.where(visible, nt(d_mix, v_ref[:, vv]), 0.0).astype(BF)
        dq_in = nn(d_scores, ks)
        dk_in = tn(d_scores, qs)
        dq_out = nn(d_mix, state_ref[0, h])
        dq_ref[:, kk] = (dq_in * up[:, kk] + dq_out * from_start[:, kk]).astype(BF)
        dk_ref[:, kk] = dk_in * down[:, kk]
        dv_ref[:, vv] = tn(scores, d_mix)
        later.append(
            qs.astype(F32) * dq_in - ks.astype(F32) * dk_in + reach[:, kk].astype(F32) * dq_out
        )
    at_i = lax.broadcasted_iota(jnp.int32, (length, length), 0)
    at_j = lax.broadcasted_iota(jnp.int32, (length, length), 1)
    decay_ref[...] = nn((at_i <= at_j).astype(F32), jnp.concatenate(later, axis=1), HIGHEST)


def mix_local_all(q, k, v, cum, dmix, state, docs, dims):
    row_count, length, width, kw, vw, ndocs, parts = dims
    tokens = row_count * length
    hk, hv = kw // HEADS, vw // HEADS
    tile = lambda n: block((length, n), lambda i, *_: (i, 0))
    return call(
        functools.partial(mix_local_body, ndocs, length, hk, hv),
        (
            shape((tokens, kw), BF), shape((tokens, kw), F32), shape((tokens, vw), F32),
            shape((tokens, kw), F32),
        ),
        (row_count,),
        [
            tile(kw), tile(kw), tile(vw), tile(kw), tile(vw),
            block((1, HEADS, hv, hk), lambda i, *_: (i, 0, 0, 0)),
        ],
        (tile(kw), tile(kw), tile(vw), tile(kw)),
        prefetch=1,
        room=28,
    )(docs, q, k, v, cum, dmix, state)


def mix_back_body(
    docs, length, hk, hv, parts,
    docs_ref, table_ref, k_ref, v_ref, cum_ref, gp_ref, ra_ref, state_ref, dk_ref, dv_ref, decay_ref,
    near_ref, far_ref, wru_ref,
    dk_out_ref, dv_out_ref, drank_ref, grup_ref, gbias_ref,
):
    row = pl.program_id(0)
    _, _, tail, whole_alive = reset_masks(docs_ref, row, docs, length)
    cum = cum_ref[...]
    last = cum[length - 1 :, :]
    to_end = jnp.exp(last - cum) * tail
    weighted = (k_ref[...].astype(F32) * to_end).astype(BF)
    earlier, crossing = [], []
    for h in range(HEADS):
        kk = slice(h * hk, (h + 1) * hk)
        vv = slice(h * hv, (h + 1) * hv)
        grad32 = gather_state(near_ref, far_ref, table_ref, h, parts)
        grad = grad32.astype(BF)
        dk_out = nn(v_ref[:, vv], grad)
        dk_out_ref[:, kk] = (dk_ref[:, kk] + dk_out * to_end[:, kk]).astype(BF)
        dv_out_ref[:, vv] = (
            dv_ref[:, vv] + nt(weighted[:, kk], grad)
        ).astype(BF)
        earlier.append(weighted[:, kk].astype(F32) * dk_out)
        crossing.append(jnp.sum(state_ref[0, h].astype(F32) * grad32, axis=0, keepdims=True))
    d_decay = (
        decay_ref[...]
        + nn(lower_ones(length, True), jnp.concatenate(earlier, axis=1), HIGHEST)
        + jnp.exp(last) * whole_alive * jnp.concatenate(crossing, axis=1)
    )
    d_gate = (d_decay * jax.nn.sigmoid(-gp_ref[...]) * (1.0 / 16.0)).astype(BF)
    drank_ref[...] = nt(d_gate, wru_ref[...]).astype(BF)
    grup = tn(ra_ref[...], d_gate)
    gbias = jnp.sum(d_gate.astype(F32), axis=0, keepdims=True)

    @pl.when(row == 0)
    def _():
        grup_ref[...] = grup
        gbias_ref[...] = gbias

    @pl.when(row > 0)
    def _():
        grup_ref[...] += grup
        gbias_ref[...] += gbias


def mix_back_all(k, v, cum, gp, ra, state, dk, dv, decay, near, far, wru, docs, table, dims):
    row_count, length, width, kw, vw, ndocs, parts = dims
    tokens = row_count * length
    hk, hv = kw // HEADS, vw // HEADS
    rank = wru.shape[0]
    tile = lambda n: block((length, n), lambda i, *_: (i, 0))
    half = block((parts // 2, 1, HEADS, hv // parts, hk), lambda i, *_: (0, i, 0, 0, 0))
    return call(
        functools.partial(mix_back_body, ndocs, length, hk, hv, parts),
        (
            shape((tokens, kw), BF), shape((tokens, vw), BF), shape((tokens, rank), BF),
            shape((rank, kw), F32), shape((1, kw), F32),
        ),
        (row_count,),
        [
            tile(kw), tile(vw), tile(kw), tile(kw), tile(rank),
            block((1, HEADS, hv, hk), lambda i, *_: (i, 0, 0, 0)),
            tile(kw), tile(vw), tile(kw), half, half, whole((rank, kw)),
        ],
        (tile(kw), tile(vw), tile(rank), whole((rank, kw)), whole((1, kw))),
        prefetch=2,
        room=28,
    )(docs, table, k, v, cum, gp, ra, state, dk, dv, decay, near, far, wru)


def input_back_body(
    x_ref, dmid_ref, dq_ref, dk_ref, dv_ref, dog_ref, drank_ref, gain_ref, wq_ref, wk_ref, wv_ref, wog_ref, wrd_ref,
    gin_ref, gnorm_ref,
):
    step = pl.program_id(0)
    d_normed = (
        nt(dq_ref[...], wq_ref[...])
        + nt(dk_ref[...], wk_ref[...])
        + nt(dv_ref[...], wv_ref[...])
        + nt(dog_ref[...], wog_ref[...])
        + nn(drank_ref[...], wrd_ref[...])
    )
    x = x_ref[...].astype(F32)
    inv = lax.rsqrt(jnp.mean(x * x, axis=-1, keepdims=True) + EPS)
    gnorm = jnp.sum(d_normed * x * inv, axis=0, keepdims=True)
    scaled = d_normed * gain_ref[...]
    gin_ref[...] = (
        dmid_ref[...]
        + inv * scaled
        - x * (inv * inv * inv) * jnp.mean(scaled * x, axis=-1, keepdims=True)
    )

    @pl.when(step == 0)
    def _():
        gnorm_ref[...] = gnorm

    @pl.when(step > 0)
    def _():
        gnorm_ref[...] += gnorm


def input_back_all(x, dmid, dq, dk, dv, dog, drank, gain, wq, wk, wv, wog, wrd):
    tokens, width = x.shape
    kw, vw = wq.shape[1], wv.shape[1]
    tm = 256 if tokens % 256 == 0 else 128
    tile = lambda n: block((tm, n), lambda i: (i, 0))
    return call(
        input_back_body,
        (shape((tokens, width), F32), shape((1, width), F32)),
        (tokens // tm,),
        [
            tile(width), tile(width), tile(kw), tile(kw), tile(vw), tile(vw), tile(drank.shape[1]),
            whole((1, width)), whole(wq.shape), whole(wk.shape), whole(wv.shape), whole(wog.shape),
            whole(wrd.shape),
        ],
        (tile(width), whole((1, width))),
        room=28,
    )(x, dmid, dq, dk, dv, dog, drank, gain.reshape(1, -1), wq, wk, wv, wog, wrd)


def weight_body(groups, lefts, pieces, *refs):
    tables = refs[: len(groups)]
    refs = refs[len(groups) :]
    left_refs, refs = refs[:lefts], refs[lefts:]
    count = sum(len(group) for group in groups)
    rights, refs = refs[:count], refs[count:]
    outs, refs = refs[: 2 * len(groups)], refs[2 * len(groups) :]
    turned, holds = refs[:lefts], refs[lefts:]

    @pl.when(pl.program_id(0) == 0)
    def _():
        for n in range(lefts):
            turned[n][...] = left_refs[n][...].T

    at = 0
    for g, group in enumerate(groups):
        keep_ref, send_ref = outs[2 * g], outs[2 * g + 1]
        place = 0
        for left in group:
            hold = holds[g]
            hold[...] = nn(turned[left][...], rights[at][...])
            per = hold.shape[0] // pieces
            rows = slice(place, place + per)
            for j in range(pieces // 2):
                first = pl.multiple_of(tables[g][j] * per, per)
                keep_ref[j, rows, :] = hold[pl.ds(first, per), :]
                second = pl.multiple_of(tables[g][pieces // 2 + j] * per, per)
                send_ref[j, rows, :] = hold[pl.ds(second, per), :]
            at, place = at + 1, place + per


def weight_grads(groups, tables, room, steps=2):
    pieces = tables[0].shape[0]
    tokens = groups[0][0][0].shape[0]
    out = []
    if any(left.shape[1] // pieces % 8 for group in groups for left, _ in group):
        for group, table in zip(groups, tables):
            parts = [tn(left, right) for left, right in group]
            parts = [part.reshape(pieces, -1, part.shape[1]) for part in parts]
            parts = jnp.concatenate(parts, axis=1)[table]
            out.append((parts[: pieces // 2], parts[pieces // 2 :]))
        return out
    lefts, index = [], []
    for group in groups:
        index.append([])
        for left, _ in group:
            known = [n for n, other in enumerate(lefts) if other is left]
            if not known:
                lefts.append(left)
            index[-1].append(known[0] if known else len(lefts) - 1)
    rights = [right for group in groups for _, right in group]
    column = lambda n: block((tokens, n // steps), lambda i, *_: (0, i))
    shapes, blocks, holds = [], [], []
    for group in groups:
        rows, cols = group[0][0].shape[1], group[0][1].shape[1]
        dims = (pieces // 2, len(group) * rows // pieces, cols)
        shapes += [shape(dims, F32)] * 2
        blocks += [block(dims[:2] + (cols // steps,), lambda i, *_: (0, 0, i))] * 2
        holds.append(pltpu.VMEM((rows, cols // steps), F32))
    flat = call(
        functools.partial(weight_body, index, len(lefts), pieces),
        tuple(shapes),
        (steps,),
        [whole(left.shape) for left in lefts] + [column(right.shape[1]) for right in rights],
        tuple(blocks),
        prefetch=len(groups),
        scratch=[pltpu.VMEM(left.shape[::-1], BF) for left in lefts] + holds,
        room=room,
    )(*tables, *lefts, *rights)
    return [(flat[2 * g], flat[2 * g + 1]) for g in range(len(groups))]


def small_body(
    pieces,
    table_ref, normed_ref, drank_ref, gnorm1_ref, gnorm2_ref, grup_ref, gbias_ref, ggroup_ref,
    keep_ref, send_ref,
    hold,
):
    width, kw, hv = gnorm1_ref.shape[1], gbias_ref.shape[1], ggroup_ref.shape[1]
    rank = grup_ref.shape[0]

    def stand(rows):
        have = sum(row.shape[0] for row in rows)
        return jnp.concatenate(rows + [jnp.zeros((128 - have, rows[0].shape[1]), F32)], axis=0).T

    spread = jnp.zeros((normed_ref.shape[0], 128 - rank), BF)
    hold[:width, :] = tn(normed_ref[...], jnp.concatenate([drank_ref[...], spread], axis=1)) + stand(
        [jnp.zeros((rank, width), F32), gnorm1_ref[...], gnorm2_ref[...]]
    )
    hold[width : width + kw, :] = stand([grup_ref[...], gbias_ref[...]])
    hold[width + kw :, :] = stand([ggroup_ref[...]])
    first, place = 0, 0
    for rows in (width, kw, hv):
        per = rows // pieces
        for j in range(pieces // 2):
            keep = pl.multiple_of(first + table_ref[j] * per, per)
            keep_ref[j, place : place + per, :] = hold[pl.ds(keep, per), :]
            send = pl.multiple_of(first + table_ref[pieces // 2 + j] * per, per)
            send_ref[j, place : place + per, :] = hold[pl.ds(send, per), :]
        first, place = first + rows, place + per


def small_grads(normed, drank, gnorm1, gnorm2, grup, gbias, ggroup, table):
    pieces, rank = table.shape[0], grup.shape[0]
    width, kw, hv = gnorm1.shape[1], gbias.shape[1], ggroup.shape[1]
    rows = (width + kw + hv) // pieces
    if hv // pieces % 8:
        wide = lambda value: jnp.pad(value, ((0, 0), (0, 128 - value.shape[1])))
        cut = lambda value: wide(value).reshape(pieces, -1, 128)
        both = jnp.concatenate(
            [
                cut(jnp.concatenate([tn(normed, drank), gnorm1.T, gnorm2.T], axis=1)),
                cut(jnp.concatenate([grup.T, gbias.T], axis=1)),
                cut(ggroup.T),
            ],
            axis=1,
        )[table]
        return both[: pieces // 2], both[pieces // 2 :]
    half = shape((pieces // 2, rows, 128), F32)
    operands = (normed, drank, gnorm1, gnorm2, grup, gbias, ggroup)
    return call(
        functools.partial(small_body, pieces),
        (half, half),
        (1,),
        [whole(value.shape) for value in operands],
        (whole(half.shape), whole(half.shape)),
        prefetch=1,
        scratch=[pltpu.VMEM((width + kw + hv, 128), F32)],
        room=16,
    )(table, *operands)


def bits_of(n):
    return n.bit_length() - 1


class Links:
    def __init__(self):
        self.n_dp, self.n_seq = lax.axis_size("dp"), lax.axis_size("seq")
        self.seq_bits, self.dp_bits = bits_of(self.n_seq), bits_of(self.n_dp)
        self.at_seq = lax.axis_index("seq")
        self.me = lax.axis_index("dp") * self.n_seq + self.at_seq

    def swap(self, value, bit):
        name, n, flip = "seq", self.n_seq, 1 << bit
        if bit >= self.seq_bits:
            name, n, flip = "dp", self.n_dp, 1 << (bit - self.seq_bits)
        return lax.ppermute(value, name, [(i, i ^ flip) for i in range(n)])

    def table(self, order):
        n = 1 << len(order)
        places = [
            sum(((at >> (len(order) - 1 - k)) & 1) << bit for k, bit in enumerate(order))
            for at in range(n)
        ]
        here = self.me if n == self.n_dp * self.n_seq else self.at_seq
        return jnp.array(places, jnp.int32) ^ here

    def order(self, *names):
        across = tuple(range(self.seq_bits, self.seq_bits + self.dp_bits))
        bits = [0]
        for name in names:
            bits.extend(across if name == "x" else [{"y": 1, "z0": 2, "z1": 3}[name]])
        return tuple(bits) + tuple(b for b in range(self.seq_bits) if b not in bits)


class Turns:
    def __init__(self):
        self.last = ()

    def after(self, value):
        return lax.optimization_barrier((value,) + self.last)[0]

    def done(self, *values):
        self.last = values


class Task:
    def __init__(self, steps):
        self.steps, self.wanted, self.got, self.begun, self.over = steps, [], None, False, False

    def advance(self, turns):
        if self.over:
            return
        if self.wanted:
            start([self], turns)
        try:
            self.wanted = self.steps.send(self.got) if self.begun else next(self.steps)
            self.begun = True
        except StopIteration:
            self.wanted, self.over = [], True

    def finish(self, turns):
        while not self.over:
            self.advance(turns)


def start(tasks, turns):
    tasks = [task for task in tasks if task.wanted]
    values = [value for task in tasks for value, _ in task.wanted]
    if not values:
        return
    tied = lax.optimization_barrier(tuple(values) + turns.last)[: len(values)]
    turns.done(tied[0])
    tied = iter(tied)
    for task in tasks:
        task.got = [move(next(tied)) for _, move in task.wanted]
        task.wanted = []


def reduce_steps(links, turns, make, order, out, name):
    keep, send = make()
    turns.done(keep, send)
    for k, bit in enumerate(order):
        (got,) = yield [(send, functools.partial(links.swap, bit=bit))]
        keep = turns.after(keep)
        if k == len(order) - 1:
            out[name] = keep + got
            turns.done(out[name])
            return
        half = keep.shape[0] // 2
        send = keep[half:] + got[half:]
        keep = keep[:half] + got[:half]
        turns.done(keep, send)


def scan_steps(links, turns, make, decays, backwards, out):
    keep, send, decay = make()
    bits = links.seq_bits
    levels = []
    kept = [] if decays is None else decays
    turns.done(keep, send)
    for bit in range(bits - 1):
        swap = functools.partial(links.swap, bit=bit)
        if decays is None:
            got, got_d = yield [(send, swap), (decay, swap)]
            kept.append((decay, got_d))
            decay = decay * got_d
        else:
            (got,) = yield [(send, swap)]
        mine_d, got_d = kept[bit]
        keep = turns.after(keep)
        odd = (links.at_seq >> bit) & 1
        second = (odd == 0) if backwards else (odd == 1)
        levels.append((second, keep, got, mine_d, got_d))
        total = jnp.where(second, mine_d * got + keep, got_d * keep + got)
        half = total.shape[0] // 2
        if bit < bits - 2:
            keep, send = total[:half], total[half:]
            turns.done(keep, send)
        else:
            send = total
            turns.done(send)
    flip = 1 << (bits - 1)
    pairs = [(i, i ^ flip) for i in range(links.n_seq) if ((i >> (bits - 1)) & 1) == int(backwards)]
    (state,) = yield [(send, lambda value: lax.ppermute(value, "seq", pairs))]
    for bit in reversed(range(bits - 1)):
        second, keep, got, mine_d, got_d = levels[bit]
        keep = turns.after(keep)
        theirs = jnp.where(second, state, mine_d * state + keep)
        mine = jnp.where(second, got_d * state + got, state)
        turns.done(theirs, mine)
        (far,) = yield [(theirs, functools.partial(links.swap, bit=bit))]
        if bit == 0:
            out["near"], out["far"], out["decays"] = mine, far, kept
        else:
            mine = turns.after(mine)
            state = jnp.concatenate([mine, far], axis=0)


ROUTES = {
    "gate": ("x", "y", "z0", "z1"),
    "up": ("y", "x", "z0", "z1"),
    "down": ("z0", "x", "y", "z1"),
    "mid": ("x", "y", "z0", "z1"),
    "qk": ("x", "y", "z0", "z1"),
    "v": ("y", "x", "z0", "z1"),
    "small": ("x", "y", "z0", "z1"),
}
SCHEDULE = (
    "gate", "up", ("gate", "up"), "down", ("down",), "gate", ("gate",), "up", ("up",), "down",
    ("down",), "ff", "scan", ("scan",), "mid", "gate", "up", "down", "scan", ("scan", "up",
    "mid"), "mid", "scan", ("scan", "gate"), "up", "scan", ("scan", "mid"), "local", "gate",
    "scan", ("scan",), "scan", ("scan",), "mid", "scan", ("scan", "gate", "up", "down", "mid"),
    "scan", "qk", "v", "gate", "up", "down", "mid", ("qk", "v", "gate", "up", "mid"), "qk", "v",
    ("qk", "v"), "small", "small", "qk", "v", ("qk", "v"), "gate", "up", ("small", "down"),
    "mid", ("mid",), "qk", "v", ("qk", "v"), "small", ("small",), "qk", "v", ("qk", "v"),
    "down", ("down",), "small", ("small",), "mid", "small", ("small",), "qk", "v", "small",
    ("small",), "down", "small",
)


def local(
    block_in, doc_starts, cotangent, norm1_gain, w_query, w_key, w_value, w_outgate, w_rank_down,
    w_rank_up, decay_bias, group_gain, w_output, norm2_gain, w_ffgate, w_ffup, w_ffdown,
):
    row_count, length, width = block_in.shape
    tokens = row_count * length
    kw, vw = w_query.shape[1], w_value.shape[1]
    links, turns = Links(), Turns()
    parts = links.n_seq
    everyone = links.n_dp * links.n_seq
    dims = (row_count, length, width, kw, vw, doc_starts.shape[1], parts)
    x = block_in.reshape(tokens, width)
    cot = cotangent.reshape(tokens, width)
    docs = (doc_starts - links.at_seq * length).reshape(-1)
    rank_down_t = w_rank_down.T

    levels = range(links.seq_bits - 1)
    step = 1 << len(levels)
    size = parts // step
    low = links.at_seq & (step - 1)
    turn = lambda p: sum(((p >> b) & 1) << (len(levels) - 1 - b) for b in levels)
    reverse = jnp.array([turn(p) for p in range(step)], jnp.int32)
    spread = jnp.arange(size)
    to_piece = ((reverse ^ low)[:, None] * size + spread).reshape(-1)
    to_place = ((reverse ^ turn(low))[:, None] * size + spread).reshape(-1)
    state_table = jnp.concatenate([to_piece, to_place]).astype(jnp.int32)

    normed, k, v, ra, gp, cum, keep_a, send_a, keep_b, send_b, decay = project_all(
        x, docs, state_table, norm1_gain, w_key, w_value, rank_down_t, w_rank_up, decay_bias, dims
    )
    decay = decay.reshape(1, row_count, HEADS, 1, kw // HEADS)
    fwd_a, fwd_b = {}, {}
    one = Task(scan_steps(
        links, turns, lambda: (keep_a, send_a, decay[:, :, : HEADS // 2]), None, False, fwd_a
    ))
    two = Task(scan_steps(
        links, turns, lambda: (keep_b, send_b, decay[:, :, HEADS // 2 :]), None, False, fwd_b
    ))
    one.advance(turns)
    start([one], turns)
    two.advance(turns)
    start([two], turns)
    one.advance(turns)
    start([one], turns)
    two.advance(turns)
    start([two], turns)
    dh = hidden_back_all(turns.after(cot), w_ffdown)
    turns.done(dh)
    one.advance(turns)
    start([one], turns)
    two.advance(turns)
    start([two], turns)
    q, og = readers_all(turns.after(normed), w_query, w_outgate)
    turns.done(q)
    one.advance(turns)
    start([one], turns)
    two.advance(turns)
    start([two], turns)
    inner = inner_all(q, k, v, cum, turns.after(docs), dims)
    turns.done(inner)
    while not two.over:
        one.advance(turns)
        start([one], turns)
        two.advance(turns)
        start([two], turns)
    decays = [
        tuple(jnp.concatenate(pair, axis=2) for pair in zip(*both))
        for both in zip(fwd_a["decays"], fwd_b["decays"])
    ]
    states = (fwd_a["near"], fwd_a["far"], fwd_b["near"], fwd_b["far"])
    mixed, gated, state_kept = mix_all(
        q, cum, inner, og, states, group_gain, turns.after(docs), state_table, dims
    )
    hidden, dg, du, normed2, middle = ff_all(
        x, gated, w_output, norm2_gain, w_ffgate, w_ffup, dh
    )
    turns.done(normed2)

    routes = {name: links.order(*route) for name, route in ROUTES.items()}
    tables = {route: links.table(route) for route in set(routes.values())}
    back, grads, held = {}, {}, {}
    ff = w_ffgate.shape[1]

    def ff_steps():
        out, d_middle, d_out, d_gated, gnorm2 = ff_back_all(
            hidden, dg, du, w_ffdown, w_ffgate, w_ffup, middle, turns.after(cot), w_output, norm2_gain
        )
        held.update(out=out, d_middle=d_middle, d_out=d_out, d_gated=d_gated, gnorm2=gnorm2)
        turns.done(d_out)
        return
        yield

    def head_back():
        d_mix, d_og, keep, send, ggroup = head_back_all(
            held["d_gated"], og, mixed, q, cum, group_gain, turns.after(docs), state_table, dims
        )
        held.update(d_mix=d_mix, d_og=d_og, ggroup=ggroup)
        return keep, send, None

    def local_steps():
        held["d_q"], held["own_k"], held["own_v"], held["decay"] = mix_local_all(
            q, k, v, cum, held["d_mix"], state_kept, turns.after(docs), dims
        )
        turns.done(held["d_q"])
        return
        yield

    def all_back():
        yield from scan_steps(links, turns, head_back, decays, True, back)
        held["d_k"], held["d_v"], held["d_rank"], held["grup"], held["gbias"] = mix_back_all(
            k, v, cum, gp, ra, state_kept, held["own_k"], held["own_v"], held["decay"], back["near"],
            back["far"], w_rank_up, turns.after(docs), state_table, dims,
        )
        turns.done(held["d_rank"])

    operands = {
        "gate": lambda: [(normed2, dg)],
        "up": lambda: [(normed2, du)],
        "down": lambda: [(hidden, cot)],
        "mid": lambda: [(gated, held["d_out"]), (normed, held["d_og"])],
        "qk": lambda: [(normed, held["d_q"]), (normed, held["d_k"])],
        "v": lambda: [(normed, held["d_v"])],
    }
    made = {}

    def weights(name, *names):
        def make():
            if name not in made:
                ordered = [tables[routes[each]] for each in names]
                ordered[0] = turns.after(ordered[0])
                room = 60 if name in ("gate", "up", "down") else 32
                groups = weight_grads([operands[each]() for each in names], ordered, room)
                made.update(zip(names, groups))
            return made[name]

        return reduce_steps(links, turns, make, routes[name], grads, name)

    def small_steps():
        grad_in, gnorm1 = input_back_all(
            x, held["d_middle"], held["d_q"], held["d_k"], held["d_v"], held["d_og"], held["d_rank"],
            turns.after(norm1_gain), w_query, w_key, w_value, w_outgate, rank_down_t,
        )
        held["grad_in"] = grad_in
        turns.done(gnorm1)
        yield []
        make = lambda: small_grads(
            normed, held["d_rank"], gnorm1, held["gnorm2"], held["grup"], held["gbias"],
            held["ggroup"], turns.after(tables[routes["small"]]),
        )
        yield from reduce_steps(links, turns, make, routes["small"], grads, "small")

    rank = w_rank_up.shape[0]
    work = {
        "ff": ff_steps(),
        "scan": all_back(),
        "gate": weights("gate", "gate", "up"),
        "up": weights("up", "gate", "up"),
        "down": weights("down", "down"),
        "mid": weights("mid", "mid"),
        "local": local_steps(),
        "qk": weights("qk", "qk", "v"),
        "v": weights("v", "qk", "v"),
        "small": small_steps(),
    }
    work = {name: Task(steps) for name, steps in work.items()}
    for name in SCHEDULE + tuple(work) * (2 * len(routes["gate"])):
        if isinstance(name, tuple):
            start([work[each] for each in name], turns)
            continue
        if name in ("scan", "mid", "local"):
            work["ff"].finish(turns)
        if name in ("qk", "v", "small"):
            work["local"].finish(turns)
            work["scan"].finish(turns)
        work[name].advance(turns)

    per, per_k = width // everyone, kw // everyone
    small = grads["small"][0]
    first, second, third = small[:per], small[per : per + per_k], small[per + per_k :]
    mid, qk = grads["mid"][0], grads["qk"][0]
    return (
        held["out"].reshape(row_count, length, width),
        held["grad_in"].reshape(row_count, length, width),
        first[:, rank],
        qk[:per],
        qk[per:],
        grads["v"][0],
        mid[per:],
        first[:, :rank],
        second[:, :rank].T,
        second[:, rank],
        third[:, 0],
        mid[:per],
        first[:, rank + 1],
        grads["gate"][0],
        grads["up"][0],
        grads["down"][0],
    )


def solution(mesh):
    tokens = P("dp", "seq", None)
    rows = P(("dp", "seq"), None)
    vector = P(("dp", "seq"))
    return jax.shard_map(
        local,
        mesh=mesh,
        in_specs=(tokens, P("dp", None), tokens) + (P(),) * 14,
        out_specs=(
            tokens, tokens, vector, rows, rows, rows, rows, rows, P(None, ("dp", "seq")), vector,
            vector, rows, vector, rows, rows, rows,
        ),
        check_vma=False,
    )
```

```python
import functools

import jax
import jax.numpy as jnp
from jax import lax
from jax.experimental import pallas as pl
from jax.experimental.pallas import tpu as pltpu
from jax.sharding import PartitionSpec as P

HEADS = 4
EPS = 1e-06
MIB = 1 << 20
BF = jnp.bfloat16
F32 = jnp.float32
HIGHEST = lax.Precision.HIGHEST


def nn(a, b, precision=None):
    return lax.dot_general(
        a, b, (((1,), (0,)), ((), ())), precision=precision, preferred_element_type=F32
    )


def nt(a, b):
    return lax.dot_general(a, b, (((1,), (1,)), ((), ())), preferred_element_type=F32)


def tn(a, b):
    return lax.dot_general(a, b, (((0,), (0,)), ((), ())), preferred_element_type=F32)


def shape(dims, dtype):
    return jax.ShapeDtypeStruct(dims, dtype)


def call(body, out_shape, grid, in_specs, out_specs, prefetch=0, scratch=(), room=60):
    return pl.pallas_call(
        body,
        out_shape=out_shape,
        grid_spec=pltpu.PrefetchScalarGridSpec(
            num_scalar_prefetch=prefetch,
            grid=grid,
            in_specs=in_specs,
            out_specs=out_specs,
            scratch_shapes=list(scratch),
        ),
        compiler_params=pltpu.CompilerParams(vmem_limit_bytes=room * MIB),
        cost_estimate=pl.CostEstimate(flops=1, bytes_accessed=1, transcendentals=0),
    )


def block(dims, index):
    return pl.BlockSpec(dims, index)


def whole(dims):
    zero = (0,) * len(dims)
    return pl.BlockSpec(dims, lambda *_: zero)


def reset_masks(docs_ref, row, docs, length):
    at_i = lax.broadcasted_iota(jnp.int32, (length, length), 0)
    at_j = lax.broadcasted_iota(jnp.int32, (length, length), 1)
    token = lax.broadcasted_iota(jnp.int32, (length, 1), 0)
    visible = at_i >= at_j
    alive = token >= 0
    tail = token >= 0
    whole_alive = jnp.float32(1.0)
    for n in range(docs):
        start = docs_ref[row * docs + n]
        visible = visible & jnp.logical_not((at_j < start) & (start <= at_i))
        inside = (start >= 0) & (start < length)
        first = jnp.where(start >= 0, start, length)
        alive = alive & (token < first)
        last = jnp.where(start < length, start, -1)
        tail = tail & (token >= last)
        whole_alive = whole_alive * jnp.where(inside, 0.0, 1.0)
    return visible, alive.astype(F32), tail.astype(F32), whole_alive


def lower_ones(length, strict=False):
    at_i = lax.broadcasted_iota(jnp.int32, (length, length), 0)
    at_j = lax.broadcasted_iota(jnp.int32, (length, length), 1)
    return (at_i > at_j if strict else at_i >= at_j).astype(F32)


def project_body(
    rows, docs, length, hk, hv, parts,
    docs_ref, table_ref, x_ref, gain_ref, wk_ref, wv_ref, wrd_ref, wru_ref, bias_ref,
    normed_ref, k_ref, v_ref, ra_ref, gp_ref, cum_ref, keep_a_ref, send_a_ref, keep_b_ref,
    send_b_ref, decay_ref,
    hold,
):
    x = x_ref[...].astype(F32)
    inv = lax.rsqrt(jnp.mean(x * x, axis=-1, keepdims=True) + EPS)
    normed = (x * inv * gain_ref[...]).astype(BF)
    normed_ref[...] = normed
    rank = nt(normed, wrd_ref[...]).astype(BF)
    ra_ref[...] = rank
    gate = nn(rank, wru_ref[...]) + bias_ref[...]
    gp_ref[...] = gate
    key = nn(normed, wk_ref[...]).astype(BF)
    k_ref[...] = key
    value = nn(normed, wv_ref[...]).astype(BF)
    v_ref[...] = value
    log_decay = (jnp.minimum(gate, 0.0) - jnp.log1p(jnp.exp(-jnp.abs(gate)))) * (1.0 / 16.0)
    tri = lower_ones(length)
    size = hv // parts
    for r in range(rows):
        at = slice(r * length, (r + 1) * length)
        row = pl.program_id(0) * rows + r
        cum = nn(tri, log_decay[at], HIGHEST)
        cum_ref[at, :] = cum
        _, _, tail, whole_alive = reset_masks(docs_ref, row, docs, length)
        last = cum[length - 1 :, :]
        decay_ref[r] = jnp.exp(last) * whole_alive
        weighted = (key[at].astype(F32) * jnp.exp(last - cum) * tail).astype(BF)
        for h in range(HEADS):
            hold[...] = tn(value[at, h * hv : (h + 1) * hv], weighted[:, h * hk : (h + 1) * hk])
            keep_ref, send_ref = (keep_a_ref, send_a_ref) if h < HEADS // 2 else (keep_b_ref, send_b_ref)
            for j in range(parts // 2):
                first = pl.multiple_of(table_ref[j] * size, size)
                keep_ref[j, r, h % (HEADS // 2)] = hold[pl.ds(first, size), :]
                second = pl.multiple_of(table_ref[parts // 2 + j] * size, size)
                send_ref[j, r, h % (HEADS // 2)] = hold[pl.ds(second, size), :]


def project_all(x, docs, table, gain, wk, wv, wrd, wru, bias, dims):
    row_count, length, width, kw, vw, ndocs, parts = dims
    tokens = row_count * length
    rows = 2 if row_count % 2 == 0 else 1
    tm = rows * length
    hk, hv = kw // HEADS, vw // HEADS
    rank = wrd.shape[0]
    size = hv // parts
    tile = lambda n: block((tm, n), lambda i, *_: (i, 0))
    half = (parts // 2, row_count, HEADS // 2, size, hk)
    half_block = block((parts // 2, rows, HEADS // 2, size, hk), lambda i, *_: (0, i, 0, 0, 0))
    body = functools.partial(project_body, rows, ndocs, length, hk, hv, parts)
    return call(
        body,
        (
            shape((tokens, width), BF),
            shape((tokens, kw), BF),
            shape((tokens, vw), BF),
            shape((tokens, rank), BF),
            shape((tokens, kw), F32),
            shape((tokens, kw), F32),
            shape(half, F32),
            shape(half, F32),
            shape(half, F32),
            shape(half, F32),
            shape((row_count, 1, kw), F32),
        ),
        (row_count // rows,),
        [
            tile(width), whole((1, width)), whole(wk.shape), whole(wv.shape), whole(wrd.shape),
            whole(wru.shape), whole((1, kw)),
        ],
        (
            tile(width), tile(kw), tile(vw), tile(rank), tile(kw), tile(kw),
            half_block, half_block, half_block, half_block,
            block((rows, 1, kw), lambda i, *_: (i, 0, 0)),
        ),
        prefetch=2,
        scratch=[pltpu.VMEM((hv, hk), F32)],
    )(docs, table, x, gain.reshape(1, -1), wk, wv, wrd, wru, bias.reshape(1, -1))


def readers_body(normed_ref, wq_ref, wog_ref, q_ref, og_ref):
    q_ref[...] = nn(normed_ref[...], wq_ref[...]).astype(BF)
    og_ref[...] = nn(normed_ref[...], wog_ref[...])


def readers_all(normed, wq, wog):
    tokens, width = normed.shape
    tm = 256 if tokens % 256 == 0 else 128
    tile = lambda n: block((tm, n), lambda i: (i, 0))
    return call(
        readers_body,
        (shape((tokens, wq.shape[1]), BF), shape((tokens, wog.shape[1]), F32)),
        (tokens // tm,),
        [tile(width), whole(wq.shape), whole(wog.shape)],
        (tile(wq.shape[1]), tile(wog.shape[1])),
        room=28,
    )(normed, wq, wog)


def span_factors(cum, length):
    middle = cum[length // 2 - 1 : length // 2, :]
    return jnp.exp(cum - middle), jnp.exp(middle - cum)


def inner_body(docs, length, hk, hv, docs_ref, q_ref, k_ref, v_ref, cum_ref, inner_ref):
    visible, _, _, _ = reset_masks(docs_ref, pl.program_id(0), docs, length)
    up, down = span_factors(cum_ref[...], length)
    q = (q_ref[...].astype(F32) * up).astype(BF)
    k = (k_ref[...].astype(F32) * down).astype(BF)
    for h in range(HEADS):
        kk = slice(h * hk, (h + 1) * hk)
        vv = slice(h * hv, (h + 1) * hv)
        scores = jnp.where(visible, nt(q[:, kk], k[:, kk]), 0.0).astype(BF)
        inner_ref[:, vv] = nn(scores, v_ref[:, vv])


def inner_all(q, k, v, cum, docs, dims):
    row_count, length, width, kw, vw, ndocs, parts = dims
    tokens = row_count * length
    tile = lambda n: block((length, n), lambda i, *_: (i, 0))
    return call(
        functools.partial(inner_body, ndocs, length, kw // HEADS, vw // HEADS),
        shape((tokens, vw), F32),
        (row_count,),
        [tile(kw), tile(kw), tile(vw), tile(kw)],
        tile(vw),
        prefetch=1,
        room=28,
    )(docs, q, k, v, cum)


def gather_state(near_ref, far_ref, table_ref, h, parts):
    half = parts // 2
    pieces = []
    for p in range(parts):
        place = table_ref[parts + p]
        near = near_ref[jnp.minimum(place, half - 1), 0, h]
        far = far_ref[jnp.maximum(place - half, 0), 0, h]
        pieces.append(jnp.where(place < half, near, far))
    return jnp.concatenate(pieces, axis=0)


def mix_body(
    docs, length, hk, hv, parts,
    docs_ref, table_ref, q_ref, cum_ref, inner_ref, og_ref, near_a_ref, far_a_ref, near_b_ref, far_b_ref,
    gain_ref,
    mixed_ref, gated_ref, kept_ref,
):
    _, alive, _, _ = reset_masks(docs_ref, pl.program_id(0), docs, length)
    reach = (q_ref[...].astype(F32) * jnp.exp(cum_ref[...]) * alive).astype(BF)
    scale = hk ** (-0.5)
    for h in range(HEADS):
        kk = slice(h * hk, (h + 1) * hk)
        vv = slice(h * hv, (h + 1) * hv)
        near_ref, far_ref = (near_a_ref, far_a_ref) if h < HEADS // 2 else (near_b_ref, far_b_ref)
        state = gather_state(near_ref, far_ref, table_ref, h % (HEADS // 2), parts).astype(BF)
        kept_ref[0, h] = state
        mixed = scale * (inner_ref[:, vv] + nt(reach[:, kk], state))
        mixed_ref[:, vv] = mixed
        inv = lax.rsqrt(jnp.mean(mixed * mixed, axis=-1, keepdims=True) + EPS)
        og = og_ref[:, vv]
        gated_ref[:, vv] = (mixed * inv * gain_ref[...] * og * jax.nn.sigmoid(og)).astype(BF)


def mix_all(q, cum, inner, og, states, gain, docs, table, dims):
    row_count, length, width, kw, vw, ndocs, parts = dims
    tokens = row_count * length
    hk, hv = kw // HEADS, vw // HEADS
    tile = lambda n: block((length, n), lambda i, *_: (i, 0))
    half = block((parts // 2, 1, HEADS // 2, hv // parts, hk), lambda i, *_: (0, i, 0, 0, 0))
    return call(
        functools.partial(mix_body, ndocs, length, hk, hv, parts),
        (
            shape((tokens, vw), F32),
            shape((tokens, vw), BF),
            shape((row_count, HEADS, hv, hk), BF),
        ),
        (row_count,),
        [
            tile(kw), tile(kw), tile(vw), tile(vw), half, half, half, half, whole((1, hv)),
        ],
        (tile(vw), tile(vw), block((1, HEADS, hv, hk), lambda i, *_: (i, 0, 0, 0))),
        prefetch=2,
    )(docs, table, q, cum, inner, og, *states, gain.reshape(1, -1))


def hidden_back_body(cot_ref, wd_ref, dh_ref):
    dh_ref[...] = nt(cot_ref[...], wd_ref[...])


def hidden_back_all(cot, wd):
    tokens, width = cot.shape
    ff, tile = wd.shape[0], 256
    return call(
        hidden_back_body,
        shape((tokens, ff), F32),
        (ff // tile,),
        [whole((tokens, width)), block((tile, width), lambda i: (i, 0))],
        block((tokens, tile), lambda i: (0, i)),
    )(cot, wd)


def ff_body(
    x_ref, gated_ref, wo_ref, gain_ref, wg_ref, wu_ref, dh_ref,
    hidden_ref, dg_ref, du_ref, normed2_ref, middle_ref,
):
    @pl.when(pl.program_id(0) == 0)
    def _():
        mid = x_ref[...].astype(F32) + nn(gated_ref[...], wo_ref[...])
        middle_ref[...] = mid
        inv = lax.rsqrt(jnp.mean(mid * mid, axis=-1, keepdims=True) + EPS)
        normed2_ref[...] = (mid * inv * gain_ref[...]).astype(BF)

    normed2 = normed2_ref[...]
    gate = nn(normed2, wg_ref[...])
    up = nn(normed2, wu_ref[...])
    d_hidden = dh_ref[...]
    sig = jax.nn.sigmoid(gate)
    act = gate * sig
    hidden_ref[...] = (act * up).astype(BF)
    dg_ref[...] = (d_hidden * up * sig * (1.0 + gate * (1.0 - sig))).astype(BF)
    du_ref[...] = (d_hidden * act).astype(BF)


def ff_all(x, gated, wo, gain, wg, wu, dh):
    tokens, width = x.shape
    ff = wg.shape[1]
    tile = 256
    col = lambda n: block((n, tile), lambda i: (0, i))
    once = lambda dims: pl.BlockSpec(dims, lambda i: (0, 0), pipeline_mode=pl.Buffered(1))
    return call(
        ff_body,
        (
            shape((tokens, ff), BF), shape((tokens, ff), BF), shape((tokens, ff), BF),
            shape((tokens, width), BF), shape((tokens, width), F32),
        ),
        (ff // tile,),
        [
            once((tokens, width)), once(gated.shape), once(wo.shape), once((1, width)),
            col(width), col(width), col(tokens),
        ],
        (
            col(tokens), col(tokens), col(tokens), whole((tokens, width)), whole((tokens, width)),
        ),
    )(x, gated, wo, gain.reshape(1, -1), wg, wu, dh)


def ff_back_body(
    steps,
    hidden_ref, dg_ref, du_ref, wd_ref, wg_ref, wu_ref, middle_ref, cot_ref, wo_ref, gain_ref,
    out_ref, dmid_ref, dout_ref, dgated_ref, gnorm_ref,
):
    total, back = dgated_ref, dmid_ref
    step = pl.program_id(0)
    tokens = middle_ref.shape[0]
    rows = 256 if tokens % 256 == 0 else tokens
    for first in range(0, tokens, rows):
        at = slice(first, first + rows)
        more = nn(hidden_ref[at, :], wd_ref[...])
        more_back = nt(dg_ref[at, :], wg_ref[...]) + nt(du_ref[at, :], wu_ref[...])

        @pl.when(step == 0)
        def _(at=at, more=more, more_back=more_back):
            total[at, :] = more
            back[at, :] = more_back

        @pl.when(step > 0)
        def _(at=at, more=more, more_back=more_back):
            total[at, :] += more
            back[at, :] += more_back

    @pl.when(step == steps - 1)
    def _():
        gnorm = jnp.zeros((1, middle_ref.shape[1]), F32)
        for first in range(0, tokens, rows):
            at = slice(first, first + rows)
            mid = middle_ref[at, :]
            out_ref[at, :] = (mid + total[at, :]).astype(BF)
            inv = lax.rsqrt(jnp.mean(mid * mid, axis=-1, keepdims=True) + EPS)
            d_normed2 = back[at, :]
            gnorm = gnorm + jnp.sum(d_normed2 * mid * inv, axis=0, keepdims=True)
            scaled = d_normed2 * gain_ref[...]
            d_middle = (
                cot_ref[at, :].astype(F32)
                + inv * scaled
                - mid * (inv * inv * inv) * jnp.mean(scaled * mid, axis=-1, keepdims=True)
            )
            dmid_ref[at, :] = d_middle
            d_out = d_middle.astype(BF)
            dout_ref[at, :] = d_out
            dgated_ref[at, :] = nt(d_out, wo_ref[...])
        gnorm_ref[...] = gnorm


def ff_back_all(hidden, dg, du, wd, wg, wu, middle, cot, wo, gain):
    tokens, width = middle.shape
    vw, ff = wo.shape[0], wg.shape[1]
    tile = 1408 if ff % 1408 == 0 else 256
    steps = ff // tile
    col = lambda n: block((n, tile), lambda i: (0, i))
    once = lambda dims: pl.BlockSpec(dims, lambda i: (0, 0), pipeline_mode=pl.Buffered(1))
    return call(
        functools.partial(ff_back_body, steps),
        (
            shape((tokens, width), BF), shape((tokens, width), F32), shape((tokens, width), BF),
            shape((tokens, vw), F32), shape((1, width), F32),
        ),
        (steps,),
        [
            col(tokens), col(tokens), col(tokens), block((tile, width), lambda i: (i, 0)),
            col(width), col(width), once((tokens, width)), once((tokens, width)), once(wo.shape),
            once((1, width)),
        ],
        (
            whole((tokens, width)), whole((tokens, width)), whole((tokens, width)),
            whole((tokens, vw)), whole((1, width)),
        ),
    )(hidden, dg, du, wd, wg, wu, middle, cot, wo, gain.reshape(1, -1))


def head_back_body(
    docs, length, hk, hv, parts,
    docs_ref, table_ref, dgated_ref, og_ref, mixed_ref, q_ref, cum_ref, gain_ref,
    dmix_ref, dog_ref, keep_ref, send_ref, ggroup_ref,
    hold,
):
    row = pl.program_id(0)
    _, alive, _, _ = reset_masks(docs_ref, row, docs, length)
    reach = (q_ref[...].astype(F32) * jnp.exp(cum_ref[...]) * alive).astype(BF)
    scale = hk ** (-0.5)
    size = hv // parts
    ggroup = jnp.zeros((1, hv), F32)
    for h in range(HEADS):
        kk = slice(h * hk, (h + 1) * hk)
        vv = slice(h * hv, (h + 1) * hv)
        mixed = mixed_ref[:, vv]
        inv = lax.rsqrt(jnp.mean(mixed * mixed, axis=-1, keepdims=True) + EPS)
        og = og_ref[:, vv]
        sig = jax.nn.sigmoid(og)
        dgated = dgated_ref[:, vv]
        unit = mixed * inv
        dog_ref[:, vv] = (
            dgated * unit * gain_ref[...] * sig * (1.0 + og * (1.0 - sig))
        ).astype(BF)
        d_heads = dgated * og * sig
        ggroup = ggroup + jnp.sum(d_heads * unit, axis=0, keepdims=True)
        scaled = d_heads * gain_ref[...]
        d_mixed = inv * scaled - mixed * (inv * inv * inv) * jnp.mean(
            scaled * mixed, axis=-1, keepdims=True
        )
        d_mixed = (scale * d_mixed).astype(BF)
        dmix_ref[:, vv] = d_mixed
        hold[...] = tn(d_mixed, reach[:, kk])
        for j in range(parts // 2):
            first = pl.multiple_of(table_ref[j] * size, size)
            keep_ref[j, 0, h] = hold[pl.ds(first, size), :]
            second = pl.multiple_of(table_ref[parts // 2 + j] * size, size)
            send_ref[j, 0, h] = hold[pl.ds(second, size), :]

    @pl.when(row == 0)
    def _():
        ggroup_ref[...] = ggroup

    @pl.when(row > 0)
    def _():
        ggroup_ref[...] += ggroup


def head_back_all(dgated, og, mixed, q, cum, gain, docs, table, dims):
    row_count, length, width, kw, vw, ndocs, parts = dims
    tokens = row_count * length
    hk, hv = kw // HEADS, vw // HEADS
    size = hv // parts
    tile = lambda n: block((length, n), lambda i, *_: (i, 0))
    half = (parts // 2, row_count, HEADS, size, hk)
    half_block = block((parts // 2, 1, HEADS, size, hk), lambda i, *_: (0, i, 0, 0, 0))
    return call(
        functools.partial(head_back_body, ndocs, length, hk, hv, parts),
        (
            shape((tokens, vw), BF), shape((tokens, vw), BF),
            shape(half, F32), shape(half, F32), shape((1, hv), F32),
        ),
        (row_count,),
        [tile(vw), tile(vw), tile(vw), tile(kw), tile(kw), whole((1, hv))],
        (tile(vw), tile(vw), half_block, half_block, whole((1, hv))),
        prefetch=2,
        scratch=[pltpu.VMEM((hv, hk), F32)],
    )(docs, table, dgated, og, mixed, q, cum, gain.reshape(1, -1))


def mix_local_body(
    docs, length, hk, hv,
    docs_ref, q_ref, k_ref, v_ref, cum_ref, dmix_ref, state_ref,
    dq_ref, dk_ref, dv_ref, decay_ref,
):
    visible, alive, _, _ = reset_masks(docs_ref, pl.program_id(0), docs, length)
    cum = cum_ref[...]
    up, down = span_factors(cum, length)
    from_start = jnp.exp(cum) * alive
    q = q_ref[...].astype(F32)
    q_span = (q * up).astype(BF)
    k_span = (k_ref[...].astype(F32) * down).astype(BF)
    reach = (q * from_start).astype(BF)
    later = []
    for h in range(HEADS):
        kk = slice(h * hk, (h + 1) * hk)
        vv = slice(h * hv, (h + 1) * hv)
        qs, ks = q_span[:, kk], k_span[:, kk]
        d_mix = dmix_ref[:, vv]
        scores = jnp.where(visible, nt(qs, ks), 0.0).astype(BF)
        d_scores = jnp.where(visible, nt(d_mix, v_ref[:, vv]), 0.0).astype(BF)
        dq_in = nn(d_scores, ks)
        dk_in = tn(d_scores, qs)
        dq_out = nn(d_mix, state_ref[0, h])
        dq_ref[:, kk] = (dq_in * up[:, kk] + dq_out * from_start[:, kk]).astype(BF)
        dk_ref[:, kk] = dk_in * down[:, kk]
        dv_ref[:, vv] = tn(scores, d_mix)
        later.append(
            qs.astype(F32) * dq_in - ks.astype(F32) * dk_in + reach[:, kk].astype(F32) * dq_out
        )
    at_i = lax.broadcasted_iota(jnp.int32, (length, length), 0)
    at_j = lax.broadcasted_iota(jnp.int32, (length, length), 1)
    decay_ref[...] = nn((at_i <= at_j).astype(F32), jnp.concatenate(later, axis=1), HIGHEST)


def mix_local_all(q, k, v, cum, dmix, state, docs, dims):
    row_count, length, width, kw, vw, ndocs, parts = dims
    tokens = row_count * length
    hk, hv = kw // HEADS, vw // HEADS
    tile = lambda n: block((length, n), lambda i, *_: (i, 0))
    return call(
        functools.partial(mix_local_body, ndocs, length, hk, hv),
        (
            shape((tokens, kw), BF), shape((tokens, kw), F32), shape((tokens, vw), F32),
            shape((tokens, kw), F32),
        ),
        (row_count,),
        [
            tile(kw), tile(kw), tile(vw), tile(kw), tile(vw),
            block((1, HEADS, hv, hk), lambda i, *_: (i, 0, 0, 0)),
        ],
        (tile(kw), tile(kw), tile(vw), tile(kw)),
        prefetch=1,
        room=28,
    )(docs, q, k, v, cum, dmix, state)


def mix_back_body(
    docs, length, hk, hv, parts,
    docs_ref, table_ref, k_ref, v_ref, cum_ref, gp_ref, ra_ref, state_ref, dk_ref, dv_ref, decay_ref,
    near_ref, far_ref, wru_ref,
    dk_out_ref, dv_out_ref, drank_ref, grup_ref, gbias_ref,
):
    row = pl.program_id(0)
    _, _, tail, whole_alive = reset_masks(docs_ref, row, docs, length)
    cum = cum_ref[...]
    last = cum[length - 1 :, :]
    to_end = jnp.exp(last - cum) * tail
    weighted = (k_ref[...].astype(F32) * to_end).astype(BF)
    earlier, crossing = [], []
    for h in range(HEADS):
        kk = slice(h * hk, (h + 1) * hk)
        vv = slice(h * hv, (h + 1) * hv)
        grad32 = gather_state(near_ref, far_ref, table_ref, h, parts)
        grad = grad32.astype(BF)
        dk_out = nn(v_ref[:, vv], grad)
        dk_out_ref[:, kk] = (dk_ref[:, kk] + dk_out * to_end[:, kk]).astype(BF)
        dv_out_ref[:, vv] = (
            dv_ref[:, vv] + nt(weighted[:, kk], grad)
        ).astype(BF)
        earlier.append(weighted[:, kk].astype(F32) * dk_out)
        crossing.append(jnp.sum(state_ref[0, h].astype(F32) * grad32, axis=0, keepdims=True))
    d_decay = (
        decay_ref[...]
        + nn(lower_ones(length, True), jnp.concatenate(earlier, axis=1), HIGHEST)
        + jnp.exp(last) * whole_alive * jnp.concatenate(crossing, axis=1)
    )
    d_gate = (d_decay * jax.nn.sigmoid(-gp_ref[...]) * (1.0 / 16.0)).astype(BF)
    drank_ref[...] = nt(d_gate, wru_ref[...]).astype(BF)
    grup = tn(ra_ref[...], d_gate)
    gbias = jnp.sum(d_gate.astype(F32), axis=0, keepdims=True)

    @pl.when(row == 0)
    def _():
        grup_ref[...] = grup
        gbias_ref[...] = gbias

    @pl.when(row > 0)
    def _():
        grup_ref[...] += grup
        gbias_ref[...] += gbias


def mix_back_all(k, v, cum, gp, ra, state, dk, dv, decay, near, far, wru, docs, table, dims):
    row_count, length, width, kw, vw, ndocs, parts = dims
    tokens = row_count * length
    hk, hv = kw // HEADS, vw // HEADS
    rank = wru.shape[0]
    tile = lambda n: block((length, n), lambda i, *_: (i, 0))
    half = block((parts // 2, 1, HEADS, hv // parts, hk), lambda i, *_: (0, i, 0, 0, 0))
    return call(
        functools.partial(mix_back_body, ndocs, length, hk, hv, parts),
        (
            shape((tokens, kw), BF), shape((tokens, vw), BF), shape((tokens, rank), BF),
            shape((rank, kw), F32), shape((1, kw), F32),
        ),
        (row_count,),
        [
            tile(kw), tile(vw), tile(kw), tile(kw), tile(rank),
            block((1, HEADS, hv, hk), lambda i, *_: (i, 0, 0, 0)),
            tile(kw), tile(vw), tile(kw), half, half, whole((rank, kw)),
        ],
        (tile(kw), tile(vw), tile(rank), whole((rank, kw)), whole((1, kw))),
        prefetch=2,
        room=28,
    )(docs, table, k, v, cum, gp, ra, state, dk, dv, decay, near, far, wru)


def input_back_body(
    x_ref, dmid_ref, dq_ref, dk_ref, dv_ref, dog_ref, drank_ref, gain_ref, wq_ref, wk_ref, wv_ref, wog_ref, wrd_ref,
    gin_ref, gnorm_ref,
):
    step = pl.program_id(0)
    d_normed = (
        nt(dq_ref[...], wq_ref[...])
        + nt(dk_ref[...], wk_ref[...])
        + nt(dv_ref[...], wv_ref[...])
        + nt(dog_ref[...], wog_ref[...])
        + nn(drank_ref[...], wrd_ref[...])
    )
    x = x_ref[...].astype(F32)
    inv = lax.rsqrt(jnp.mean(x * x, axis=-1, keepdims=True) + EPS)
    gnorm = jnp.sum(d_normed * x * inv, axis=0, keepdims=True)
    scaled = d_normed * gain_ref[...]
    gin_ref[...] = (
        dmid_ref[...]
        + inv * scaled
        - x * (inv * inv * inv) * jnp.mean(scaled * x, axis=-1, keepdims=True)
    )

    @pl.when(step == 0)
    def _():
        gnorm_ref[...] = gnorm

    @pl.when(step > 0)
    def _():
        gnorm_ref[...] += gnorm


def input_back_all(x, dmid, dq, dk, dv, dog, drank, gain, wq, wk, wv, wog, wrd):
    tokens, width = x.shape
    kw, vw = wq.shape[1], wv.shape[1]
    tm = 256 if tokens % 256 == 0 else 128
    tile = lambda n: block((tm, n), lambda i: (i, 0))
    return call(
        input_back_body,
        (shape((tokens, width), F32), shape((1, width), F32)),
        (tokens // tm,),
        [
            tile(width), tile(width), tile(kw), tile(kw), tile(vw), tile(vw), tile(drank.shape[1]),
            whole((1, width)), whole(wq.shape), whole(wk.shape), whole(wv.shape), whole(wog.shape),
            whole(wrd.shape),
        ],
        (tile(width), whole((1, width))),
        room=28,
    )(x, dmid, dq, dk, dv, dog, drank, gain.reshape(1, -1), wq, wk, wv, wog, wrd)


def weight_body(groups, lefts, pieces, *refs):
    tables = refs[: len(groups)]
    refs = refs[len(groups) :]
    left_refs, refs = refs[:lefts], refs[lefts:]
    count = sum(len(group) for group in groups)
    rights, refs = refs[:count], refs[count:]
    outs, refs = refs[: 2 * len(groups)], refs[2 * len(groups) :]
    turned, holds = refs[:lefts], refs[lefts:]

    @pl.when(pl.program_id(0) == 0)
    def _():
        for n in range(lefts):
            turned[n][...] = left_refs[n][...].T

    at = 0
    for g, group in enumerate(groups):
        keep_ref, send_ref = outs[2 * g], outs[2 * g + 1]
        place = 0
        for left in group:
            hold = holds[g]
            hold[...] = nn(turned[left][...], rights[at][...])
            per = hold.shape[0] // pieces
            rows = slice(place, place + per)
            for j in range(pieces // 2):
                first = pl.multiple_of(tables[g][j] * per, per)
                keep_ref[j, rows, :] = hold[pl.ds(first, per), :]
                second = pl.multiple_of(tables[g][pieces // 2 + j] * per, per)
                send_ref[j, rows, :] = hold[pl.ds(second, per), :]
            at, place = at + 1, place + per


def weight_grads(groups, tables, room, steps=2):
    pieces = tables[0].shape[0]
    tokens = groups[0][0][0].shape[0]
    out = []
    if any(left.shape[1] // pieces % 8 for group in groups for left, _ in group):
        for group, table in zip(groups, tables):
            parts = [tn(left, right) for left, right in group]
            parts = [part.reshape(pieces, -1, part.shape[1]) for part in parts]
            parts = jnp.concatenate(parts, axis=1)[table]
            out.append((parts[: pieces // 2], parts[pieces // 2 :]))
        return out
    lefts, index = [], []
    for group in groups:
        index.append([])
        for left, _ in group:
            known = [n for n, other in enumerate(lefts) if other is left]
            if not known:
                lefts.append(left)
            index[-1].append(known[0] if known else len(lefts) - 1)
    rights = [right for group in groups for _, right in group]
    column = lambda n: block((tokens, n // steps), lambda i, *_: (0, i))
    shapes, blocks, holds = [], [], []
    for group in groups:
        rows, cols = group[0][0].shape[1], group[0][1].shape[1]
        dims = (pieces // 2, len(group) * rows // pieces, cols)
        shapes += [shape(dims, F32)] * 2
        blocks += [block(dims[:2] + (cols // steps,), lambda i, *_: (0, 0, i))] * 2
        holds.append(pltpu.VMEM((rows, cols // steps), F32))
    flat = call(
        functools.partial(weight_body, index, len(lefts), pieces),
        tuple(shapes),
        (steps,),
        [whole(left.shape) for left in lefts] + [column(right.shape[1]) for right in rights],
        tuple(blocks),
        prefetch=len(groups),
        scratch=[pltpu.VMEM(left.shape[::-1], BF) for left in lefts] + holds,
        room=room,
    )(*tables, *lefts, *rights)
    return [(flat[2 * g], flat[2 * g + 1]) for g in range(len(groups))]


def small_body(
    pieces,
    table_ref, normed_ref, drank_ref, gnorm1_ref, gnorm2_ref, grup_ref, gbias_ref, ggroup_ref,
    keep_ref, send_ref,
    hold,
):
    width, kw, hv = gnorm1_ref.shape[1], gbias_ref.shape[1], ggroup_ref.shape[1]
    rank = grup_ref.shape[0]

    def stand(rows):
        have = sum(row.shape[0] for row in rows)
        return jnp.concatenate(rows + [jnp.zeros((128 - have, rows[0].shape[1]), F32)], axis=0).T

    spread = jnp.zeros((normed_ref.shape[0], 128 - rank), BF)
    hold[:width, :] = tn(normed_ref[...], jnp.concatenate([drank_ref[...], spread], axis=1)) + stand(
        [jnp.zeros((rank, width), F32), gnorm1_ref[...], gnorm2_ref[...]]
    )
    hold[width : width + kw, :] = stand([grup_ref[...], gbias_ref[...]])
    hold[width + kw :, :] = stand([ggroup_ref[...]])
    first, place = 0, 0
    for rows in (width, kw, hv):
        per = rows // pieces
        for j in range(pieces // 2):
            keep = pl.multiple_of(first + table_ref[j] * per, per)
            keep_ref[j, place : place + per, :] = hold[pl.ds(keep, per), :]
            send = pl.multiple_of(first + table_ref[pieces // 2 + j] * per, per)
            send_ref[j, place : place + per, :] = hold[pl.ds(send, per), :]
        first, place = first + rows, place + per


def small_grads(normed, drank, gnorm1, gnorm2, grup, gbias, ggroup, table):
    pieces, rank = table.shape[0], grup.shape[0]
    width, kw, hv = gnorm1.shape[1], gbias.shape[1], ggroup.shape[1]
    rows = (width + kw + hv) // pieces
    if hv // pieces % 8:
        wide = lambda value: jnp.pad(value, ((0, 0), (0, 128 - value.shape[1])))
        cut = lambda value: wide(value).reshape(pieces, -1, 128)
        both = jnp.concatenate(
            [
                cut(jnp.concatenate([tn(normed, drank), gnorm1.T, gnorm2.T], axis=1)),
                cut(jnp.concatenate([grup.T, gbias.T], axis=1)),
                cut(ggroup.T),
            ],
            axis=1,
        )[table]
        return both[: pieces // 2], both[pieces // 2 :]
    half = shape((pieces // 2, rows, 128), F32)
    operands = (normed, drank, gnorm1, gnorm2, grup, gbias, ggroup)
    return call(
        functools.partial(small_body, pieces),
        (half, half),
        (1,),
        [whole(value.shape) for value in operands],
        (whole(half.shape), whole(half.shape)),
        prefetch=1,
        scratch=[pltpu.VMEM((width + kw + hv, 128), F32)],
        room=16,
    )(table, *operands)


def bits_of(n):
    return n.bit_length() - 1


class Links:
    def __init__(self):
        self.n_dp, self.n_seq = lax.axis_size("dp"), lax.axis_size("seq")
        self.seq_bits, self.dp_bits = bits_of(self.n_seq), bits_of(self.n_dp)
        self.at_seq = lax.axis_index("seq")
        self.me = lax.axis_index("dp") * self.n_seq + self.at_seq

    def swap(self, value, bit):
        name, n, flip = "seq", self.n_seq, 1 << bit
        if bit >= self.seq_bits:
            name, n, flip = "dp", self.n_dp, 1 << (bit - self.seq_bits)
        return lax.ppermute(value, name, [(i, i ^ flip) for i in range(n)])

    def table(self, order):
        n = 1 << len(order)
        places = [
            sum(((at >> (len(order) - 1 - k)) & 1) << bit for k, bit in enumerate(order))
            for at in range(n)
        ]
        here = self.me if n == self.n_dp * self.n_seq else self.at_seq
        return jnp.array(places, jnp.int32) ^ here

    def order(self, *names):
        across = tuple(range(self.seq_bits, self.seq_bits + self.dp_bits))
        bits = [0]
        for name in names:
            bits.extend(across if name == "x" else [{"y": 1, "z0": 2, "z1": 3}[name]])
        return tuple(bits) + tuple(b for b in range(self.seq_bits) if b not in bits)


class Turns:
    def __init__(self):
        self.last = ()

    def after(self, value):
        return lax.optimization_barrier((value,) + self.last)[0]

    def done(self, *values):
        self.last = values


class Task:
    def __init__(self, steps):
        self.steps, self.wanted, self.got, self.begun, self.over = steps, [], None, False, False

    def advance(self, turns):
        if self.over:
            return
        if self.wanted:
            start([self], turns)
        try:
            self.wanted = self.steps.send(self.got) if self.begun else next(self.steps)
            self.begun = True
        except StopIteration:
            self.wanted, self.over = [], True

    def finish(self, turns):
        while not self.over:
            self.advance(turns)


def start(tasks, turns):
    tasks = [task for task in tasks if task.wanted]
    values = [value for task in tasks for value, _ in task.wanted]
    if not values:
        return
    tied = lax.optimization_barrier(tuple(values) + turns.last)[: len(values)]
    turns.done(tied[0])
    tied = iter(tied)
    for task in tasks:
        task.got = [move(next(tied)) for _, move in task.wanted]
        task.wanted = []


def reduce_steps(links, turns, make, order, out, name):
    keep, send = make()
    turns.done(keep, send)
    for k, bit in enumerate(order):
        (got,) = yield [(send, functools.partial(links.swap, bit=bit))]
        keep = turns.after(keep)
        if k == len(order) - 1:
            out[name] = keep + got
            turns.done(out[name])
            return
        half = keep.shape[0] // 2
        send = keep[half:] + got[half:]
        keep = keep[:half] + got[:half]
        turns.done(keep, send)


def scan_steps(links, turns, make, decays, backwards, out):
    keep, send, decay = make()
    bits = links.seq_bits
    levels = []
    kept = [] if decays is None else decays
    turns.done(keep, send)
    for bit in range(bits - 1):
        swap = functools.partial(links.swap, bit=bit)
        if decays is None:
            got, got_d = yield [(send, swap), (decay, swap)]
            kept.append((decay, got_d))
            decay = decay * got_d
        else:
            (got,) = yield [(send, swap)]
        mine_d, got_d = kept[bit]
        keep = turns.after(keep)
        odd = (links.at_seq >> bit) & 1
        second = (odd == 0) if backwards else (odd == 1)
        levels.append((second, keep, got, mine_d, got_d))
        total = jnp.where(second, mine_d * got + keep, got_d * keep + got)
        half = total.shape[0] // 2
        if bit < bits - 2:
            keep, send = total[:half], total[half:]
            turns.done(keep, send)
        else:
            send = total
            turns.done(send)
    flip = 1 << (bits - 1)
    pairs = [(i, i ^ flip) for i in range(links.n_seq) if ((i >> (bits - 1)) & 1) == int(backwards)]
    (state,) = yield [(send, lambda value: lax.ppermute(value, "seq", pairs))]
    for bit in reversed(range(bits - 1)):
        second, keep, got, mine_d, got_d = levels[bit]
        keep = turns.after(keep)
        theirs = jnp.where(second, state, mine_d * state + keep)
        mine = jnp.where(second, got_d * state + got, state)
        turns.done(theirs, mine)
        (far,) = yield [(theirs, functools.partial(links.swap, bit=bit))]
        if bit == 0:
            out["near"], out["far"], out["decays"] = mine, far, kept
        else:
            mine = turns.after(mine)
            state = jnp.concatenate([mine, far], axis=0)


ROUTES = {
    "gate": ("x", "y", "z0", "z1"),
    "up": ("y", "x", "z0", "z1"),
    "down": ("z0", "x", "y", "z1"),
    "mid": ("x", "y", "z0", "z1"),
    "qk": ("x", "y", "z0", "z1"),
    "v": ("y", "x", "z0", "z1"),
    "small": ("x", "y", "z0", "z1"),
}
SCHEDULE = (
    "gate", "up", ("gate", "up"), "down", ("down",), "gate", ("gate",), "up", ("up",), "down",
    ("down",), "ff", "scan", ("scan",), "mid", "gate", "up", "down", "scan", ("scan", "up",
    "mid"), "mid", "scan", ("scan", "gate"), "up", "scan", ("scan", "mid"), "local", "gate",
    "scan", ("scan",), "scan", ("scan",), "mid", "scan", ("scan", "gate", "up", "down", "mid"),
    "scan", "qk", "v", "gate", "up", "down", "mid", ("qk", "v", "gate", "up", "mid"), "qk", "v",
    ("qk", "v"), "small", "small", "qk", "v", ("qk", "v"), "gate", "up", ("small", "down"),
    "mid", ("mid",), "qk", "v", ("qk", "v"), "small", ("small",), "qk", "v", ("qk", "v"),
    "down", ("down",), "small", ("small",), "mid", "small", ("small",), "qk", "v", "small",
    ("small",), "down", "small",
)


def local(
    block_in, doc_starts, cotangent, norm1_gain, w_query, w_key, w_value, w_outgate, w_rank_down,
    w_rank_up, decay_bias, group_gain, w_output, norm2_gain, w_ffgate, w_ffup, w_ffdown,
):
    row_count, length, width = block_in.shape
    tokens = row_count * length
    kw, vw = w_query.shape[1], w_value.shape[1]
    links, turns = Links(), Turns()
    parts = links.n_seq
    everyone = links.n_dp * links.n_seq
    dims = (row_count, length, width, kw, vw, doc_starts.shape[1], parts)
    x = block_in.reshape(tokens, width)
    cot = cotangent.reshape(tokens, width)
    docs = (doc_starts - links.at_seq * length).reshape(-1)
    rank_down_t = w_rank_down.T

    levels = range(links.seq_bits - 1)
    step = 1 << len(levels)
    size = parts // step
    low = links.at_seq & (step - 1)
    turn = lambda p: sum(((p >> b) & 1) << (len(levels) - 1 - b) for b in levels)
    reverse = jnp.array([turn(p) for p in range(step)], jnp.int32)
    spread = jnp.arange(size)
    to_piece = ((reverse ^ low)[:, None] * size + spread).reshape(-1)
    to_place = ((reverse ^ turn(low))[:, None] * size + spread).reshape(-1)
    state_table = jnp.concatenate([to_piece, to_place]).astype(jnp.int32)

    normed, k, v, ra, gp, cum, keep_a, send_a, keep_b, send_b, decay = project_all(
        x, docs, state_table, norm1_gain, w_key, w_value, rank_down_t, w_rank_up, decay_bias, dims
    )
    decay = decay.reshape(1, row_count, HEADS, 1, kw // HEADS)
    fwd_a, fwd_b = {}, {}
    one = Task(scan_steps(
        links, turns, lambda: (keep_a, send_a, decay[:, :, : HEADS // 2]), None, False, fwd_a
    ))
    two = Task(scan_steps(
        links, turns, lambda: (keep_b, send_b, decay[:, :, HEADS // 2 :]), None, False, fwd_b
    ))
    one.advance(turns)
    start([one], turns)
    two.advance(turns)
    start([two], turns)
    one.advance(turns)
    start([one], turns)
    two.advance(turns)
    start([two], turns)
    dh = hidden_back_all(turns.after(cot), w_ffdown)
    turns.done(dh)
    one.advance(turns)
    start([one], turns)
    two.advance(turns)
    start([two], turns)
    q, og = readers_all(turns.after(normed), w_query, w_outgate)
    turns.done(q)
    one.advance(turns)
    start([one], turns)
    two.advance(turns)
    start([two], turns)
    inner = inner_all(q, k, v, cum, turns.after(docs), dims)
    turns.done(inner)
    while not two.over:
        one.advance(turns)
        start([one], turns)
        two.advance(turns)
        start([two], turns)
    decays = [
        tuple(jnp.concatenate(pair, axis=2) for pair in zip(*both))
        for both in zip(fwd_a["decays"], fwd_b["decays"])
    ]
    states = (fwd_a["near"], fwd_a["far"], fwd_b["near"], fwd_b["far"])
    mixed, gated, state_kept = mix_all(
        q, cum, inner, og, states, group_gain, turns.after(docs), state_table, dims
    )
    hidden, dg, du, normed2, middle = ff_all(
        x, gated, w_output, norm2_gain, w_ffgate, w_ffup, dh
    )
    turns.done(normed2)

    routes = {name: links.order(*route) for name, route in ROUTES.items()}
    tables = {route: links.table(route) for route in set(routes.values())}
    back, grads, held = {}, {}, {}
    ff = w_ffgate.shape[1]

    def ff_steps():
        out, d_middle, d_out, d_gated, gnorm2 = ff_back_all(
            hidden, dg, du, w_ffdown, w_ffgate, w_ffup, middle, turns.after(cot), w_output, norm2_gain
        )
        held.update(out=out, d_middle=d_middle, d_out=d_out, d_gated=d_gated, gnorm2=gnorm2)
        turns.done(d_out)
        return
        yield

    def head_back():
        d_mix, d_og, keep, send, ggroup = head_back_all(
            held["d_gated"], og, mixed, q, cum, group_gain, turns.after(docs), state_table, dims
        )
        held.update(d_mix=d_mix, d_og=d_og, ggroup=ggroup)
        return keep, send, None

    def local_steps():
        held["d_q"], held["own_k"], held["own_v"], held["decay"] = mix_local_all(
            q, k, v, cum, held["d_mix"], state_kept, turns.after(docs), dims
        )
        turns.done(held["d_q"])
        return
        yield

    def all_back():
        yield from scan_steps(links, turns, head_back, decays, True, back)
        held["d_k"], held["d_v"], held["d_rank"], held["grup"], held["gbias"] = mix_back_all(
            k, v, cum, gp, ra, state_kept, held["own_k"], held["own_v"], held["decay"], back["near"],
            back["far"], w_rank_up, turns.after(docs), state_table, dims,
        )
        turns.done(held["d_rank"])

    operands = {
        "gate": lambda: [(normed2, dg)],
        "up": lambda: [(normed2, du)],
        "down": lambda: [(hidden, cot)],
        "mid": lambda: [(gated, held["d_out"]), (normed, held["d_og"])],
        "qk": lambda: [(normed, held["d_q"]), (normed, held["d_k"])],
        "v": lambda: [(normed, held["d_v"])],
    }
    made = {}

    def weights(name, *names):
        def make():
            if name not in made:
                ordered = [tables[routes[each]] for each in names]
                ordered[0] = turns.after(ordered[0])
                room = 60 if name in ("gate", "up", "down") else 32
                groups = weight_grads([operands[each]() for each in names], ordered, room)
                made.update(zip(names, groups))
            return made[name]

        return reduce_steps(links, turns, make, routes[name], grads, name)

    def small_steps():
        grad_in, gnorm1 = input_back_all(
            x, held["d_middle"], held["d_q"], held["d_k"], held["d_v"], held["d_og"], held["d_rank"],
            turns.after(norm1_gain), w_query, w_key, w_value, w_outgate, rank_down_t,
        )
        held["grad_in"] = grad_in
        turns.done(gnorm1)
        yield []
        make = lambda: small_grads(
            normed, held["d_rank"], gnorm1, held["gnorm2"], held["grup"], held["gbias"],
            held["ggroup"], turns.after(tables[routes["small"]]),
        )
        yield from reduce_steps(links, turns, make, routes["small"], grads, "small")

    rank = w_rank_up.shape[0]
    work = {
        "ff": ff_steps(),
        "scan": all_back(),
        "gate": weights("gate", "gate", "up"),
        "up": weights("up", "gate", "up"),
        "down": weights("down", "down"),
        "mid": weights("mid", "mid"),
        "local": local_steps(),
        "qk": weights("qk", "qk", "v"),
        "v": weights("v", "qk", "v"),
        "small": small_steps(),
    }
    work = {name: Task(steps) for name, steps in work.items()}
    for name in SCHEDULE + tuple(work) * (2 * len(routes["gate"])):
        if isinstance(name, tuple):
            start([work[each] for each in name], turns)
            continue
        if name in ("scan", "mid", "local"):
            work["ff"].finish(turns)
        if name in ("qk", "v", "small"):
            work["local"].finish(turns)
            work["scan"].finish(turns)
        work[name].advance(turns)

    per, per_k = width // everyone, kw // everyone
    small = grads["small"][0]
    first, second, third = small[:per], small[per : per + per_k], small[per + per_k :]
    mid, qk = grads["mid"][0], grads["qk"][0]
    return (
        held["out"].reshape(row_count, length, width),
        held["grad_in"].reshape(row_count, length, width),
        first[:, rank],
        qk[:per],
        qk[per:],
        grads["v"][0],
        mid[per:],
        first[:, :rank],
        second[:, :rank].T,
        second[:, rank],
        third[:, 0],
        mid[:per],
        first[:, rank + 1],
        grads["gate"][0],
        grads["up"][0],
        grads["down"][0],
    )


def solution(mesh):
    tokens = P("dp", "seq", None)
    rows = P(("dp", "seq"), None)
    vector = P(("dp", "seq"))
    return jax.shard_map(
        local,
        mesh=mesh,
        in_specs=(tokens, P("dp", None), tokens) + (P(),) * 14,
        out_specs=(
            tokens, tokens, vector, rows, rows, rows, rows, rows, P(None, ("dp", "seq")), vector,
            vector, rows, vector, rows, rows, rows,
        ),
        check_vma=False,
    )
```
